256 devices in a mesh: band: 32 (over x_hi, z, core), tm: 8 (over x_lo, y).
Axes of the slice: x: 4 (x_hi: 2, x_lo: 2; x = x_hi * 2 + x_lo), y: 4, z: 8, core: 2. Of those that a mesh axis runs over, the one named last changes fastest.
Arguments:
- intensity: bfloat16 [16384, 8192], P('band', 'tm')
- shifts: int32 [12, 4096], P(None, 'band'), may hold values from 0 to 32, as said below
- boxcar_widths: int32 [8], replicated, may hold values from 1 to 64, as said below
Outputs:
- dedispersed: float32 [4096, 8192], P('band', 'tm')
- peak_snr: float32 [4096, 8192], P('band', 'tm')
The draws below stay inside these ranges and needn't reach their ends.
Inputs may be any that keep to these rules, and one draw needn't show every extreme that they name: Every section s has some entry shifts[s, n] equal to 32. `boxcar_widths`: one of the widths equals 64; widths may repeat.
All inputs are finite; a program needn't handle non-finite values.
Results may differ from the reference program's by a relative error of at most 0.0003.
Values sent between devices are 32-bit elements; how exact they have to be, the bound alone decides.
A program may use at most 64 MiB of HBM per device.

```python
import jax
import jax.numpy as jnp
from jax import lax

PRESUM = 4
HALO = 32
NBOX = 8
WMAX = 64
DM_DEV = 128
CHAN = 16384
DMS = 4096
TIME = 8192
SECTIONS = 12


def draw_intensity(key, part):
    base_key = jax.random.fold_in(key, 101)
    noise_key = jax.random.fold_in(base_key, 0)
    time_pos = jnp.arange(TIME, dtype=jnp.float32) / TIME
    values = jax.random.normal(noise_key, (CHAN, TIME), jnp.float32)
    values = values * (1.0 + 2.0 * time_pos)[None, :]
    return values.astype(jnp.bfloat16)


def draw_shifts(key, part):
    base_key = jax.random.fold_in(key, 202)
    value_key, place_key = jax.random.split(base_key)
    values = jax.random.randint(value_key, (SECTIONS, DMS), 0, HALO + 1, dtype=jnp.int32)
    places = jax.random.randint(place_key, (SECTIONS, 1), 0, DMS, dtype=jnp.int32)
    columns = jnp.arange(DMS, dtype=jnp.int32)[None, :]
    return jnp.where(columns == places, HALO, values).astype(jnp.int32)


def draw_boxcar_widths(key, part):
    base_key = jax.random.fold_in(key, 303)
    value_key, place_key = jax.random.split(base_key)
    values = jax.random.randint(value_key, (NBOX,), 1, WMAX + 1, dtype=jnp.int32)
    place = jax.random.randint(place_key, (), 0, NBOX, dtype=jnp.int32)
    return jnp.where(jnp.arange(NBOX, dtype=jnp.int32) == place, WMAX, values).astype(jnp.int32)


def setup_inputs(seed: int = 0) -> dict:
    keys = jax.random.split(jax.random.key(seed), 4)
    return {
        "intensity": draw_intensity(jax.random.fold_in(keys[3], 71), 0),
        "shifts": draw_shifts(jax.random.fold_in(keys[3], 71), 0),
        "boxcar_widths": draw_boxcar_widths(jax.random.fold_in(keys[3], 71), 0),
    }


def reference(intensity, shifts, boxcar_widths):
    levels = lax.optimization_barrier(jnp.sum(intensity.reshape(DMS, PRESUM, TIME), axis=1, dtype=jnp.float32))
    for section in range(1, SECTIONS + 1):
        group_size = 2 ** section
        half_size = group_size // 2
        new_rows = jnp.arange(group_size, dtype=jnp.int32)
        if group_size <= DM_DEV:
            source_rows = new_rows // 2
        else:
            source_rows = DM_DEV * (new_rows % half_size // DM_DEV) + DM_DEV // 2 * (new_rows // half_size) + new_rows % DM_DEV // 2
        grouped = levels.reshape(DMS // group_size, 2, half_size, TIME)
        first_half = grouped[:, 0][:, source_rows]
        second_half = grouped[:, 1][:, source_rows]
        delays = shifts[section - 1].reshape(DMS // group_size, group_size)
        padded = jnp.pad(second_half, ((0, 0), (0, 0), (HALO, 0)))
        positions = (HALO + jnp.arange(TIME, dtype=jnp.int32)[None, None, :] - delays[:, :, None]).astype(jnp.int32)
        levels = (first_half + jnp.take_along_axis(padded, positions, axis=2)).reshape(DMS, TIME)
    dedispersed = levels * CHAN ** (-0.5)
    row_mean = lax.optimization_barrier(jnp.sum(dedispersed, axis=1, keepdims=True)) / TIME
    centred = dedispersed - row_mean
    spread = jnp.sqrt(lax.optimization_barrier(jnp.sum(centred * centred, axis=1, keepdims=True)) / TIME + 1e-06)
    padded_series = jnp.pad(dedispersed, ((0, 0), (WMAX, 0)))

    def add_lag(step_index, state_pair):
        running, best_snr = state_pair
        shifted = lax.dynamic_slice_in_dim(padded_series, (WMAX - step_index).astype(jnp.int32), TIME, 1)
        running = running + shifted
        width_count = (step_index + 1).astype(jnp.int32)
        width_f = width_count.astype(jnp.float32)
        active = jnp.any(boxcar_widths == width_count)
        candidate = (running - width_f * row_mean) / (spread * jnp.sqrt(width_f))
        best_snr = jnp.where(active, jnp.maximum(best_snr, candidate), best_snr)
        return (running, best_snr)
    start_pair = (jnp.zeros((DMS, TIME), jnp.float32), jnp.full((DMS, TIME), -1e+30, jnp.float32))
    running, peak_snr = lax.fori_loop(0, WMAX, add_lag, start_pair)
    return (dedispersed, peak_snr)
```

```python
import jax
import jax.numpy as jnp
from jax import lax
from jax.experimental import pallas as pl
from jax.experimental.pallas import tpu as pltpu
from jax.sharding import PartitionSpec as P

MESH = pl.DeviceIdType.MESH
F32, BF16, I32 = jnp.float32, jnp.bfloat16, jnp.int32
NB, NT = 32, 8
NBOX = 8
LOCAL, CROSS = 7, 5
TILES = 4
SAMPLES = 8192

_ROWS = lax.GatherDimensionNumbers(
    offset_dims=(),
    collapsed_slice_dims=(1,),
    start_index_map=(1,),
    operand_batching_dims=(0,),
    start_indices_batching_dims=(0,),
)


def iota(shape, dim):
    return lax.broadcasted_iota(I32, shape, dim)


def take_lanes(x, index):
    return lax.gather(
        x, index[..., None], _ROWS, (1, 1), mode=lax.GatherScatterMode.PROMISE_IN_BOUNDS
    )


def rev5(v):
    out = 0
    for k in range(5):
        out = out + (v // 2**k) % 2 * 2 ** (4 - k)
    return out


def delay_add(firsts, seconds, index, keep):
    wraps = index > iota(index.shape, 1)
    turned = [take_lanes(s, index) for s in seconds]
    outs = []
    for j in range(len(firsts) - keep, len(firsts)):
        term = turned[j] if j == 0 else jnp.where(wraps, turned[j - 1], turned[j])
        outs.append(firsts[j] + term)
    return outs


def major_section(tiles, index, apart, keep):
    rows = index.shape[0]
    shape = (rows // (2 * apart), 2, apart, 128)

    def both(x, which):
        part = x.reshape(shape)[:, which : which + 1]
        return jnp.broadcast_to(part, shape).reshape(rows, 128)

    return delay_add([both(x, 0) for x in tiles], [both(x, 1) for x in tiles], index, keep)


def minor_section(tiles, index, apart, keep):
    rows = index.shape[0]
    is_set = iota(index.shape, 0) // apart % 2 == 1
    firsts = [jnp.where(is_set, pltpu.roll(x, apart, 0), x) for x in tiles]
    seconds = [jnp.where(is_set, x, pltpu.roll(x, rows - apart, 0)) for x in tiles]
    return delay_add(firsts, seconds, index, keep)


def swap_halves(x):
    rows = x.shape[0]
    return jnp.where(
        iota(x.shape, 0) % 8 < 4, pltpu.roll(x, rows - 4, 0), pltpu.roll(x, 4, 0)
    )


def kernel(
    x_hbm, sh_hbm, w_hbm, ded_hbm, snr_hbm,
    xc, shv, wsm, shsend, shbuf, idx1, idx2, l0, work, s7, hsend, hrecv, gsend, grecv,
    recv, t2, hi, lo, bc, band, roots, pk, dedv, snrv, stsend, stbuf,
    local_sem, shs_sem, shr_sem, halo_sem, a2a_send, a2a_recv, st_send, st_recv,
):
    me, t = lax.axis_index("band"), lax.axis_index("tm")
    later = lax.rem(t + 1, NT)
    slot = rev5(me)
    lane8 = iota((8, 128), 1)
    lane64 = iota((64, 128), 1)

    copy_x1 = pltpu.make_async_copy(x_hbm.at[:, pl.ds(512, 512)], xc.at[pl.ds(512, 512)], local_sem.at[0])
    copy_x0 = pltpu.make_async_copy(x_hbm.at[:, pl.ds(0, 512)], xc.at[pl.ds(0, 512)], local_sem.at[1])
    copy_sh = pltpu.make_async_copy(sh_hbm, shv, local_sem.at[2])
    copy_w = pltpu.make_async_copy(w_hbm, wsm, local_sem.at[3])
    copy_sh.start()
    copy_x1.start()
    copy_x0.start()
    copy_w.start()

    barrier = pltpu.get_barrier_semaphore()

    def greet_band(i, carry):
        pl.semaphore_signal(barrier, inc=1, device_id={"band": lax.rem(me + i, NB)}, device_id_type=MESH)
        return carry

    def greet_tm(i, carry):
        pl.semaphore_signal(barrier, inc=1, device_id={"tm": lax.rem(t + i, NT)}, device_id_type=MESH)
        return carry

    lax.fori_loop(1, NB, greet_band, 0)
    lax.fori_loop(1, NT, greet_tm, 0)

    def group_of(i, halves):
        blocks = i // 8 if halves else i // 4
        return blocks + 32 * (i // 2 % 2) + 64 * (i % 2)

    i = iota((256, 1024), 0)
    target = i // 4 % 2 * 128 + group_of(i, True)
    presum = jnp.where(iota((256, 1024), 1) // 4 == target, 1.0, 0.0).astype(BF16)
    i = iota((128, 512), 0)
    presum_edge = jnp.where(iota((128, 512), 1) // 4 == group_of(i, False), 1.0, 0.0).astype(BF16)

    copy_sh.wait()
    i, lane = iota((256, 128), 0), iota((256, 128), 1)
    place = group_of(i, True)
    turned = jnp.zeros((256, 128), I32)
    for s in range(1, LOCAL + 1):
        turned = 2 * turned + place // 2 ** (s - 1) % 2
        new_row = turned + place // 2**s * 2**s
        delay = take_lanes(jnp.broadcast_to(shv[s - 1 : s, :], (256, 128)), new_row)
        idx1[s - 1] = ((lane - delay) & 127).reshape(4, 8, 8, 128)
    for j in range(CROSS - 1):
        shsend[j] = shv[LOCAL + j : LOCAL + j + 1, :]
        shbuf[me, j] = shv[LOCAL + j : LOCAL + j + 1, :]

    pl.semaphore_wait(barrier, NB + NT - 2)

    def shift_copy(i):
        return pltpu.make_async_remote_copy(
            src_ref=shsend, dst_ref=shbuf.at[me], send_sem=shs_sem.at[i], recv_sem=shr_sem.at[i],
            device_id={"band": lax.rem(me + 2 * i, NB)}, device_id_type=MESH,
        )

    def start_shift(i, carry):
        shift_copy(i).start()
        return carry

    lax.fori_loop(1, NB // 2, start_shift, 0)

    copy_x1.wait()
    edge = jnp.dot(presum_edge, xc[512:1024, 256:512], preferred_element_type=F32)
    for k in range(2):
        hsend[k] = edge[:, k * 128 : (k + 1) * 128]
    halo_copy = pltpu.make_async_remote_copy(
        src_ref=hsend, dst_ref=hrecv, send_sem=halo_sem.at[0], recv_sem=halo_sem.at[1],
        device_id={"tm": later}, device_id_type=MESH,
    )
    halo_copy.start()

    copy_x0.wait()
    level = jnp.dot(presum, xc[...], preferred_element_type=F32)
    for k in range(TILES):
        l0[2 + k] = level[:, k * 128 : (k + 1) * 128].reshape(4, 8, 8, 128)

    def local_sections(first, out):
        for h in range(4):
            tiles = [l0[first + k, h].reshape(64, 128) for k in range(4)]
            for s, keep in ((1, 4), (2, 4), (3, 3)):
                tiles = major_section(tiles, idx1[s - 1, h].reshape(64, 128), 8 * 2 ** (s - 1), keep)
            for k in range(3):
                work[k, h] = tiles[k].reshape(8, 8, 128)
        for g in range(4):
            at = pl.ds(2 * g, 2)
            tiles = [work[k, :, at].reshape(64, 128) for k in range(3)]
            for s, keep in ((4, 3), (5, 3)):
                tiles = major_section(tiles, idx1[s - 1, :, at].reshape(64, 128), 16 * 2 ** (s - 4), keep)
            for s, keep in ((6, 3), (7, 2)):
                tiles = minor_section(tiles, idx1[s - 1, :, at].reshape(64, 128), 2 ** (7 - s), keep)
            for k in range(2):
                s7[out + k, :, at] = tiles[k].reshape(4, 2, 8, 128)

    def part_copy(c, i):
        dest = lax.rem(me + i, NB)
        return pltpu.make_async_remote_copy(
            src_ref=s7.at[pl.ds(2 * c, 2), dest // 8, dest % 8],
            dst_ref=recv.at[pl.ds(2 + 2 * c, 2), slot // 8, slot % 8],
            send_sem=a2a_send.at[c, i], recv_sem=a2a_recv.at[c, i],
            device_id={"band": dest}, device_id_type=MESH,
        )

    def start_parts(c):
        def body(i, carry):
            part_copy(c, i).start()
            return carry

        lax.fori_loop(1, NB, body, 0)
        for k in range(2):
            recv[2 + 2 * c + k, slot // 8, slot % 8] = s7[2 * c + k, me // 8, me % 8]

    def await_parts(c):
        def body(i, carry):
            part_copy(c, i).wait_recv()
            return carry

        lax.fori_loop(1, NB, body, 0)

    local_sections(2, 2)
    start_parts(1)

    before = jnp.dot(presum[:, 512:], xc[0:512, 256:512], preferred_element_type=F32)
    halo_copy.wait_recv()
    is_low = iota((256, 128), 0) % 8 < 4
    for k in range(2):
        edge = jnp.where(t > 0, hrecv[k], 0.0)
        edge = jnp.broadcast_to(edge.reshape(16, 1, 8, 128), (16, 2, 8, 128)).reshape(256, 128)
        odd = iota((256, 128), 0) // 8 % 2 == 1
        edge = jnp.where(odd, swap_halves(edge), edge)
        own = before[:, k * 128 : (k + 1) * 128]
        l0[k] = jnp.where(is_low, edge, own).reshape(4, 8, 8, 128)
    local_sections(0, 0)
    start_parts(0)

    copy_w.wait()
    offset, column = iota((256, 128), 0) - 128, iota((256, 128), 1)
    for j in range(NBOX):
        width = wsm[j]
        inside = (offset <= column) & (offset > column - width)
        band[:, j * 128 : (j + 1) * 128] = jnp.where(inside, 1.0, 0.0).astype(BF16)
        root = jnp.sqrt(jnp.full((8, 128), width, I32).astype(F32))
        roots[0, j] = root
        roots[1, j] = 1.0 / root

    def await_shift(i, carry):
        shift_copy(i).wait_recv()
        return carry

    lax.fori_loop(1, NB // 2, await_shift, 0)
    quarter = iota((8, 128), 0) % 4
    for j in range(1, CROSS + 1):
        base = 0
        for bit in range(j, CROSS):
            base = base + me // 2**bit % 2 * 2 ** (6 - bit + j)
        for low in range(2 ** (CROSS - j)):
            if j < CROSS:
                source = me % 2**j
                for bit in range(j, CROSS):
                    source = source + 2**bit * ((low >> (4 - bit)) & 1)
                row = shbuf[source, j - 1]
            else:
                row = shv[LOCAL + j - 1 : LOCAL + j, :]
            row = jnp.broadcast_to(row, (8, 128))
            for high in range(2**j):
                delay = take_lanes(row, base + 2**j * quarter + high)
                at = low + 2 ** (CROSS - j) * high
                idx2[j - 1, at // 8, at % 8] = (lane8 - delay) & 127

    await_parts(1)
    low8 = iota((128, 128), 0) % 8 < 4
    for k in range(2):
        ahead = recv[4 + k].reshape(16, 2, 8, 128)
        even, odd = ahead[:, 0].reshape(128, 128), ahead[:, 1].reshape(128, 128)
        gsend[k] = jnp.where(low8, swap_halves(even), odd)
    edge_copy = pltpu.make_async_remote_copy(
        src_ref=gsend, dst_ref=grecv, send_sem=halo_sem.at[2], recv_sem=halo_sem.at[3],
        device_id={"tm": later}, device_id_type=MESH,
    )
    edge_copy.start()
    edge_copy.wait_recv()
    for k in range(2):
        edge = jnp.where(t > 0, grecv[k], 0.0)
        edge = jnp.broadcast_to(edge.reshape(16, 1, 8, 128), (16, 2, 8, 128)).reshape(256, 128)
        odd = iota((256, 128), 0) // 8 % 2 == 1
        edge = jnp.where(odd, swap_halves(edge), edge)
        own = swap_halves(recv[4 + k].reshape(256, 128))
        recv[k] = jnp.where(is_low, edge, own).reshape(4, 8, 8, 128)

    await_parts(0)
    for g in range(4):
        at = pl.ds(2 * g, 2)
        tiles = [recv[k, :, at].reshape(64, 128) for k in range(6)]
        for j, keep in ((1, 6), (2, 6)):
            tiles = major_section(tiles, idx2[j - 1, :, at].reshape(64, 128), 32 // 2 ** (j - 1), keep)
        for k in range(6):
            l0[k, :, at] = tiles[k].reshape(4, 2, 8, 128)
    stats = []
    for h in range(4):
        tiles = [l0[k, h].reshape(64, 128) for k in range(6)]
        for j in (3, 4, 5):
            tiles = major_section(tiles, idx2[j - 1, h].reshape(64, 128), 32 // 2 ** (j - 3), 5)
        tiles = [x * (16384.0 ** (-0.5)) for x in tiles]
        at = pl.ds(64 * h, 64)
        for k in range(5):
            t2[k, at] = tiles[k]
        total = tiles[1] + tiles[2] + tiles[3] + tiles[4]
        total = jnp.sum(total + swap_halves(total), axis=1, keepdims=True)
        pivot = jnp.broadcast_to(total * (1.0 / 1024), (64, 128))
        squares = jnp.zeros((64, 128), F32)
        for k in range(5):
            centred = tiles[k] - pivot
            if k:
                squares = squares + centred * centred
            high = centred.astype(BF16)
            hi[at, k * 128 : (k + 1) * 128] = high
            lo[at, k * 128 : (k + 1) * 128] = (centred - high.astype(F32)).astype(BF16)
        squares = jnp.sum(squares + swap_halves(squares), axis=1, keepdims=True)
        stats.append((pivot, jnp.where(lane64 == 0, pivot, jnp.broadcast_to(squares, (64, 128)))))
    packed = jnp.concatenate([s[1] for s in stats], axis=0)
    mine = jnp.transpose(packed)[0:8]
    stsend[...] = mine
    stbuf[t] = mine

    def stat_copy(i):
        return pltpu.make_async_remote_copy(
            src_ref=stsend, dst_ref=stbuf.at[t], send_sem=st_send.at[i], recv_sem=st_recv.at[i],
            device_id={"tm": lax.rem(t + i, NT)}, device_id_type=MESH,
        )

    for i in range(1, NT):
        stat_copy(i).start()

    def unmix(source, first, out):
        for k in range(TILES):
            for s in range(8):
                for b in range(4):
                    rows = source[first + k, pl.ds(b * 64 + s, 8, stride=8), :]
                    out[pl.ds(s % 4 * 32 + b * 8, 8), pl.ds(s // 4 * 512 + k * 128, 128)] = rows

    unmix(t2, 1, dedv)
    copy_ded = pltpu.make_async_copy(dedv, ded_hbm, local_sem.at[4])
    copy_ded.start()

    for k in range(TILES):
        at = pl.ds(k * 128, 256)
        both = jnp.dot(hi[:, at], band[...], preferred_element_type=F32)
        bc[k] = both + jnp.dot(lo[:, at], band[...], preferred_element_type=F32)

    for i in range(1, NT):
        stat_copy(i).wait_recv()
    means = [stbuf[i][0:1] for i in range(NT)]
    mean = sum(means) * (1.0 / NT)
    centred = [stbuf[i][1:2] + 1024.0 * ((m - mean) * (m - mean)) for i, m in enumerate(means)]
    scale = 1.0 / jnp.sqrt(sum(centred) * (1.0 / SAMPLES) + 1e-6)
    row_of = iota((8, 256), 0)
    shared = jnp.where(row_of == 0, jnp.broadcast_to(mean, (8, 256)), jnp.broadcast_to(scale, (8, 256)))
    shared = jnp.transpose(shared)
    for h in range(4):
        at = pl.ds(64 * h, 64)
        part = shared[64 * h : 64 * h + 64]
        row_mean = jnp.broadcast_to(part[:, 0:1], (64, 128))
        row_scale = jnp.broadcast_to(part[:, 1:2], (64, 128))
        off = stats[h][0] - row_mean
        for k in range(TILES):
            best = None
            for j in range(NBOX):
                up = jnp.broadcast_to(roots[0, j].reshape(1, 8, 128), (8, 8, 128)).reshape(64, 128)
                down = jnp.broadcast_to(roots[1, j].reshape(1, 8, 128), (8, 8, 128)).reshape(64, 128)
                score = bc[k, at, j * 128 : (j + 1) * 128] * down + up * off
                best = score if best is None else jnp.maximum(best, score)
            pk[k, at] = best * row_scale
    unmix(pk, 0, snrv)
    copy_snr = pltpu.make_async_copy(snrv, snr_hbm, local_sem.at[5])
    copy_snr.start()

    def drain_parts(i, carry):
        part_copy(0, i).wait_send()
        part_copy(1, i).wait_send()
        return carry

    def drain_shifts(i, carry):
        shift_copy(i).wait_send()
        return carry

    lax.fori_loop(1, NB, drain_parts, 0)
    lax.fori_loop(1, NB // 2, drain_shifts, 0)
    halo_copy.wait_send()
    edge_copy.wait_send()
    for i in range(1, NT):
        stat_copy(i).wait_send()
    copy_ded.wait()
    copy_snr.wait()


def body(intensity, shifts, boxcar_widths):
    dma = pltpu.SemaphoreType.DMA
    vmem = pltpu.VMEM
    state = (4, 8, 8, 128)
    out = jax.ShapeDtypeStruct((128, 1024), F32)
    return pl.pallas_call(
        kernel,
        out_shape=(out, out),
        in_specs=[pl.BlockSpec(memory_space=pl.ANY)] * 3,
        out_specs=[pl.BlockSpec(memory_space=pl.ANY)] * 2,
        scratch_shapes=[
            vmem((1024, 512), BF16),
            vmem((12, 128), I32),
            pltpu.SMEM((NBOX,), I32),
            vmem((4, 1, 128), I32),
            vmem((NB, 4, 1, 128), I32),
            vmem((LOCAL, *state), I32),
            vmem((CROSS, *state), I32),
            vmem((6, *state), F32),
            vmem((3, *state), F32),
            vmem((TILES, *state), F32),
            vmem((2, 128, 128), F32),
            vmem((2, 128, 128), F32),
            vmem((2, 128, 128), F32),
            vmem((2, 128, 128), F32),
            vmem((2 + TILES, *state), F32),
            vmem((5, 256, 128), F32),
            vmem((256, 640), BF16),
            vmem((256, 640), BF16),
            vmem((TILES, 256, 1024), F32),
            vmem((256, 1024), BF16),
            vmem((2, NBOX, 8, 128), F32),
            vmem((TILES, 256, 128), F32),
            vmem((128, 1024), F32),
            vmem((128, 1024), F32),
            vmem((8, 256), F32),
            vmem((NT, 8, 256), F32),
            dma((6,)),
            dma((NB // 2,)),
            dma((NB // 2,)),
            dma((4,)),
            dma((2, NB)),
            dma((2, NB)),
            dma((NT,)),
            dma((NT,)),
        ],
        compiler_params=pltpu.CompilerParams(
            collective_id=0, has_side_effects=True, vmem_limit_bytes=40 * 2**20
        ),
    )(intensity, shifts, boxcar_widths)


def solution(mesh):
    assert mesh.shape["band"] == NB and mesh.shape["tm"] == NT
    in_specs = (P("band", "tm"), P(None, "band"), P())
    out_specs = (P("band", "tm"), P("band", "tm"))
    return jax.shard_map(body, mesh=mesh, in_specs=in_specs, out_specs=out_specs, check_vma=False)
```

```python
import jax
import jax.numpy as jnp
from jax import lax
from jax.experimental import pallas as pl
from jax.experimental.pallas import tpu as pltpu
from jax.sharding import PartitionSpec as P

MESH = pl.DeviceIdType.MESH
F32, BF16, I32 = jnp.float32, jnp.bfloat16, jnp.int32
NB, NT = 32, 8
NBOX = 8
NCOL = 16
LOCAL, CROSS = 7, 5
TILES = 4
SAMPLES = 8192

_ROWS = lax.GatherDimensionNumbers(
    offset_dims=(),
    collapsed_slice_dims=(1,),
    start_index_map=(1,),
    operand_batching_dims=(0,),
    start_indices_batching_dims=(0,),
)


def iota(shape, dim):
    return lax.broadcasted_iota(I32, shape, dim)


def take_lanes(x, index):
    return lax.gather(
        x, index[..., None], _ROWS, (1, 1), mode=lax.GatherScatterMode.PROMISE_IN_BOUNDS
    )


def rev5(v):
    out = 0
    for k in range(5):
        out = out + (v // 2**k) % 2 * 2 ** (4 - k)
    return out


OFFSETS = sorted(
    [(dx, dz, dc) for dx in range(2) for dz in range(8) for dc in range(2)][1:],
    key=lambda o: (o[0], -min(o[1], 8 - o[1])),
)


def delay_add(firsts, seconds, index, keep):
    rows, tiles = firsts.shape[:2]
    spread = jnp.broadcast_to(index[:, None], firsts.shape).reshape(-1, 128)
    turned = take_lanes(seconds.reshape(-1, 128), spread).reshape(firsts.shape)
    wraps = index > iota(index.shape, 2)
    later = tiles - max(1, tiles - keep)
    wraps = jnp.broadcast_to(wraps[:, None], (rows, later, 8, 128))
    term = jnp.where(wraps, turned[:, tiles - later - 1 : tiles - 1], turned[:, tiles - later :])
    out = firsts[:, tiles - later :] + term
    if keep == tiles:
        out = jnp.concatenate([firsts[:, :1] + turned[:, :1], out], axis=1)
    return out


def major_section(x, index, apart, keep):
    rows, tiles = x.shape[:2]
    shape = (rows // (2 * apart), 2, apart, tiles, 8, 128)
    pairs = x.reshape(shape)
    both = [jnp.broadcast_to(pairs[:, e : e + 1], shape).reshape(x.shape) for e in (0, 1)]
    return delay_add(*both, index, keep)


def minor_section(x, index, apart, keep):
    flat = x.reshape(-1, 8, 128)
    is_set = iota(flat.shape, 1) // apart % 2 == 1
    firsts = jnp.where(is_set, pltpu.roll(flat, apart, 1), flat)
    seconds = jnp.where(is_set, flat, pltpu.roll(flat, 8 - apart, 1))
    return delay_add(firsts.reshape(x.shape), seconds.reshape(x.shape), index, keep)


def swap_halves(x):
    return pltpu.roll(x.reshape(-1, 8, 128), 4, 1).reshape(x.shape)


def kernel(
    x_hbm, par_hbm, ded_ref, snr_ref,
    xc, par, shsend, shbuf, idx1, idx2, l0, s7, hsend, hrecv, gsend, grecv,
    recv, t2, hi, lo, bc, band, roots, stsend, stbuf,
    local_sem, shs_sem, shr_sem, halo_sem, a2a_send, a2a_recv, st_send, st_recv,
):
    me, t = lax.axis_index("band"), lax.axis_index("tm")
    copy_par = pltpu.make_async_copy(par_hbm, par, local_sem.at[0])
    copy_x1 = pltpu.make_async_copy(x_hbm.at[:, pl.ds(512, 512)], xc.at[pl.ds(512, 512)], local_sem.at[1])
    copy_x0 = pltpu.make_async_copy(x_hbm.at[:, pl.ds(0, 512)], xc.at[pl.ds(0, 512)], local_sem.at[2])
    copy_par.start()
    copy_x1.start()
    copy_x0.start()

    barrier = pltpu.get_barrier_semaphore()
    for i in range(1, NB):
        pl.semaphore_signal(barrier, inc=1, device_id={"band": lax.rem(me + i, NB)}, device_id_type=MESH)
    for i in range(1, NT):
        pl.semaphore_signal(barrier, inc=1, device_id={"tm": lax.rem(t + i, NT)}, device_id_type=MESH)

    column, place = me // NCOL, me % NCOL
    z, core = place // 2, place % 2
    later = lax.rem(t + 1, NT)
    slot = rev5(me)
    sub8, lane8 = iota((8, 128), 0), iota((8, 128), 1)

    def group_of(i, halves):
        blocks = i // 8 if halves else i // 4
        return blocks + 32 * (i // 2 % 2) + 64 * (i % 2)

    copy_par.wait()
    for s in range(1, LOCAL + 1):
        row = jnp.broadcast_to(par[s - 1 : s, :], (8, 128))
        if s <= 5:
            base = sub8 // 2 % 2 * 32 + sub8 % 2 * 64
        else:
            base = sub8 // 2 % 2 * (1, 2)[s - 6] + sub8 % 2 * (64, 1)[s - 6]
        for m in range(32):
            turned = int(f"{m:05b}"[::-1], 2)
            if s <= 5:
                turned = (turned >> (5 - s)) + (m >> s << s)
            else:
                turned = turned << (s - 5)
            idx1[s - 1, m] = (lane8 - take_lanes(row, base + turned)) & 127
    for j in range(CROSS - 1):
        shsend[j] = par[LOCAL + j : LOCAL + j + 1, :]
        shbuf[me, j] = par[LOCAL + j : LOCAL + j + 1, :]

    i = iota((256, 1024), 0)
    target = i // 4 % 2 * 128 + group_of(i, True)
    presum = jnp.where(iota((256, 1024), 1) // 4 == target, 1.0, 0.0).astype(BF16)
    i = iota((128, 512), 0)
    presum_edge = jnp.where(iota((128, 512), 1) // 4 == group_of(i, False), 1.0, 0.0).astype(BF16)
    copy_x1.wait()
    copy_x0.wait()
    level = jnp.dot(presum, xc[...], preferred_element_type=F32)
    for k in range(TILES):
        l0[:, 2 + k] = level[:, k * 128 : (k + 1) * 128].reshape(32, 8, 128)
    edge = jnp.dot(presum_edge, xc[512:1024, 256:512], preferred_element_type=F32)
    for k in range(2):
        hsend[k] = edge[:, k * 128 : (k + 1) * 128]

    def local_sections(first, tiles):
        x = l0[:, first : first + tiles + 2]
        for s, keep in ((1, tiles + 2), (2, tiles + 2), (3, tiles + 1), (4, tiles + 1), (5, tiles + 1)):
            x = major_section(x, idx1[s - 1], 2 ** (s - 1), keep)
        for s, keep in ((6, tiles + 1), (7, tiles)):
            x = minor_section(x, idx1[s - 1], 2 ** (7 - s), keep)
        s7[:, first : first + tiles] = x

    def part_copy(c, k):
        dx, dz, dc = OFFSETS[k]
        dest = (column + dx) % 2 * NCOL + (z + dz) % 8 * 2 + (core + dc) % 2
        return pltpu.make_async_remote_copy(
            src_ref=s7.at[dest, pl.ds(2 * c, 2)], dst_ref=recv.at[slot, pl.ds(2 + 2 * c, 2)],
            send_sem=a2a_send.at[c, k], recv_sem=a2a_recv.at[c, k],
            device_id={"band": dest}, device_id_type=MESH,
        )

    def start_parts(c, order):
        for k in order:
            part_copy(c, k).start()
        recv[slot, 2 + 2 * c : 4 + 2 * c] = s7[me, 2 * c : 2 * c + 2]

    def await_parts(c):
        for k in range(NB - 1):
            part_copy(c, k).wait_recv()

    def shift_copy(i):
        return pltpu.make_async_remote_copy(
            src_ref=shsend, dst_ref=shbuf.at[me], send_sem=shs_sem.at[i], recv_sem=shr_sem.at[i],
            device_id={"band": lax.rem(me + 2 * i, NB)}, device_id_type=MESH,
        )

    halo_copy = pltpu.make_async_remote_copy(
        src_ref=hsend, dst_ref=hrecv, send_sem=halo_sem.at[0], recv_sem=halo_sem.at[1],
        device_id={"tm": later}, device_id_type=MESH,
    )
    edge_copy = pltpu.make_async_remote_copy(
        src_ref=gsend, dst_ref=grecv, send_sem=halo_sem.at[2], recv_sem=halo_sem.at[3],
        device_id={"tm": later}, device_id_type=MESH,
    )
    has_next, has_last = t < NT - 1, t > 0

    local_sections(2, 2)
    pl.semaphore_wait(barrier, NB + NT - 2)
    pl.when(has_next)(halo_copy.start)
    for i in range(1, NB // 2):
        shift_copy(i).start()
    start_parts(1, range(NB - 1))

    before = jnp.dot(presum[:, 512:], xc[0:512, 256:512], preferred_element_type=F32)

    @pl.when(t == 0)
    def _():
        hrecv[...] = jnp.zeros((2, 128, 128), F32)
        grecv[...] = jnp.zeros((2, 128, 128), F32)

    pl.when(has_last)(halo_copy.wait_recv)
    is_low = iota((32, 8, 128), 1) < 4

    def spread_edge(packed):
        return jnp.stack([packed, swap_halves(packed)], axis=1).reshape(32, 8, 128)

    for k in range(2):
        own = before[:, k * 128 : (k + 1) * 128].reshape(32, 8, 128)
        l0[:, k] = jnp.where(is_low, spread_edge(hrecv[k].reshape(16, 8, 128)), own)
    local_sections(0, 2)
    start_parts(0, [*range(NCOL - 1, NB - 1), *range(NCOL - 1)])

    offset, sample = iota((256, 128), 0) - 128, iota((256, 128), 1)
    row = jnp.broadcast_to(par[12:13, :], (8, 128))
    for j in range(NBOX):
        width = take_lanes(row, jnp.full((8, 128), j, I32))
        root = jnp.sqrt(width.astype(F32))
        roots[0, j] = root
        roots[1, j] = 1.0 / root
        width = jnp.broadcast_to(width[None], (32, 8, 128)).reshape(256, 128)
        inside = (offset <= sample) & (offset > sample - width)
        band[:, j * 128 : (j + 1) * 128] = jnp.where(inside, 1.0, 0.0).astype(BF16)

    for i in range(1, NB // 2):
        shift_copy(i).wait_recv()
    quarter = sub8 % 4
    for j in range(1, CROSS + 1):
        base = 0
        for bit in range(j, CROSS):
            base = base + me // 2**bit % 2 * 2 ** (6 - bit + j)
        for low in range(2 ** (CROSS - j)):
            if j < CROSS:
                source = me % 2**j
                for bit in range(j, CROSS):
                    source = source + 2**bit * ((low >> (4 - bit)) & 1)
                row = shbuf[source, j - 1]
            else:
                row = par[LOCAL + j - 1 : LOCAL + j, :]
            row = jnp.broadcast_to(row, (8, 128))
            for high in range(2**j):
                delay = take_lanes(row, base + 2**j * quarter + high)
                idx2[j - 1, low + 2 ** (CROSS - j) * high] = (lane8 - delay) & 127

    await_parts(1)
    for k in range(2):
        pairs = recv[:, 4 + k].reshape(16, 2, 8, 128)
        even, odd = swap_halves(pairs[:, 0]), pairs[:, 1]
        gsend[k] = jnp.where(iota((16, 8, 128), 1) < 4, even, odd).reshape(128, 128)
    pl.when(has_next)(edge_copy.start)
    pl.when(has_last)(edge_copy.wait_recv)
    for k in range(2):
        own = swap_halves(recv[:, 4 + k])
        recv[:, k] = jnp.where(is_low, spread_edge(grecv[k].reshape(16, 8, 128)), own)

    await_parts(0)
    x = recv[...]
    for j, keep in ((1, 6), (2, 6), (3, 5), (4, 5), (5, 5)):
        x = major_section(x, idx2[j - 1], 2 ** (CROSS - j), keep)
    x = x * (16384.0 ** (-0.5))
    for k in range(5):
        t2[k] = x[:, k].reshape(256, 128)
    total = x[:, 1] + x[:, 2] + x[:, 3] + x[:, 4]
    total = jnp.sum(total + swap_halves(total), axis=2, keepdims=True)
    pivot = jnp.broadcast_to(total * (1.0 / 1024), (32, 8, 128))
    squares = jnp.zeros((32, 8, 128), F32)
    for k in range(5):
        centred = x[:, k] - pivot
        if k:
            squares = squares + centred * centred
        centred = centred.reshape(256, 128)
        high = centred.astype(BF16)
        hi[:, k * 128 : (k + 1) * 128] = high
        lo[:, k * 128 : (k + 1) * 128] = (centred - high.astype(F32)).astype(BF16)
    squares = jnp.sum(squares + swap_halves(squares), axis=2, keepdims=True)
    packed = jnp.where(iota((32, 8, 128), 2) == 0, pivot, jnp.broadcast_to(squares, (32, 8, 128)))
    mine = jnp.transpose(packed.reshape(256, 128))[0:8]
    stsend[...] = mine
    stbuf[t] = mine

    def stat_copy(i):
        return pltpu.make_async_remote_copy(
            src_ref=stsend, dst_ref=stbuf.at[t], send_sem=st_send.at[i], recv_sem=st_recv.at[i],
            device_id={"tm": lax.rem(t + i, NT)}, device_id_type=MESH,
        )

    for i in range(1, NT):
        stat_copy(i).start()

    def unmix(source, first, out):
        for k in range(TILES):
            for s in range(8):
                for b in range(4):
                    rows = source[first + k, pl.ds(b * 64 + s, 8, stride=8), :]
                    out[pl.ds(s % 4 * 32 + b * 8, 8), pl.ds(s // 4 * 512 + k * 128, 128)] = rows

    unmix(t2, 1, ded_ref)
    for k in range(TILES):
        at = pl.ds(k * 128, 256)
        both = jnp.dot(hi[:, at], band[...], preferred_element_type=F32)
        bc[k] = both + jnp.dot(lo[:, at], band[...], preferred_element_type=F32)

    for c in range(2):
        for k in range(NB - 1):
            part_copy(c, k).wait_send()
    for i in range(1, NB // 2):
        shift_copy(i).wait_send()
    pl.when(has_next)(halo_copy.wait_send)
    pl.when(has_next)(edge_copy.wait_send)
    for i in range(1, NT):
        stat_copy(i).wait_recv()
    means = [stbuf[i][0:1] for i in range(NT)]
    mean = sum(means) * (1.0 / NT)
    centred = [stbuf[i][1:2] + 1024.0 * ((m - mean) * (m - mean)) for i, m in enumerate(means)]
    scale = 1.0 / jnp.sqrt(sum(centred) * (1.0 / SAMPLES) + 1e-6)
    row_of = iota((8, 256), 0)
    shared = jnp.where(row_of == 0, jnp.broadcast_to(mean, (8, 256)), jnp.broadcast_to(scale, (8, 256)))
    shared = jnp.transpose(shared)
    row_mean = jnp.broadcast_to(shared[:, 0:1], (256, 128))
    row_scale = jnp.broadcast_to(shared[:, 1:2], (256, 128))
    off = pivot.reshape(256, 128) - row_mean
    for h in range(4):
        at = pl.ds(64 * h, 64)
        best = [None] * TILES
        for j in range(NBOX):
            up, down = (jnp.broadcast_to(roots[e, j][None], (8, 8, 128)).reshape(64, 128) for e in range(2))
            bias = up * off[64 * h : 64 * h + 64]
            for k in range(TILES):
                score = bc[k, at, j * 128 : (j + 1) * 128] * down + bias
                best[k] = score if j == 0 else jnp.maximum(best[k], score)
        for k in range(TILES):
            t2[k, at] = best[k] * row_scale[64 * h : 64 * h + 64]
    unmix(t2, 0, snr_ref)
    for i in range(1, NT):
        stat_copy(i).wait_send()


def store(a, b, a_hbm, b_hbm, sem):
    copies = [pltpu.make_async_copy(a, a_hbm, sem.at[0]), pltpu.make_async_copy(b, b_hbm, sem.at[1])]
    for copy in copies:
        copy.start()
    for copy in copies:
        copy.wait()


def body(intensity, shifts, boxcar_widths):
    dma = pltpu.SemaphoreType.DMA
    vmem, whole = pltpu.VMEM, pl.BlockSpec(memory_space=pl.ANY)
    in_vmem = pl.BlockSpec(memory_space=pltpu.VMEM)
    out = jax.ShapeDtypeStruct((128, 1024), F32)
    widths = jnp.pad(boxcar_widths[None], ((12, 3), (0, 128 - NBOX)))
    params = jnp.pad(shifts, ((0, 4), (0, 0))) + widths
    ded, snr = pl.pallas_call(
        kernel,
        out_shape=(out, out),
        in_specs=[whole] * 2,
        out_specs=[in_vmem] * 2,
        scratch_shapes=[
            vmem((1024, 512), BF16),
            vmem((16, 128), I32),
            vmem((4, 1, 128), I32),
            vmem((NB, 4, 1, 128), I32),
            vmem((LOCAL, 32, 8, 128), I32),
            vmem((CROSS, 32, 8, 128), I32),
            vmem((32, 6, 8, 128), F32),
            vmem((32, TILES, 8, 128), F32),
            vmem((2, 128, 128), F32),
            vmem((2, 128, 128), F32),
            vmem((2, 128, 128), F32),
            vmem((2, 128, 128), F32),
            vmem((32, 2 + TILES, 8, 128), F32),
            vmem((5, 256, 128), F32),
            vmem((256, 640), BF16),
            vmem((256, 640), BF16),
            vmem((TILES, 256, 1024), F32),
            vmem((256, 1024), BF16),
            vmem((2, NBOX, 8, 128), F32),
            vmem((8, 256), F32),
            vmem((NT, 8, 256), F32),
            dma((3,)),
            dma((NB // 2,)),
            dma((NB // 2,)),
            dma((4,)),
            dma((2, NB - 1)),
            dma((2, NB - 1)),
            dma((NT,)),
            dma((NT,)),
        ],
        compiler_params=pltpu.CompilerParams(
            collective_id=0, has_side_effects=True, vmem_limit_bytes=52 * 2**20
        ),
    )(intensity, params)
    return pl.pallas_call(
        store,
        out_shape=(out, out),
        in_specs=[in_vmem] * 2,
        out_specs=[whole] * 2,
        scratch_shapes=[dma((2,))],
        compiler_params=pltpu.CompilerParams(vmem_limit_bytes=52 * 2**20),
    )(ded, snr)


def solution(mesh):
    assert mesh.shape["band"] == NB and mesh.shape["tm"] == NT
    in_specs = (P("band", "tm"), P(None, "band"), P())
    out_specs = (P("band", "tm"), P("band", "tm"))
    return jax.shard_map(body, mesh=mesh, in_specs=in_specs, out_specs=out_specs, check_vma=False)
```

```python
import jax
import jax.numpy as jnp
from jax import lax
from jax.experimental import pallas as pl
from jax.experimental.pallas import tpu as pltpu
from jax.sharding import PartitionSpec as P

MESH = pl.DeviceIdType.MESH
F32, BF16, I32 = jnp.float32, jnp.bfloat16, jnp.int32
NB, NT = 32, 8
NBOX = 8
NCOL = 16
LOCAL, CROSS = 7, 5
TILES = 4
SAMPLES = 8192

_ROWS = lax.GatherDimensionNumbers(
    offset_dims=(),
    collapsed_slice_dims=(1,),
    start_index_map=(1,),
    operand_batching_dims=(0,),
    start_indices_batching_dims=(0,),
)


def iota(shape, dim):
    return lax.broadcasted_iota(I32, shape, dim)


def take_lanes(x, index):
    return lax.gather(
        x, index[..., None], _ROWS, (1, 1), mode=lax.GatherScatterMode.PROMISE_IN_BOUNDS
    )


def rev5(v):
    out = 0
    for k in range(5):
        out = out + (v // 2**k) % 2 * 2 ** (4 - k)
    return out


OFFSETS = sorted(
    [(dx, dz, dc) for dx in range(2) for dz in range(8) for dc in range(2)][1:],
    key=lambda o: (o[0], -min(o[1], 8 - o[1])),
)


def delay_add(firsts, seconds, index, ahead=None):
    spread = jnp.broadcast_to(index[:, None], firsts.shape).reshape(-1, 128)
    turned = take_lanes(seconds.reshape(-1, 128), spread).reshape(firsts.shape)
    last = turned[:, -1:]
    if ahead is not None:
        before = jnp.concatenate([ahead, turned[:, :-1]], axis=1)
    elif firsts.shape[1] == 1:
        return firsts + turned, last
    else:
        before = jnp.concatenate([turned[:, :1], turned[:, :-1]], axis=1)
    wraps = jnp.broadcast_to((index > iota(index.shape, 2))[:, None], firsts.shape)
    return firsts + jnp.where(wraps, before, turned), last


def major_section(x, index, apart, ahead=None):
    rows, tiles = x.shape[:2]
    shape = (rows // (2 * apart), 2, apart, tiles, 8, 128)
    pairs = x.reshape(shape)
    both = [jnp.broadcast_to(pairs[:, e : e + 1], shape).reshape(x.shape) for e in (0, 1)]
    return delay_add(*both, index, ahead)


def minor_section(x, index, apart):
    flat = x.reshape(-1, 8, 128)
    is_set = iota(flat.shape, 1) // apart % 2 == 1
    firsts = jnp.where(is_set, pltpu.roll(flat, apart, 1), flat)
    seconds = jnp.where(is_set, flat, pltpu.roll(flat, 8 - apart, 1))
    return delay_add(firsts.reshape(x.shape), seconds.reshape(x.shape), index)


def swap_halves(x):
    return pltpu.roll(x.reshape(-1, 8, 128), 4, 1).reshape(x.shape)


def kernel(
    x_hbm, par, ded_ref, snr_ref,
    xc, shsend, shbuf, idx1, idx2, l0, s7, hsend, hrecv, gsend, grecv, fsend, frecv,
    recv, extra, t2, hi, lo, bc, band, roots, stsend, stbuf,
    local_sem, shs_sem, shr_sem, halo_sem, back_send, back_recv, front_send, front_recv, st_send, st_recv,
):
    me, t = lax.axis_index("band"), lax.axis_index("tm")
    copy_x1 = pltpu.make_async_copy(x_hbm.at[:, pl.ds(512, 512)], xc.at[pl.ds(512, 512)], local_sem.at[0])
    copy_x0 = pltpu.make_async_copy(x_hbm.at[:, pl.ds(0, 512)], xc.at[pl.ds(0, 512)], local_sem.at[1])
    copy_x1.start()
    copy_x0.start()

    barrier = pltpu.get_barrier_semaphore()
    for i in range(1, NB):
        pl.semaphore_signal(barrier, inc=1, device_id={"band": lax.rem(me + i, NB)}, device_id_type=MESH)
    for i in range(1, NT):
        pl.semaphore_signal(barrier, inc=1, device_id={"tm": lax.rem(t + i, NT)}, device_id_type=MESH)

    column, place = me // NCOL, me % NCOL
    z, core = place // 2, place % 2
    later = lax.rem(t + 1, NT)
    slot = rev5(me)
    sub8, lane8 = iota((8, 128), 0), iota((8, 128), 1)

    def group_of(i, halves):
        blocks = i // 8 if halves else i // 4
        return blocks + 32 * (i // 2 % 2) + 64 * (i % 2)

    for s in range(1, LOCAL + 1):
        row = jnp.broadcast_to(par[s - 1 : s, :], (8, 128))
        if s <= 5:
            base = sub8 // 2 % 2 * 32 + sub8 % 2 * 64
        else:
            base = sub8 // 2 % 2 * (1, 2)[s - 6] + sub8 % 2 * (64, 1)[s - 6]
        for m in range(32):
            turned = int(f"{m:05b}"[::-1], 2)
            if s <= 5:
                turned = (turned >> (5 - s)) + (m >> s << s)
            else:
                turned = turned << (s - 5)
            idx1[s - 1, m] = (lane8 - take_lanes(row, base + turned)) & 127
    for j in range(CROSS - 1):
        shsend[j] = par[LOCAL + j : LOCAL + j + 1, :]
        shbuf[me, j] = par[LOCAL + j : LOCAL + j + 1, :]

    i = iota((256, 1024), 0)
    target = i // 4 % 2 * 128 + group_of(i, True)
    presum = jnp.where(iota((256, 1024), 1) // 4 == target, 1.0, 0.0).astype(BF16)
    i = iota((128, 512), 0)
    presum_edge = jnp.where(iota((128, 512), 1) // 4 == group_of(i, False), 1.0, 0.0).astype(BF16)
    copy_x1.wait()
    copy_x0.wait()
    level = jnp.dot(presum, xc[...], preferred_element_type=F32)
    for k in range(TILES):
        l0[:, 2 + k] = level[:, k * 128 : (k + 1) * 128].reshape(32, 8, 128)
    edge = jnp.dot(presum_edge, xc[512:1024, 256:512], preferred_element_type=F32)
    for k in range(2):
        hsend[:, k] = edge[:, k * 128 : (k + 1) * 128].reshape(16, 8, 128)

    def local_sections(first):
        x = l0[:, first : first + 4]
        for s in range(1, LOCAL + 1):
            if s <= 5:
                x = major_section(x, idx1[s - 1], 2 ** (s - 1))[0]
            else:
                x = minor_section(x, idx1[s - 1], 2 ** (7 - s))[0]
            if s in (3, 7):
                x = x[:, 1:]
        return x

    def dest_of(k):
        dx, dz, dc = OFFSETS[k]
        return (column + dx) % 2 * NCOL + (z + dz) % 8 * 2 + (core + dc) % 2

    def back_copy(k):
        dest = dest_of(k)
        return pltpu.make_async_remote_copy(
            src_ref=s7.at[dest], dst_ref=recv.at[slot // 2, slot % 2],
            send_sem=back_send.at[k], recv_sem=back_recv.at[k],
            device_id={"band": dest}, device_id_type=MESH,
        )

    def front_copy(half, k):
        dest = dest_of(k)
        return pltpu.make_async_remote_copy(
            src_ref=fsend.at[half, dest], dst_ref=frecv.at[half, slot // 2, slot % 2],
            send_sem=front_send.at[half, k], recv_sem=front_recv.at[half, k],
            device_id={"band": dest}, device_id_type=MESH,
        )

    own_first = range(NB - 1)
    own_last = [*range(NCOL - 1, NB - 1), *range(NCOL - 1)]

    def start_front(half):
        for k in own_last:
            front_copy(half, k).start()
        frecv[half, slot // 2, slot % 2] = fsend[half, me]

    def shift_copy(i):
        return pltpu.make_async_remote_copy(
            src_ref=shsend, dst_ref=shbuf.at[me], send_sem=shs_sem.at[i], recv_sem=shr_sem.at[i],
            device_id={"band": lax.rem(me + 2 * i, NB)}, device_id_type=MESH,
        )

    halo_copy = pltpu.make_async_remote_copy(
        src_ref=hsend, dst_ref=hrecv, send_sem=halo_sem.at[0], recv_sem=halo_sem.at[1],
        device_id={"tm": later}, device_id_type=MESH,
    )
    edge_copies = [
        pltpu.make_async_remote_copy(
            src_ref=gsend.at[e], dst_ref=grecv.at[e],
            send_sem=halo_sem.at[2 + 2 * e], recv_sem=halo_sem.at[3 + 2 * e],
            device_id={"tm": later}, device_id_type=MESH,
        )
        for e in range(2)
    ]
    has_next, has_last = t < NT - 1, t > 0

    s7[...] = local_sections(2)
    pl.semaphore_wait(barrier, NB + NT - 2)
    pl.when(has_next)(halo_copy.start)
    for i in range(1, NB // 2):
        shift_copy(i).start()
    for k in own_first:
        back_copy(k).start()
    recv[slot // 2, slot % 2] = s7[me]

    before = jnp.dot(presum[:, 512:], xc[0:512, 256:512], preferred_element_type=F32)
    for k in range(2):
        l0[:, k] = before[:, k * 128 : (k + 1) * 128].reshape(32, 8, 128)
    is_low = iota((32, 8, 128), 1) < 4

    def pack(two_tiles, half):
        first, second = two_tiles
        return jnp.where(is_low, *((swap_halves(first), second) if half else (first, swap_halves(second))))

    x = local_sections(0)
    for half in range(2):
        fsend[half] = pack((x[:, 0], x[:, 1]), half)
    start_front(1)

    @pl.when(t == 0)
    def _():
        hrecv[...] = jnp.zeros(hrecv.shape, F32)
        grecv[...] = jnp.zeros(grecv.shape, F32)

    pl.when(has_last)(halo_copy.wait_recv)
    def spread_edge(packed):
        return jnp.stack([packed, swap_halves(packed)], axis=1).reshape(-1, 8, 128)

    x = hrecv[...]
    empty = jnp.zeros((16, 1, 8, 128), F32)
    for s in range(1, LOCAL + 1):
        pairs = idx1[s - 1].reshape(16, 2, 8, 128)
        index = jnp.where(iota((16, 8, 128), 1) < 4, pairs[:, 0], pairs[:, 1])
        if s in (1, 5):
            x = jnp.concatenate([x, empty], axis=1)
        if 2 <= s <= 5:
            x = major_section(x, index, 2 ** (s - 2))[0]
        else:
            x = minor_section(x, index, 4 if s == 1 else 2 ** (7 - s))[0]
        if s in (3, 7):
            x = x[:, 1:]
    fsend[0] = fsend[0] + pack((spread_edge(x[:, 0]), spread_edge(x[:, 1])), 0)
    start_front(0)

    offset, sample = iota((256, 128), 0) - 128, iota((256, 128), 1)
    row = jnp.broadcast_to(par[12:13, :], (8, 128))
    for j in range(NBOX):
        width = take_lanes(row, jnp.full((8, 128), j, I32))
        root = jnp.sqrt(width.astype(F32))
        roots[0, j] = root
        roots[1, j] = 1.0 / root
        width = jnp.broadcast_to(width[None], (32, 8, 128)).reshape(256, 128)
        inside = (offset <= sample) & (offset > sample - width)
        band[:, j * 128 : (j + 1) * 128] = jnp.where(inside, 1.0, 0.0).astype(BF16)

    for i in range(1, NB // 2):
        shift_copy(i).wait_recv()
    quarter = sub8 % 4
    for j in range(1, CROSS + 1):
        base = 0
        for bit in range(j, CROSS):
            base = base + me // 2**bit % 2 * 2 ** (6 - bit + j)
        for low in range(2 ** (CROSS - j)):
            if j < CROSS:
                source = me % 2**j
                for bit in range(j, CROSS):
                    source = source + 2**bit * ((low >> (4 - bit)) & 1)
                row = shbuf[source, j - 1]
            else:
                row = par[LOCAL + j - 1 : LOCAL + j, :]
            row = jnp.broadcast_to(row, (8, 128))
            for high in range(2**j):
                delay = take_lanes(row, base + 2**j * quarter + high)
                idx2[j - 1, low + 2 ** (CROSS - j) * high] = (lane8 - delay) & 127

    parity = [column, 1 - column]
    for e in range(2):
        for k in range(NCOL - 1) if e == 0 else range(NCOL - 1, NB - 1):
            back_copy(k).wait_recv()
        for k in range(2):
            pairs = recv[:, pl.ds(parity[e], 1), k].reshape(8, 2, 8, 128)
            gsend[e, k] = jnp.where(iota((8, 8, 128), 1) < 4, swap_halves(pairs[:, 0]), pairs[:, 1])
        pl.when(has_next)(edge_copies[e].start)

    x = recv[...].reshape(32, 2, 8, 128)
    for j in range(1, CROSS):
        x = major_section(x, idx2[j - 1], 2 ** (CROSS - j))[0]
    tail = x[:, 1:]

    x = jnp.stack([swap_halves(recv[:, :, k].reshape(32, 8, 128)) for k in range(2)], axis=1)
    x = jnp.where(jnp.broadcast_to(is_low[:, None], x.shape), 0.0, x)
    aheads = []
    for j in range(1, CROSS + 1):
        x, ahead = major_section(x, idx2[j - 1], 2 ** (CROSS - j))
        aheads.append(ahead)
        if j == 3:
            x = x[:, 1:]
    front = x

    def add_edge():
        for copy in edge_copies:
            pl.when(has_last)(copy.wait_recv)
        x = jnp.stack([grecv[column if f == 0 else 1 - column] for f in range(2)])
        x = jnp.stack([x[:, 0].reshape(16, 8, 128), x[:, 1].reshape(16, 8, 128)], axis=1)
        for j in range(1, CROSS + 1):
            rows = idx2[j - 1].reshape(8, 2, 2, 8, 128)
            index = [jnp.where(iota((8, 8, 128), 1) < 4, rows[:, 0, f], rows[:, 1, f]) for f in range(2)]
            index = jnp.concatenate(index, axis=0)
            if j in (1, CROSS):
                x = jnp.concatenate([x, jnp.zeros((16, 1, 8, 128), F32)], axis=1)
            if j == 4:
                x = minor_section(x, index, 4)[0]
            else:
                x = major_section(x, index, 8 if j == CROSS else 2 ** (3 - j))[0]
            if j == 3:
                x = x[:, 1:]
        for k in range(3):
            parts = [jnp.stack([p, swap_halves(p)], axis=1) for p in (x[:8, k], x[8:, k])]
            added = jnp.stack(parts, axis=2).reshape(32, 8, 128)
            extra[:, k] = jnp.where(is_low, added, 0.0)

    is_late = t == NT // 2
    pl.when(jnp.logical_not(is_late))(add_edge)

    for half in (1, 0):
        for k in range(NB - 1):
            front_copy(half, k).wait_recv()
    low, high = (frecv[half].reshape(32, 8, 128) for half in range(2))
    first = jnp.where(is_low, low, swap_halves(high))
    second = jnp.where(is_low, swap_halves(low), high)
    x = jnp.stack([first, second, recv[:, :, 0].reshape(32, 8, 128)], axis=1)
    for j in range(1, CROSS + 1):
        if j == CROSS:
            x = jnp.concatenate([x, tail], axis=1)
        x = major_section(x, idx2[j - 1], 2 ** (CROSS - j), aheads[j - 1])[0]
    pl.when(is_late)(add_edge)
    x = [x[:, k] + extra[:, k + 1] if k < 2 else x[:, k] for k in range(TILES)]
    x = jnp.stack([front[:, 0] + extra[:, 0], *x], axis=1) * (16384.0 ** (-0.5))
    for k in range(5):
        t2[k] = x[:, k].reshape(256, 128)
    total = x[:, 1] + x[:, 2] + x[:, 3] + x[:, 4]
    total = jnp.sum(total + swap_halves(total), axis=2, keepdims=True)
    pivot = jnp.broadcast_to(total * (1.0 / 1024), (32, 8, 128))
    squares = jnp.zeros((32, 8, 128), F32)
    for k in range(5):
        centred = x[:, k] - pivot
        if k:
            squares = squares + centred * centred
        centred = centred.reshape(256, 128)
        high = centred.astype(BF16)
        hi[:, k * 128 : (k + 1) * 128] = high
        lo[:, k * 128 : (k + 1) * 128] = (centred - high.astype(F32)).astype(BF16)
    squares = jnp.sum(squares + swap_halves(squares), axis=2, keepdims=True)
    packed = jnp.where(iota((32, 8, 128), 2) == 0, pivot, jnp.broadcast_to(squares, (32, 8, 128)))
    mine = jnp.transpose(packed.reshape(256, 128))[0:8]
    stsend[...] = mine
    stbuf[t] = mine

    def stat_copy(i):
        return pltpu.make_async_remote_copy(
            src_ref=stsend, dst_ref=stbuf.at[t], send_sem=st_send.at[i], recv_sem=st_recv.at[i],
            device_id={"tm": lax.rem(t + i, NT)}, device_id_type=MESH,
        )

    for i in range(1, NT):
        stat_copy(i).start()

    def unmix(source, first, out):
        for k in range(TILES):
            for s in range(8):
                for b in range(4):
                    rows = source[first + k, pl.ds(b * 64 + s, 8, stride=8), :]
                    out[pl.ds(s % 4 * 32 + b * 8, 8), pl.ds(s // 4 * 512 + k * 128, 128)] = rows

    unmix(t2, 1, ded_ref)
    for k in range(TILES):
        at = pl.ds(k * 128, 256)
        both = jnp.dot(hi[:, at], band[...], preferred_element_type=F32)
        both = both + jnp.dot(lo[:, at], band[...], preferred_element_type=F32)
        for j in range(NBOX):
            part = both[:, j * 128 : (j + 1) * 128].reshape(32, 8, 128)
            bc[k, j] = (part * jnp.broadcast_to(roots[1, j][None], part.shape)).reshape(256, 128)

    for k in range(NB - 1):
        back_copy(k).wait_send()
        for half in range(2):
            front_copy(half, k).wait_send()
    for i in range(1, NB // 2):
        shift_copy(i).wait_send()
    pl.when(has_next)(halo_copy.wait_send)
    for e in range(2):
        pl.when(has_next)(edge_copies[e].wait_send)
    for i in range(1, NT):
        stat_copy(i).wait_recv()
    means = [stbuf[i][0:1] for i in range(NT)]
    mean = sum(means) * (1.0 / NT)
    centred = [stbuf[i][1:2] + 1024.0 * ((m - mean) * (m - mean)) for i, m in enumerate(means)]
    scale = 1.0 / jnp.sqrt(sum(centred) * (1.0 / SAMPLES) + 1e-6)
    row_of = iota((8, 256), 0)
    shared = jnp.where(row_of == 0, jnp.broadcast_to(mean, (8, 256)), jnp.broadcast_to(scale, (8, 256)))
    shared = jnp.transpose(shared)
    row_mean = jnp.broadcast_to(shared[:, 0:1], (256, 128))
    row_scale = jnp.broadcast_to(shared[:, 1:2], (256, 128))
    off = pivot.reshape(256, 128) - row_mean
    for h in range(8):
        at = pl.ds(32 * h, 32)
        best = [None] * TILES
        for j in range(NBOX):
            up = jnp.broadcast_to(roots[0, j][None], (4, 8, 128)).reshape(32, 128)
            bias = up * off[32 * h : 32 * h + 32]
            for k in range(TILES):
                score = bc[k, j, at] + bias
                best[k] = score if j == 0 else jnp.maximum(best[k], score)
        for k in range(TILES):
            t2[k, at] = best[k] * row_scale[32 * h : 32 * h + 32]
    unmix(t2, 0, snr_ref)
    for i in range(1, NT):
        stat_copy(i).wait_send()


def store(a, b, a_hbm, b_hbm, sem):
    copies = [pltpu.make_async_copy(a, a_hbm, sem.at[0]), pltpu.make_async_copy(b, b_hbm, sem.at[1])]
    for copy in copies:
        copy.start()
    for copy in copies:
        copy.wait()


def body(intensity, shifts, boxcar_widths):
    dma = pltpu.SemaphoreType.DMA
    vmem, whole = pltpu.VMEM, pl.BlockSpec(memory_space=pl.ANY)
    in_vmem = pl.BlockSpec(memory_space=pltpu.VMEM)
    out = jax.ShapeDtypeStruct((128, 1024), F32)
    params = jnp.pad(shifts, ((0, 4), (0, 0)))
    params = lax.dynamic_update_slice(params, boxcar_widths[None], (12, 0))
    ded, snr = pl.pallas_call(
        kernel,
        out_shape=(out, out),
        in_specs=[whole, in_vmem],
        out_specs=[in_vmem] * 2,
        scratch_shapes=[
            vmem((1024, 512), BF16),
            vmem((4, 1, 128), I32),
            vmem((NB, 4, 1, 128), I32),
            vmem((LOCAL, 32, 8, 128), I32),
            vmem((CROSS, 32, 8, 128), I32),
            vmem((32, 6, 8, 128), F32),
            vmem((32, 2, 8, 128), F32),
            vmem((16, 2, 8, 128), F32),
            vmem((16, 2, 8, 128), F32),
            vmem((2, 2, 8, 8, 128), F32),
            vmem((2, 2, 8, 8, 128), F32),
            vmem((2, 32, 8, 128), F32),
            vmem((2, 16, 2, 8, 128), F32),
            vmem((16, 2, 2, 8, 128), F32),
            vmem((32, 3, 8, 128), F32),
            vmem((5, 256, 128), F32),
            vmem((256, 640), BF16),
            vmem((256, 640), BF16),
            vmem((TILES, NBOX, 256, 128), F32),
            vmem((256, 1024), BF16),
            vmem((2, NBOX, 8, 128), F32),
            vmem((8, 256), F32),
            vmem((NT, 8, 256), F32),
            dma((2,)),
            dma((NB // 2,)),
            dma((NB // 2,)),
            dma((6,)),
            dma((NB - 1,)),
            dma((NB - 1,)),
            dma((2, NB - 1)),
            dma((2, NB - 1)),
            dma((NT,)),
            dma((NT,)),
        ],
        compiler_params=pltpu.CompilerParams(
            collective_id=0, has_side_effects=True, vmem_limit_bytes=52 * 2**20
        ),
    )(intensity, params)
    return pl.pallas_call(
        store,
        out_shape=(out, out),
        in_specs=[in_vmem] * 2,
        out_specs=[whole] * 2,
        scratch_shapes=[dma((2,))],
        compiler_params=pltpu.CompilerParams(vmem_limit_bytes=52 * 2**20),
    )(ded, snr)


def solution(mesh):
    assert mesh.shape["band"] == NB and mesh.shape["tm"] == NT
    in_specs = (P("band", "tm"), P(None, "band"), P())
    out_specs = (P("band", "tm"), P("band", "tm"))
    return jax.shard_map(body, mesh=mesh, in_specs=in_specs, out_specs=out_specs, check_vma=False)
```

```python
import jax
import jax.numpy as jnp
from jax import lax
from jax.experimental import pallas as pl
from jax.experimental.pallas import tpu as pltpu
from jax.sharding import PartitionSpec as P

MESH = pl.DeviceIdType.MESH
F32, BF16, I32 = jnp.float32, jnp.bfloat16, jnp.int32
NB, NT = 32, 8
NBOX = 8
NCOL = 16
LOCAL, CROSS = 7, 5
TILES = 4
SAMPLES = 8192

_ROWS = lax.GatherDimensionNumbers(
    offset_dims=(),
    collapsed_slice_dims=(1,),
    start_index_map=(1,),
    operand_batching_dims=(0,),
    start_indices_batching_dims=(0,),
)


def iota(shape, dim):
    return lax.broadcasted_iota(I32, shape, dim)


def take_lanes(x, index):
    return lax.gather(
        x, index[..., None], _ROWS, (1, 1), mode=lax.GatherScatterMode.PROMISE_IN_BOUNDS
    )


def rev5(v):
    out = 0
    for k in range(5):
        out = out + (v // 2**k) % 2 * 2 ** (4 - k)
    return out


OFFSETS = sorted(
    [(dx, dz, dc) for dx in range(2) for dz in range(8) for dc in range(2)][1:],
    key=lambda o: (o[0], -min(o[1], 8 - o[1])),
)


def delay_add(firsts, seconds, index, ahead=None):
    spread = jnp.broadcast_to(index[:, None], firsts.shape).reshape(-1, 128)
    turned = take_lanes(seconds.reshape(-1, 128), spread).reshape(firsts.shape)
    last = turned[:, -1:]
    if ahead is not None:
        before = jnp.concatenate([ahead, turned[:, :-1]], axis=1)
    elif firsts.shape[1] == 1:
        return firsts + turned, last
    else:
        before = jnp.concatenate([turned[:, :1], turned[:, :-1]], axis=1)
    wraps = jnp.broadcast_to((index > iota(index.shape, 2))[:, None], firsts.shape)
    return firsts + jnp.where(wraps, before, turned), last


def major_section(x, index, apart, ahead=None):
    rows, tiles = x.shape[:2]
    shape = (rows // (2 * apart), 2, apart, tiles, 8, 128)
    pairs = x.reshape(shape)
    both = [jnp.broadcast_to(pairs[:, e : e + 1], shape).reshape(x.shape) for e in (0, 1)]
    return delay_add(*both, index, ahead)


def folded_section(x, index, apart, grow):
    rows, tiles = x.shape[:2]
    shape = (rows // (2 * apart), 2, apart, tiles, 8, 128)
    pairs = x.reshape(shape)
    firsts, seconds = (jnp.broadcast_to(pairs[:, e : e + 1], shape).reshape(x.shape) for e in (0, 1))
    spread = jnp.broadcast_to(index[:, None], x.shape).reshape(-1, 128)
    turned = take_lanes(seconds.reshape(-1, 128), spread).reshape(x.shape)
    swapped = swap_halves(turned)
    is_low, wraps = iota(index.shape, 1) < 4, index > iota(index.shape, 2)
    empty, outs = jnp.zeros(index.shape, F32), []
    for v in range(tiles + grow):
        before = jnp.where(is_low, swapped[:, v - 1] if v else empty, swapped[:, v] if v < tiles else empty)
        if v < tiles:
            outs.append(firsts[:, v] + jnp.where(wraps, before, turned[:, v]))
        else:
            outs.append(jnp.where(wraps, before, 0.0))
    return jnp.stack(outs, axis=1)


def minor_section(x, index, apart):
    flat = x.reshape(-1, 8, 128)
    is_set = iota(flat.shape, 1) // apart % 2 == 1
    firsts = jnp.where(is_set, pltpu.roll(flat, apart, 1), flat)
    seconds = jnp.where(is_set, flat, pltpu.roll(flat, 8 - apart, 1))
    return delay_add(firsts.reshape(x.shape), seconds.reshape(x.shape), index)


def swap_halves(x):
    return pltpu.roll(x.reshape(-1, 8, 128), 4, 1).reshape(x.shape)


def kernel(
    x_hbm, par, ded_ref, snr_ref,
    xc, shsend, shbuf, idx1, idx2, l0, s7, hsend, hrecv, grecv, fsend, frecv,
    recv, extra, t2, hi, lo, bc, band, roots, stsend, stbuf,
    local_sem, shs_sem, shr_sem, halo_sem, main_send, main_recv, front_send, front_recv, st_send, st_recv,
):
    me, t = lax.axis_index("band"), lax.axis_index("tm")
    copies_x = [
        pltpu.make_async_copy(x_hbm.at[pl.ds(128 * i, 128)], xc.at[pl.ds(128 * i, 128)], local_sem.at[i])
        for i in range(4)
    ]
    for copy in copies_x:
        copy.start()

    barrier = pltpu.get_barrier_semaphore()
    for i in range(1, NB):
        pl.semaphore_signal(barrier, inc=1, device_id={"band": lax.rem(me + i, NB)}, device_id_type=MESH)
    for i in range(1, NT):
        pl.semaphore_signal(barrier, inc=1, device_id={"tm": lax.rem(t + i, NT)}, device_id_type=MESH)

    column, place = me // NCOL, me % NCOL
    z, core = place // 2, place % 2
    later = lax.rem(t + 1, NT)
    slot = rev5(me)
    sub8, lane8 = iota((8, 128), 0), iota((8, 128), 1)

    ones = jnp.ones((128, 128), BF16)
    for s in range(1, LOCAL + 1):
        row = jnp.broadcast_to(par[s - 1 : s, :].astype(F32), (8, 128))
        if s <= 5:
            base = sub8 // 2 % 2 * 32 + sub8 % 2 * 64
        else:
            base = sub8 // 2 % 2 * (1, 2)[s - 6] + sub8 % 2 * (64, 1)[s - 6]
        picks = []
        for m in range(32):
            turned = int(f"{m:05b}"[::-1], 2)
            if s <= 5:
                turned = (turned >> (5 - s)) + (m >> s << s)
            else:
                turned = turned << (s - 5)
            picks.append(jnp.where(lane8 - base == turned, row, 0.0))
        picks = jnp.stack(picks).reshape(256, 128).astype(BF16)
        delay = jnp.dot(picks, ones, preferred_element_type=F32).astype(I32)
        idx1[s - 1] = ((iota((256, 128), 1) - delay) & 127).reshape(32, 8, 128)
    for j in range(CROSS - 1):
        shsend[j] = par[LOCAL + j : LOCAL + j + 1, :]
        shbuf[me, j] = par[LOCAL + j : LOCAL + j + 1, :]

    is_low = iota((32, 8, 128), 1) < 4
    i = iota((128, 512), 0)
    group = i // 4 + 32 * (i // 2 % 2) + 64 * (i % 2)
    presum = jnp.where(iota((128, 512), 1) // 4 == group, 1.0, 0.0).astype(BF16)
    level = 0.0
    for i in range(2):
        copies_x[2 * i].wait()
        copies_x[2 * i + 1].wait()
        at = pl.ds(256 * i, 256)
        level = level + jnp.dot(presum[:, 256 * i : 256 * i + 256], xc[at], preferred_element_type=F32)
    for k in range(TILES):
        low, high = (level[:, c * 128 : c * 128 + 128].reshape(16, 8, 128) for c in (k, k + 4))
        if k >= 2:
            hsend[:, k - 2] = high
        low, high = (jnp.stack([p, swap_halves(p)], axis=1).reshape(32, 8, 128) for p in (low, swap_halves(high)))
        l0[:, 2 + k] = jnp.where(is_low, low, high)
        if k >= 2:
            l0[:, k - 2] = jnp.where(is_low, 0.0, swap_halves(low))

    def pack(two_tiles, half):
        first, second = two_tiles
        return jnp.where(is_low, *((swap_halves(first), second) if half else (first, swap_halves(second))))

    def dest_of(k):
        dx, dz, dc = OFFSETS[k]
        return (column + dx) % 2 * NCOL + (z + dz) % 8 * 2 + (core + dc) % 2

    def main_copy(part, k):
        dest, which = dest_of(k), (pl.ds(0, 1), pl.ds(1, 2))[part]
        return pltpu.make_async_remote_copy(
            src_ref=s7.at[dest, which], dst_ref=recv.at[slot // 2, slot % 2, which],
            send_sem=main_send.at[part, k], recv_sem=main_recv.at[part, k],
            device_id={"band": dest}, device_id_type=MESH,
        )

    def front_copy(k):
        dest = dest_of(k)
        return pltpu.make_async_remote_copy(
            src_ref=fsend.at[dest], dst_ref=frecv.at[slot // 2, slot % 2],
            send_sem=front_send.at[k], recv_sem=front_recv.at[k],
            device_id={"band": dest}, device_id_type=MESH,
        )

    own, other = range(NCOL - 1), range(NCOL - 1, NB - 1)
    edges_first = t % 4 == 3

    def start_all(copies):
        for copy in copies:
            copy.start()

    def shift_copy(i):
        needed = pl.ds(0, (i & -i).bit_length())
        return pltpu.make_async_remote_copy(
            src_ref=shsend.at[needed], dst_ref=shbuf.at[me, needed], send_sem=shs_sem.at[i], recv_sem=shr_sem.at[i],
            device_id={"band": lax.rem(me + 2 * i, NB)}, device_id_type=MESH,
        )

    halo_copy = pltpu.make_async_remote_copy(
        src_ref=hsend, dst_ref=hrecv, send_sem=halo_sem.at[0], recv_sem=halo_sem.at[1],
        device_id={"tm": later}, device_id_type=MESH,
    )
    edge_copies = [
        pltpu.make_async_remote_copy(
            src_ref=recv.at[:, column if e == 0 else 1 - column, 0], dst_ref=grecv.at[e],
            send_sem=halo_sem.at[2 + 2 * e], recv_sem=halo_sem.at[3 + 2 * e],
            device_id={"tm": later}, device_id_type=MESH,
        )
        for e in range(2)
    ]
    has_next, has_last = t < NT - 1, t > 0

    def local_sections(first):
        x = l0[:, first : first + 4]
        for s in range(1, LOCAL + 1):
            if s <= 5:
                x = major_section(x, idx1[s - 1], 2 ** (s - 1))[0]
            else:
                x = minor_section(x, idx1[s - 1], 2 ** (7 - s))[0]
            if s in (3, 7):
                x = x[:, 1:]
        return x[:, 0], x[:, 1]

    tiles = local_sections(2)
    s7[:, 0] = pack(tiles, 1)
    s7[:, 1] = pack(tiles, 0)
    pl.semaphore_wait(barrier, NB + NT - 2)
    pl.when(has_next)(halo_copy.start)
    for i in range(1, NB // 2):
        shift_copy(i).start()
    start_all(main_copy(0, k) for k in [*own, *other])
    tiles = local_sections(0)
    s7[:, 2] = pack(tiles, 1)
    fsend[...] = pack(tiles, 0)
    pl.when(jnp.logical_not(edges_first))(lambda: start_all(main_copy(1, k) for k in other))
    start_all(main_copy(1, k) for k in own)
    pl.when(edges_first)(lambda: start_all(main_copy(1, k) for k in other))
    recv[slot // 2, slot % 2] = s7[me]

    offset, sample = iota((256, 128), 0) - 128, iota((256, 128), 1)
    row = jnp.broadcast_to(par[12:13, :], (8, 128))
    for j in range(NBOX):
        width = take_lanes(row, jnp.full((8, 128), j, I32))
        root = jnp.sqrt(width.astype(F32))
        roots[0, j] = root
        roots[1, j] = 1.0 / root
        width = jnp.broadcast_to(width[None], (32, 8, 128)).reshape(256, 128)
        inside = (offset <= sample) & (offset > sample - width)
        band[:, j * 128 : (j + 1) * 128] = jnp.where(inside, 1.0, 0.0).astype(BF16)

    @pl.when(t == 0)
    def _():
        hrecv[...] = jnp.zeros(hrecv.shape, F32)
        grecv[...] = jnp.zeros(grecv.shape, F32)

    pl.when(has_last)(halo_copy.wait_recv)
    def spread_edge(packed):
        return jnp.stack([packed, swap_halves(packed)], axis=1).reshape(-1, 8, 128)

    x = hrecv[...]
    empty = jnp.zeros((16, 1, 8, 128), F32)
    for s in range(1, LOCAL + 1):
        pairs = idx1[s - 1].reshape(16, 2, 8, 128)
        index = jnp.where(iota((16, 8, 128), 1) < 4, pairs[:, 0], pairs[:, 1])
        if s in (1, 5):
            x = jnp.concatenate([x, empty], axis=1)
        if 2 <= s <= 5:
            x = major_section(x, index, 2 ** (s - 2))[0]
        else:
            x = minor_section(x, index, 4 if s == 1 else 2 ** (7 - s))[0]
        if s in (3, 7):
            x = x[:, 1:]
    fsend[...] = fsend[...] + pack((spread_edge(x[:, 0]), spread_edge(x[:, 1])), 0)
    start_all(front_copy(k) for k in [*other, *own])
    frecv[slot // 2, slot % 2] = fsend[me]

    for e in range(2):
        for k in other if e else own:
            main_copy(0, k).wait_recv()
        pl.when(has_next)(edge_copies[e].start)

    for i in range(1, NB // 2):
        shift_copy(i).wait_recv()
    quarter = sub8 % 4
    for j in range(1, CROSS + 1):
        base = 0
        for bit in range(j, CROSS):
            base = base + me // 2**bit % 2 * 2 ** (6 - bit + j)
        for low in range(2 ** (CROSS - j)):
            if j < CROSS:
                source = me % 2**j
                for bit in range(j, CROSS):
                    source = source + 2**bit * ((low >> (4 - bit)) & 1)
                row = shbuf[source, j - 1]
            else:
                row = par[LOCAL + j - 1 : LOCAL + j, :]
            row = jnp.broadcast_to(row, (8, 128))
            for high in range(2**j):
                delay = take_lanes(row, base + 2**j * quarter + high)
                idx2[j - 1, low + 2 ** (CROSS - j) * high] = (lane8 - delay) & 127

    def add_edge():
        for copy in edge_copies:
            pl.when(has_last)(copy.wait_recv)
        x = jnp.stack([grecv[column if f == 0 else 1 - column] for f in range(2)], axis=1).reshape(32, 1, 8, 128)
        for j in range(1, CROSS + 1):
            x = folded_section(x, idx2[j - 1], 2 ** (CROSS - j), j == 1)
        for k, part in enumerate([swap_halves(x[:, 0]), x[:, 1], swap_halves(x[:, 1])]):
            extra[:, k] = part

    is_late = t == NT // 2
    pl.when(jnp.logical_not(is_late))(add_edge)

    for k in [*other, *own]:
        main_copy(1, k).wait_recv()

    def unpack(low, high):
        return jnp.where(is_low, low, swap_halves(high)), jnp.where(is_low, swap_halves(low), high)

    back = unpack(recv[:, :, 1].reshape(32, 8, 128), recv[:, :, 0].reshape(32, 8, 128))
    x = swap_halves(jnp.stack(back, axis=1))
    x = jnp.where(jnp.broadcast_to(is_low[:, None], x.shape), 0.0, x)
    aheads = []
    for j in range(1, CROSS + 1):
        x, ahead = major_section(x, idx2[j - 1], 2 ** (CROSS - j))
        aheads.append(ahead)
        if j == 3:
            x = x[:, 1:]
    front = x

    high = recv[:, :, 2].reshape(32, 8, 128)
    x = jnp.stack([jnp.where(is_low, 0.0, swap_halves(high)), jnp.where(is_low, 0.0, high), *back], axis=1)
    for j in range(1, CROSS + 1):
        x = major_section(x, idx2[j - 1], 2 ** (CROSS - j), aheads[j - 1])[0]
    norm = 16384.0 ** (-0.5)
    x = jnp.concatenate([front, x], axis=1) * norm
    total = x[:, 1] + x[:, 2] + x[:, 3] + x[:, 4]
    total = jnp.sum(jnp.where(is_low, 0.0, total), axis=2, keepdims=True)
    pivot = jnp.broadcast_to(total * (1.0 / 512), (32, 8, 128))
    pivot = pivot + swap_halves(pivot)

    for k in range(NB - 1):
        front_copy(k).wait_recv()
    y = frecv[...].reshape(32, 1, 8, 128)
    for j in range(1, CROSS + 1):
        y = folded_section(y, idx2[j - 1], 2 ** (CROSS - j), j == 1)
    pl.when(is_late)(add_edge)
    added = [extra[:, 0], extra[:, 1] + y[:, 0], extra[:, 2] + swap_halves(y[:, 0]), y[:, 1], swap_halves(y[:, 1])]
    x = x + jnp.stack([jnp.where(is_low, part, 0.0) * norm for part in added], axis=1)
    centred = x - jnp.broadcast_to(pivot[:, None], x.shape)
    sums, squares = centred[:, 1], centred[:, 1] * centred[:, 1]
    for k in range(2, 5):
        sums = sums + centred[:, k]
        squares = squares + centred[:, k] * centred[:, k]
    sums = jnp.broadcast_to(jnp.sum(sums + swap_halves(sums), axis=2, keepdims=True), (32, 8, 128))
    squares = jnp.broadcast_to(jnp.sum(squares + swap_halves(squares), axis=2, keepdims=True), (32, 8, 128))
    squares = squares - sums * sums * (1.0 / 1024)
    sums = pivot + sums * (1.0 / 1024)
    packed = jnp.where(iota((32, 8, 128), 2) == 0, sums, squares)
    mine = jnp.transpose(packed.reshape(256, 128))[0:2]
    stsend[...] = mine
    stbuf[t] = mine

    def stat_copy(i):
        return pltpu.make_async_remote_copy(
            src_ref=stsend, dst_ref=stbuf.at[t], send_sem=st_send.at[i], recv_sem=st_recv.at[i],
            device_id={"tm": lax.rem(t + i, NT)}, device_id_type=MESH,
        )

    for i in range(1, NT):
        stat_copy(i).start()

    def unmix(source, first, out):
        for k in range(TILES):
            for s in range(8):
                for b in range(4):
                    rows = source[first + k, pl.ds(b * 64 + s, 8, stride=8), :]
                    out[pl.ds(s % 4 * 32 + b * 8, 8), pl.ds(s // 4 * 512 + k * 128, 128)] = rows

    for k in range(5):
        t2[k] = x[:, k].reshape(256, 128)
        part = centred[:, k].reshape(256, 128)
        high = part.astype(BF16)
        hi[:, k * 128 : (k + 1) * 128] = high
        lo[:, k * 128 : (k + 1) * 128] = (part - high.astype(F32)).astype(BF16)
    unmix(t2, 1, ded_ref)
    for k in range(TILES):
        at = pl.ds(k * 128, 256)
        both = jnp.dot(hi[:, at], band[...], preferred_element_type=F32)
        both = both + jnp.dot(lo[:, at], band[...], preferred_element_type=F32)
        for j in range(NBOX):
            part = both[:, j * 128 : (j + 1) * 128].reshape(32, 8, 128)
            bc[k, j] = (part * jnp.broadcast_to(roots[1, j][None], part.shape)).reshape(256, 128)

    for k in range(NB - 1):
        main_copy(0, k).wait_send()
        main_copy(1, k).wait_send()
        front_copy(k).wait_send()
    for i in range(1, NB // 2):
        shift_copy(i).wait_send()
    pl.when(has_next)(halo_copy.wait_send)
    for e in range(2):
        pl.when(has_next)(edge_copies[e].wait_send)
    for i in range(1, NT):
        stat_copy(i).wait_recv()
    means = [stbuf[i][0:1] for i in range(NT)]
    mean = sum(means) * (1.0 / NT)
    centred = [stbuf[i][1:2] + 1024.0 * ((m - mean) * (m - mean)) for i, m in enumerate(means)]
    scale = 1.0 / jnp.sqrt(sum(centred) * (1.0 / SAMPLES) + 1e-6)
    row_mean = jnp.transpose(jnp.broadcast_to(mean, (128, 256)))
    row_scale = jnp.transpose(jnp.broadcast_to(scale, (128, 256)))
    off = pivot.reshape(256, 128) - row_mean
    for h in range(8):
        at = pl.ds(32 * h, 32)
        best = [None] * TILES
        for j in range(NBOX):
            up = jnp.broadcast_to(roots[0, j][None], (4, 8, 128)).reshape(32, 128)
            bias = up * off[32 * h : 32 * h + 32]
            for k in range(TILES):
                score = bc[k, j, at] + bias
                best[k] = score if j == 0 else jnp.maximum(best[k], score)
        for k in range(TILES):
            t2[k, at] = best[k] * row_scale[32 * h : 32 * h + 32]
    unmix(t2, 0, snr_ref)
    for i in range(1, NT):
        stat_copy(i).wait_send()


def store(a, b, a_hbm, b_hbm, sem):
    copies = []
    for i, (source, target) in enumerate(((a, a_hbm), (b, b_hbm))):
        for j in range(4):
            at = pl.ds(32 * j, 32)
            copies.append(pltpu.make_async_copy(source.at[at], target.at[at], sem.at[i, j]))
    for copy in copies:
        copy.start()
    for copy in copies:
        copy.wait()


def body(intensity, shifts, boxcar_widths):
    dma = pltpu.SemaphoreType.DMA
    vmem, whole = pltpu.VMEM, pl.BlockSpec(memory_space=pl.ANY)
    in_vmem = pl.BlockSpec(memory_space=pltpu.VMEM)
    out = jax.ShapeDtypeStruct((128, 1024), F32)
    params = jnp.pad(shifts, ((0, 4), (0, 0)))
    params = lax.dynamic_update_slice(params, boxcar_widths[None], (12, 0))
    ded, snr = pl.pallas_call(
        kernel,
        out_shape=(out, out),
        in_specs=[whole, in_vmem],
        out_specs=[in_vmem] * 2,
        scratch_shapes=[
            vmem((512, 1024), BF16),
            vmem((4, 1, 128), I32),
            vmem((NB, 4, 1, 128), I32),
            vmem((LOCAL, 32, 8, 128), I32),
            vmem((CROSS, 32, 8, 128), I32),
            vmem((32, 6, 8, 128), F32),
            vmem((32, 3, 8, 128), F32),
            vmem((16, 2, 8, 128), F32),
            vmem((16, 2, 8, 128), F32),
            vmem((2, 16, 8, 128), F32),
            vmem((32, 8, 128), F32),
            vmem((16, 2, 8, 128), F32),
            vmem((16, 2, 3, 8, 128), F32),
            vmem((32, 3, 8, 128), F32),
            vmem((5, 256, 128), F32),
            vmem((256, 640), BF16),
            vmem((256, 640), BF16),
            vmem((TILES, NBOX, 256, 128), F32),
            vmem((256, 1024), BF16),
            vmem((2, NBOX, 8, 128), F32),
            vmem((2, 256), F32),
            vmem((NT, 2, 256), F32),
            dma((4,)),
            dma((NB // 2,)),
            dma((NB // 2,)),
            dma((6,)),
            dma((2, NB - 1)),
            dma((2, NB - 1)),
            dma((NB - 1,)),
            dma((NB - 1,)),
            dma((NT,)),
            dma((NT,)),
        ],
        compiler_params=pltpu.CompilerParams(
            collective_id=0, has_side_effects=True, vmem_limit_bytes=52 * 2**20
        ),
    )(intensity, params)
    return pl.pallas_call(
        store,
        out_shape=(out, out),
        in_specs=[in_vmem] * 2,
        out_specs=[whole] * 2,
        scratch_shapes=[dma((2, 4))],
        compiler_params=pltpu.CompilerParams(vmem_limit_bytes=52 * 2**20),
    )(ded, snr)


def solution(mesh):
    assert mesh.shape["band"] == NB and mesh.shape["tm"] == NT
    in_specs = (P("band", "tm"), P(None, "band"), P())
    out_specs = (P("band", "tm"), P("band", "tm"))
    return jax.shard_map(body, mesh=mesh, in_specs=in_specs, out_specs=out_specs, check_vma=False)
```

```python
import jax
import jax.numpy as jnp
from jax import lax
from jax.experimental import pallas as pl
from jax.experimental.pallas import tpu as pltpu
from jax.sharding import PartitionSpec as P

MESH = pl.DeviceIdType.MESH
F32, BF16, I32 = jnp.float32, jnp.bfloat16, jnp.int32
NB, NT = 32, 8
NBOX = 8
NCOL = 16
LOCAL, CROSS = 7, 5
TILES = 4
SAMPLES = 8192

_ROWS = lax.GatherDimensionNumbers(
    offset_dims=(),
    collapsed_slice_dims=(1,),
    start_index_map=(1,),
    operand_batching_dims=(0,),
    start_indices_batching_dims=(0,),
)


def iota(shape, dim):
    return lax.broadcasted_iota(I32, shape, dim)


def take_lanes(x, index):
    return lax.gather(
        x, index[..., None], _ROWS, (1, 1), mode=lax.GatherScatterMode.PROMISE_IN_BOUNDS
    )


def rev5(v):
    out = 0
    for k in range(5):
        out = out + (v // 2**k) % 2 * 2 ** (4 - k)
    return out


OFFSETS = sorted(
    [(dx, dz, dc) for dx in range(2) for dz in range(8) for dc in range(2)][1:],
    key=lambda o: (o[0], -min(o[1], 8 - o[1])),
)


def delay_add(firsts, seconds, index, keep):
    rows, tiles = firsts.shape[:2]
    shape = (rows, keep, 8, 128)
    before = seconds[:, tiles - keep - 1 : tiles - 1] if keep < tiles else seconds
    if keep == tiles > 1:
        before = jnp.concatenate([seconds[:, :1], seconds[:, :-1]], axis=1)
    lane = iota(index.shape, 2)
    wraps = jnp.broadcast_to((((lane + lane - index) & 127) < lane)[:, None], shape)
    merged = jnp.where(wraps, before, seconds[:, tiles - keep :])
    spread = jnp.broadcast_to(index[:, None], shape).reshape(-1, 128)
    return firsts[:, tiles - keep :] + take_lanes(merged.reshape(-1, 128), spread).reshape(shape)


def major_section(x, index, apart, keep):
    rows, tiles = x.shape[:2]
    shape = (rows // (2 * apart), 2, apart, tiles, 8, 128)
    pairs = x.reshape(shape)
    both = [jnp.broadcast_to(pairs[:, e : e + 1], shape).reshape(x.shape) for e in (0, 1)]
    return delay_add(*both, index, keep)


def folded_section(x, index, apart, grow):
    rows, tiles = x.shape[:2]
    shape = (rows // (2 * apart), 2, apart, tiles, 8, 128)
    pairs = x.reshape(shape)
    firsts, seconds = (jnp.broadcast_to(pairs[:, e : e + 1], shape).reshape(x.shape) for e in (0, 1))
    spread = jnp.broadcast_to(index[:, None], x.shape).reshape(-1, 128)
    turned = take_lanes(seconds.reshape(-1, 128), spread).reshape(x.shape)
    swapped = swap_halves(turned)
    is_low, wraps = iota(index.shape, 1) < 4, index > iota(index.shape, 2)
    empty, outs = jnp.zeros(index.shape, F32), []
    for v in range(tiles + grow):
        before = jnp.where(is_low, swapped[:, v - 1] if v else empty, swapped[:, v] if v < tiles else empty)
        if v < tiles:
            outs.append(firsts[:, v] + jnp.where(wraps, before, turned[:, v]))
        else:
            outs.append(jnp.where(wraps, before, 0.0))
    return jnp.stack(outs, axis=1)


def minor_section(x, index, apart, keep):
    flat = x.reshape(-1, 8, 128)
    is_set = iota(flat.shape, 1) // apart % 2 == 1
    firsts = jnp.where(is_set, pltpu.roll(flat, apart, 1), flat)
    seconds = jnp.where(is_set, flat, pltpu.roll(flat, 8 - apart, 1))
    return delay_add(firsts.reshape(x.shape), seconds.reshape(x.shape), index, keep)


def swap_halves(x):
    return pltpu.roll(x.reshape(-1, 8, 128), 4, 1).reshape(x.shape)


def kernel(
    x_hbm, par, ded_ref, snr_ref,
    xc, shsend, shbuf, idx1, idx2, l0, s7, hsend, hrecv, grecv, fsend, frecv,
    recv, t2, hi, lo, bc, band, roots, stsend, stbuf,
    local_sem, shs_sem, shr_sem, halo_sem, main_send, main_recv, front_send, front_recv, st_send, st_recv,
):
    me, t = lax.axis_index("band"), lax.axis_index("tm")
    copies_x = [
        pltpu.make_async_copy(x_hbm.at[pl.ds(128 * i, 128)], xc.at[pl.ds(128 * i, 128)], local_sem.at[i])
        for i in range(4)
    ]
    for copy in copies_x:
        copy.start()

    barrier = pltpu.get_barrier_semaphore()
    column, place = me // NCOL, me % NCOL
    z, core = place // 2, place % 2

    def dest_of(k):
        dx, dz, dc = OFFSETS[k]
        return (column + dx) % 2 * NCOL + (z + dz) % 8 * 2 + (core + dc) % 2

    own, other = range(NCOL - 1), range(NCOL - 1, NB - 1)
    for k in other:
        pl.semaphore_signal(barrier, inc=1, device_id={"band": dest_of(k)}, device_id_type=MESH)
    for i in range(1, NT):
        pl.semaphore_signal(barrier, inc=1, device_id={"tm": lax.rem(t + i, NT)}, device_id_type=MESH)
    for k in own:
        pl.semaphore_signal(barrier, inc=1, device_id={"band": dest_of(k)}, device_id_type=MESH)
    later = lax.rem(t + 1, NT)
    slot = rev5(me)
    sub8, lane8 = iota((8, 128), 0), iota((8, 128), 1)

    ones = jnp.ones((128, 128), BF16)
    for s in range(1, LOCAL + 1):
        row = jnp.broadcast_to(par[s - 1 : s, :].astype(F32), (8, 128))
        if s <= 5:
            base = sub8 // 2 % 2 * 32 + sub8 % 2 * 64
        else:
            base = sub8 // 2 % 2 * (1, 2)[s - 6] + sub8 % 2 * (64, 1)[s - 6]
        picks = []
        for m in range(32):
            turned = int(f"{m:05b}"[::-1], 2)
            if s <= 5:
                turned = (turned >> (5 - s)) + (m >> s << s)
            else:
                turned = turned << (s - 5)
            picks.append(jnp.where(lane8 - base == turned, row, 0.0))
        picks = jnp.stack(picks).reshape(256, 128).astype(BF16)
        delay = jnp.dot(picks, ones, preferred_element_type=F32).astype(I32)
        idx1[s - 1] = ((iota((256, 128), 1) - delay) & 127).reshape(32, 8, 128)
    for j in range(CROSS - 1):
        shsend[j] = par[LOCAL + j : LOCAL + j + 1, :]
        shbuf[me, j] = par[LOCAL + j : LOCAL + j + 1, :]

    is_low = iota((32, 8, 128), 1) < 4
    i = iota((128, 512), 0)
    group = i // 4 + 32 * (i // 2 % 2) + 64 * (i % 2)
    presum = jnp.where(iota((128, 512), 1) // 4 == group, 1.0, 0.0).astype(BF16)
    level = 0.0
    for i in range(2):
        copies_x[2 * i].wait()
        copies_x[2 * i + 1].wait()
        at = pl.ds(256 * i, 256)
        level = level + jnp.dot(presum[:, 256 * i : 256 * i + 256], xc[at], preferred_element_type=F32)
    for k in range(TILES):
        low, high = (level[:, c * 128 : c * 128 + 128].reshape(16, 8, 128) for c in (k, k + 4))
        if k >= 2:
            hsend[:, k - 2] = high
        low, high = (jnp.stack([p, swap_halves(p)], axis=1).reshape(32, 8, 128) for p in (low, swap_halves(high)))
        l0[:, 2 + k] = jnp.where(is_low, low, high)
        if k >= 2:
            l0[:, k - 2] = jnp.where(is_low, 0.0, swap_halves(low))

    def pack(two_tiles, half):
        first, second = two_tiles
        return jnp.where(is_low, *((swap_halves(first), second) if half else (first, swap_halves(second))))

    def main_copy(part, k):
        dest, which = dest_of(k), (pl.ds(0, 1), pl.ds(1, 2))[part]
        return pltpu.make_async_remote_copy(
            src_ref=s7.at[dest, which], dst_ref=recv.at[slot // 2, slot % 2, which],
            send_sem=main_send.at[part, k], recv_sem=main_recv.at[part, k],
            device_id={"band": dest}, device_id_type=MESH,
        )

    def front_copy(k):
        dest = dest_of(k)
        return pltpu.make_async_remote_copy(
            src_ref=fsend.at[dest], dst_ref=frecv.at[slot // 2, slot % 2],
            send_sem=front_send.at[k], recv_sem=front_recv.at[k],
            device_id={"band": dest}, device_id_type=MESH,
        )

    edges_first = t % 4 == 3

    def start_all(copies):
        for copy in copies:
            copy.start()

    def shift_copy(i):
        needed = pl.ds(0, (i & -i).bit_length())
        return pltpu.make_async_remote_copy(
            src_ref=shsend.at[needed], dst_ref=shbuf.at[me, needed], send_sem=shs_sem.at[i], recv_sem=shr_sem.at[i],
            device_id={"band": lax.rem(me + 2 * i, NB)}, device_id_type=MESH,
        )

    halo_copy = pltpu.make_async_remote_copy(
        src_ref=hsend, dst_ref=hrecv, send_sem=halo_sem.at[0], recv_sem=halo_sem.at[1],
        device_id={"tm": later}, device_id_type=MESH,
    )
    edge_copies = [
        pltpu.make_async_remote_copy(
            src_ref=recv.at[:, column if e == 0 else 1 - column, 0], dst_ref=grecv.at[e],
            send_sem=halo_sem.at[2 + 2 * e], recv_sem=halo_sem.at[3 + 2 * e],
            device_id={"tm": later}, device_id_type=MESH,
        )
        for e in range(2)
    ]
    has_next, has_last = t < NT - 1, t > 0

    def local_sections(first):
        x = l0[:, first : first + 4]
        for s in range(1, LOCAL + 1):
            keep = x.shape[1] - (s in (3, 7))
            if s <= 5:
                x = major_section(x, idx1[s - 1], 2 ** (s - 1), keep)
            else:
                x = minor_section(x, idx1[s - 1], 2 ** (7 - s), keep)
        return x[:, 0], x[:, 1]

    tiles = local_sections(2)
    s7[:, 0] = pack(tiles, 1)
    s7[:, 1] = pack(tiles, 0)
    pl.semaphore_wait(barrier, NB + NT - 2)
    pl.when(has_next)(halo_copy.start)
    for i in range(1, NB // 2):
        shift_copy(i).start()
    start_all(main_copy(0, k) for k in [*own, *other])
    tiles = local_sections(0)
    s7[:, 2] = pack(tiles, 1)
    fsend[...] = pack(tiles, 0)
    pl.when(jnp.logical_not(edges_first))(lambda: start_all(main_copy(1, k) for k in other))
    start_all(main_copy(1, k) for k in own)
    pl.when(edges_first)(lambda: start_all(main_copy(1, k) for k in other))
    recv[slot // 2, slot % 2] = s7[me]

    offset, sample = iota((256, 128), 0) - 128, iota((256, 128), 1)
    row = jnp.broadcast_to(par[12:13, :], (8, 128))
    for j in range(NBOX):
        width = take_lanes(row, jnp.full((8, 128), j, I32))
        root = jnp.sqrt(width.astype(F32))
        roots[0, j] = root
        roots[1, j] = 1.0 / root
        width = jnp.broadcast_to(width[None], (32, 8, 128)).reshape(256, 128)
        inside = (offset <= sample) & (offset > sample - width)
        band[:, j * 128 : (j + 1) * 128] = jnp.where(inside, 1.0, 0.0).astype(BF16)

    @pl.when(t == 0)
    def _():
        hrecv[...] = jnp.zeros(hrecv.shape, F32)
        grecv[...] = jnp.zeros(grecv.shape, F32)

    pl.when(has_last)(halo_copy.wait_recv)
    def spread_edge(packed):
        return jnp.stack([packed, swap_halves(packed)], axis=1).reshape(-1, 8, 128)

    x = hrecv[...]
    empty = jnp.zeros((16, 1, 8, 128), F32)
    for s in range(1, LOCAL + 1):
        pairs = idx1[s - 1].reshape(16, 2, 8, 128)
        index = jnp.where(iota((16, 8, 128), 1) < 4, pairs[:, 0], pairs[:, 1])
        if s in (1, 5):
            x = jnp.concatenate([x, empty], axis=1)
        keep = x.shape[1] - (s in (3, 7))
        if 2 <= s <= 5:
            x = major_section(x, index, 2 ** (s - 2), keep)
        else:
            x = minor_section(x, index, 4 if s == 1 else 2 ** (7 - s), keep)
    fsend[...] = fsend[...] + pack((spread_edge(x[:, 0]), spread_edge(x[:, 1])), 0)
    start_all(front_copy(k) for k in [*other, *own])
    frecv[slot // 2, slot % 2] = fsend[me]

    for e in range(2):
        for k in other if e else own:
            main_copy(0, k).wait_recv()
        pl.when(has_next)(edge_copies[e].start)

    for i in range(1, NB // 2):
        shift_copy(i).wait_recv()
    quarter = sub8 % 4
    for j in range(1, CROSS + 1):
        base = 0
        for bit in range(j, CROSS):
            base = base + me // 2**bit % 2 * 2 ** (6 - bit + j)
        for low in range(2 ** (CROSS - j)):
            if j < CROSS:
                source = me % 2**j
                for bit in range(j, CROSS):
                    source = source + 2**bit * ((low >> (4 - bit)) & 1)
                row = shbuf[source, j - 1]
            else:
                row = par[LOCAL + j - 1 : LOCAL + j, :]
            row = jnp.broadcast_to(row, (8, 128))
            for high in range(2**j):
                delay = take_lanes(row, base + 2**j * quarter + high)
                idx2[j - 1, low + 2 ** (CROSS - j) * high] = (lane8 - delay) & 127

    for k in [*other, *own]:
        main_copy(1, k).wait_recv()

    def unpack(low, high):
        return jnp.where(is_low, low, swap_halves(high)), jnp.where(is_low, swap_halves(low), high)

    back = unpack(recv[:, :, 1].reshape(32, 8, 128), recv[:, :, 0].reshape(32, 8, 128))
    x = swap_halves(jnp.stack(back, axis=1))
    x = jnp.where(jnp.broadcast_to(is_low[:, None], x.shape), 0.0, x)
    aheads = []
    for j in range(1, CROSS + 1):
        aheads.append(x[:, -1:])
        x = major_section(x, idx2[j - 1], 2 ** (CROSS - j), x.shape[1] - (j == 3))
    front = x

    high = recv[:, :, 2].reshape(32, 8, 128)
    x = jnp.stack([jnp.where(is_low, 0.0, swap_halves(high)), jnp.where(is_low, 0.0, high), *back], axis=1)
    for j in range(1, CROSS + 1):
        x = major_section(jnp.concatenate([aheads[j - 1], x], axis=1), idx2[j - 1], 2 ** (CROSS - j), TILES)
    norm = 16384.0 ** (-0.5)
    x = jnp.concatenate([front, x], axis=1) * norm
    for k in range(5):
        t2[k] = x[:, k].reshape(256, 128)

    def output_rows(k, half):
        return jnp.concatenate([t2[k, pl.ds(b * 64 + half * 4 + q, 8, stride=8), :] for q in range(4) for b in range(4)])

    second = [output_rows(1 + k, 1) for k in range(TILES)]
    pivot = jnp.sum(second[0] + second[1] + second[2] + second[3], axis=1, keepdims=True) * (1.0 / 512)
    pivot = jnp.broadcast_to(pivot, (128, 128))
    sums, squares = jnp.zeros((128, 128), F32), jnp.zeros((128, 128), F32)

    def split(c, centred):
        high = centred.astype(BF16)
        low = (centred - high.astype(F32)).astype(BF16)
        for part, value in ((hi, high), (lo, low)):
            if c >= 0:
                part[128 * c : 128 * c + 128, 128:256] = value
            if c < 2 * TILES - 1:
                part[128 * c + 128 : 128 * c + 256, 0:128] = value

    for k in range(TILES):
        ded_ref[:, 512 + 128 * k : 640 + 128 * k] = second[k]
        centred = second[k] - pivot
        sums, squares = sums + centred, squares + centred * centred
        split(TILES + k, centred)

    def boxcars(first, tiles):
        at = pl.ds(128 * first, 128 * tiles)
        both = jnp.dot(hi[at], band[...], preferred_element_type=F32)
        both = both + jnp.dot(lo[at], band[...], preferred_element_type=F32)
        for j in range(NBOX):
            part = both[:, j * 128 : (j + 1) * 128].reshape(-1, 8, 128)
            part = (part * jnp.broadcast_to(roots[1, j][None], part.shape)).reshape(tiles, 128, 128)
            for c in range(tiles):
                bc[first + c, j] = part[c]

    for k in range(NB - 1):
        front_copy(k).wait_recv()
    for copy in edge_copies:
        pl.when(has_last)(copy.wait_recv)
    y = jnp.stack([grecv[column if f == 0 else 1 - column] for f in range(2)], axis=1).reshape(32, 8, 128)
    y = jnp.stack([y, frecv[...].reshape(32, 8, 128)], axis=1)
    for j in range(1, CROSS + 1):
        y = folded_section(y, idx2[j - 1], 2 ** (CROSS - j), j == 1)
    added = [swap_halves(y[:, 0]), y[:, 1], swap_halves(y[:, 1]), y[:, 2], swap_halves(y[:, 2])]
    for k in range(5):
        t2[k] = (x[:, k] + jnp.where(is_low, added[k], 0.0) * norm).reshape(256, 128)
    first = [output_rows(k, 0) for k in range(5)]
    for k in range(1, 5):
        centred = first[k] - pivot
        sums, squares = sums + centred, squares + centred * centred
    sums = jnp.broadcast_to(jnp.sum(sums, axis=1, keepdims=True), (128, 128))
    squares = jnp.broadcast_to(jnp.sum(squares, axis=1, keepdims=True), (128, 128))
    squares = squares - sums * sums * (1.0 / 1024)
    sums = pivot + sums * (1.0 / 1024)
    mine = jnp.transpose(jnp.where(iota((128, 128), 1) == 0, sums, squares))[0:2]
    stsend[...] = mine
    stbuf[t] = mine

    def stat_copy(i):
        return pltpu.make_async_remote_copy(
            src_ref=stsend, dst_ref=stbuf.at[t], send_sem=st_send.at[i], recv_sem=st_recv.at[i],
            device_id={"tm": lax.rem(t + i, NT)}, device_id_type=MESH,
        )

    for i in range(1, NT):
        stat_copy(i).start()

    for k in range(5):
        split(k - 1, first[k] - pivot)
        if k:
            ded_ref[:, 128 * k - 128 : 128 * k] = first[k]
    boxcars(0, 2 * TILES)
    for k in range(NB - 1):
        main_copy(0, k).wait_send()
        main_copy(1, k).wait_send()
        front_copy(k).wait_send()
    for i in range(1, NB // 2):
        shift_copy(i).wait_send()
    pl.when(has_next)(halo_copy.wait_send)
    for e in range(2):
        pl.when(has_next)(edge_copies[e].wait_send)
    for i in range(1, NT):
        stat_copy(i).wait_recv()
    means = [stbuf[i][0:1] for i in range(NT)]
    mean = sum(means) * (1.0 / NT)
    centred = [stbuf[i][1:2] + 1024.0 * ((m - mean) * (m - mean)) for i, m in enumerate(means)]
    scale = 1.0 / jnp.sqrt(sum(centred) * (1.0 / SAMPLES) + 1e-6)
    row_mean = jnp.transpose(jnp.broadcast_to(mean, (128, 128)))
    row_scale = jnp.transpose(jnp.broadcast_to(scale, (128, 128)))
    off = pivot - row_mean
    for h in range(8):
        at = pl.ds(16 * h, 16)
        best = [None] * (2 * TILES)
        for j in range(NBOX):
            up = jnp.broadcast_to(roots[0, j][None], (2, 8, 128)).reshape(16, 128)
            bias = up * off[16 * h : 16 * h + 16]
            for c in range(2 * TILES):
                score = bc[c, j, at] + bias
                best[c] = score if j == 0 else jnp.maximum(best[c], score)
        for c in range(2 * TILES):
            snr_ref[at, 128 * c : 128 * c + 128] = best[c] * row_scale[16 * h : 16 * h + 16]
    for i in range(1, NT):
        stat_copy(i).wait_send()


def store(a, b, a_hbm, b_hbm, sem):
    copies = [pltpu.make_async_copy(a, a_hbm, sem.at[0]), pltpu.make_async_copy(b, b_hbm, sem.at[1])]
    for copy in copies:
        copy.start()
    for copy in copies:
        copy.wait()


def body(intensity, shifts, boxcar_widths):
    dma = pltpu.SemaphoreType.DMA
    vmem, whole = pltpu.VMEM, pl.BlockSpec(memory_space=pl.ANY)
    in_vmem = pl.BlockSpec(memory_space=pltpu.VMEM)
    out = jax.ShapeDtypeStruct((128, 1024), F32)
    params = jnp.pad(shifts, ((0, 4), (0, 0)))
    params = lax.dynamic_update_slice(params, boxcar_widths[None], (12, 0))
    ded, snr = pl.pallas_call(
        kernel,
        out_shape=(out, out),
        in_specs=[whole, in_vmem],
        out_specs=[in_vmem] * 2,
        scratch_shapes=[
            vmem((512, 1024), BF16),
            vmem((4, 1, 128), I32),
            vmem((NB, 4, 1, 128), I32),
            vmem((LOCAL, 32, 8, 128), I32),
            vmem((CROSS, 32, 8, 128), I32),
            vmem((32, 6, 8, 128), F32),
            vmem((32, 3, 8, 128), F32),
            vmem((16, 2, 8, 128), F32),
            vmem((16, 2, 8, 128), F32),
            vmem((2, 16, 8, 128), F32),
            vmem((32, 8, 128), F32),
            vmem((16, 2, 8, 128), F32),
            vmem((16, 2, 3, 8, 128), F32),
            vmem((5, 256, 128), F32),
            vmem((1024, 256), BF16),
            vmem((1024, 256), BF16),
            vmem((2 * TILES, NBOX, 128, 128), F32),
            vmem((256, 1024), BF16),
            vmem((2, NBOX, 8, 128), F32),
            vmem((2, 128), F32),
            vmem((NT, 2, 128), F32),
            dma((4,)),
            dma((NB // 2,)),
            dma((NB // 2,)),
            dma((6,)),
            dma((2, NB - 1)),
            dma((2, NB - 1)),
            dma((NB - 1,)),
            dma((NB - 1,)),
            dma((NT,)),
            dma((NT,)),
        ],
        compiler_params=pltpu.CompilerParams(
            collective_id=0, has_side_effects=True, vmem_limit_bytes=52 * 2**20
        ),
    )(intensity, params)
    return pl.pallas_call(
        store,
        out_shape=(out, out),
        in_specs=[in_vmem] * 2,
        out_specs=[whole] * 2,
        scratch_shapes=[dma((2,))],
        compiler_params=pltpu.CompilerParams(vmem_limit_bytes=52 * 2**20),
    )(ded, snr)


def solution(mesh):
    assert mesh.shape["band"] == NB and mesh.shape["tm"] == NT
    in_specs = (P("band", "tm"), P(None, "band"), P())
    out_specs = (P("band", "tm"), P("band", "tm"))
    return jax.shard_map(body, mesh=mesh, in_specs=in_specs, out_specs=out_specs, check_vma=False)
```

```python
import jax
import jax.numpy as jnp
from jax import lax
from jax.experimental import pallas as pl
from jax.experimental.pallas import tpu as pltpu
from jax.sharding import PartitionSpec as P

MESH = pl.DeviceIdType.MESH
F32, BF16, I32 = jnp.float32, jnp.bfloat16, jnp.int32
NB, NT = 32, 8
NBOX = 8
NCOL = 16
LOCAL, CROSS = 7, 5
TILES = 4
SAMPLES = 8192

_ROWS = lax.GatherDimensionNumbers(
    offset_dims=(),
    collapsed_slice_dims=(1,),
    start_index_map=(1,),
    operand_batching_dims=(0,),
    start_indices_batching_dims=(0,),
)


def iota(shape, dim):
    return lax.broadcasted_iota(I32, shape, dim)


def take_lanes(x, index):
    return lax.gather(
        x, index[..., None], _ROWS, (1, 1), mode=lax.GatherScatterMode.PROMISE_IN_BOUNDS
    )


def rev5(v):
    out = 0
    for k in range(5):
        out = out + (v // 2**k) % 2 * 2 ** (4 - k)
    return out


OFFSETS = sorted(
    [(dx, dz, dc) for dx in range(2) for dz in range(8) for dc in range(2)][1:],
    key=lambda o: (o[0], -min(o[1], 8 - o[1])),
)


def delay_add(firsts, seconds, index, keep):
    rows, tiles = firsts.shape[:2]
    shape = (rows, keep, 8, 128)
    before = seconds[:, tiles - keep - 1 : tiles - 1] if keep < tiles else seconds
    if keep == tiles > 1:
        before = jnp.concatenate([seconds[:, :1], seconds[:, :-1]], axis=1)
    lane = iota(index.shape, 2)
    wraps = jnp.broadcast_to((((lane + lane - index) & 127) < lane)[:, None], shape)
    merged = jnp.where(wraps, before, seconds[:, tiles - keep :])
    spread = jnp.broadcast_to(index[:, None], shape).reshape(-1, 128)
    return firsts[:, tiles - keep :] + take_lanes(merged.reshape(-1, 128), spread).reshape(shape)


def major_section(x, index, apart, keep):
    rows, tiles = x.shape[:2]
    shape = (rows // (2 * apart), 2, apart, tiles, 8, 128)
    pairs = x.reshape(shape)
    both = [jnp.broadcast_to(pairs[:, e : e + 1], shape).reshape(x.shape) for e in (0, 1)]
    return delay_add(*both, index, keep)


def folded_section(x, index, apart, grow):
    rows, tiles = x.shape[:2]
    shape = (rows // (2 * apart), 2, apart, tiles, 8, 128)
    pairs = x.reshape(shape)
    firsts, seconds = (jnp.broadcast_to(pairs[:, e : e + 1], shape).reshape(x.shape) for e in (0, 1))
    spread = jnp.broadcast_to(index[:, None], x.shape).reshape(-1, 128)
    turned = take_lanes(seconds.reshape(-1, 128), spread).reshape(x.shape)
    swapped = swap_halves(turned)
    is_low, wraps = iota(index.shape, 1) < 4, index > iota(index.shape, 2)
    empty, outs = jnp.zeros(index.shape, F32), []
    for v in range(tiles + grow):
        before = jnp.where(is_low, swapped[:, v - 1] if v else empty, swapped[:, v] if v < tiles else empty)
        if v < tiles:
            outs.append(firsts[:, v] + jnp.where(wraps, before, turned[:, v]))
        else:
            outs.append(jnp.where(wraps, before, 0.0))
    return jnp.stack(outs, axis=1)


def minor_section(x, index, apart, keep):
    flat = x.reshape(-1, 8, 128)
    is_set = iota(flat.shape, 1) // apart % 2 == 1
    firsts = jnp.where(is_set, pltpu.roll(flat, apart, 1), flat)
    seconds = jnp.where(is_set, flat, pltpu.roll(flat, 8 - apart, 1))
    return delay_add(firsts.reshape(x.shape), seconds.reshape(x.shape), index, keep)


def swap_halves(x):
    return pltpu.roll(x.reshape(-1, 8, 128), 4, 1).reshape(x.shape)


def kernel(
    x_hbm, par, ded_ref, snr_ref,
    xc, shsend, shbuf, idx1, idx2, l0, s7, hsend, hrecv, grecv, fsend, frecv,
    recv, t2, hi, lo, bc, band, roots, stsend, stbuf,
    local_sem, shs_sem, shr_sem, halo_sem, main_send, main_recv, front_send, front_recv, st_send, st_recv,
):
    me, t = lax.axis_index("band"), lax.axis_index("tm")
    copies_x = [
        pltpu.make_async_copy(x_hbm.at[pl.ds(128 * i, 128)], xc.at[pl.ds(128 * i, 128)], local_sem.at[i])
        for i in range(4)
    ]
    for copy in copies_x:
        copy.start()

    barrier = pltpu.get_barrier_semaphore()
    column, place = me // NCOL, me % NCOL
    z, core = place // 2, place % 2

    def dest_of(k):
        dx, dz, dc = OFFSETS[k]
        return (column + dx) % 2 * NCOL + (z + dz) % 8 * 2 + (core + dc) % 2

    own, other = range(NCOL - 1), range(NCOL - 1, NB - 1)
    for k in other:
        pl.semaphore_signal(barrier, inc=1, device_id={"band": dest_of(k)}, device_id_type=MESH)
    for i in range(1, NT):
        pl.semaphore_signal(barrier, inc=1, device_id={"tm": lax.rem(t + i, NT)}, device_id_type=MESH)
    for k in own:
        pl.semaphore_signal(barrier, inc=1, device_id={"band": dest_of(k)}, device_id_type=MESH)
    later = lax.rem(t + 1, NT)
    slot = rev5(me)
    sub8, lane8 = iota((8, 128), 0), iota((8, 128), 1)

    ones = jnp.ones((128, 128), BF16)
    for s in range(1, LOCAL + 1):
        row = jnp.broadcast_to(par[s - 1 : s, :].astype(F32), (8, 128))
        if s <= 5:
            base = sub8 // 2 % 2 * 32 + sub8 % 2 * 64
        else:
            base = sub8 // 2 % 2 * (1, 2)[s - 6] + sub8 % 2 * (64, 1)[s - 6]
        picks = []
        for m in range(32):
            turned = int(f"{m:05b}"[::-1], 2)
            if s <= 5:
                turned = (turned >> (5 - s)) + (m >> s << s)
            else:
                turned = turned << (s - 5)
            picks.append(jnp.where(lane8 - base == turned, row, 0.0))
        picks = jnp.stack(picks).reshape(256, 128).astype(BF16)
        delay = jnp.dot(picks, ones, preferred_element_type=F32).astype(I32)
        idx1[s - 1] = ((iota((256, 128), 1) - delay) & 127).reshape(32, 8, 128)
    for j in range(CROSS - 1):
        shsend[j] = par[LOCAL + j : LOCAL + j + 1, :]
        shbuf[me, j] = par[LOCAL + j : LOCAL + j + 1, :]

    is_low = iota((32, 8, 128), 1) < 4
    i = iota((128, 512), 0)
    group = i // 4 + 32 * (i // 2 % 2) + 64 * (i % 2)
    presum = jnp.where(iota((128, 512), 1) // 4 == group, 1.0, 0.0).astype(BF16)
    level = 0.0
    for i in range(2):
        copies_x[2 * i].wait()
        copies_x[2 * i + 1].wait()
        at = pl.ds(256 * i, 256)
        level = level + jnp.dot(presum[:, 256 * i : 256 * i + 256], xc[at], preferred_element_type=F32)
    for k in range(TILES):
        low, high = (level[:, c * 128 : c * 128 + 128].reshape(16, 8, 128) for c in (k, k + 4))
        if k >= 2:
            hsend[:, k - 2] = high
        low, high = (jnp.stack([p, swap_halves(p)], axis=1).reshape(32, 8, 128) for p in (low, swap_halves(high)))
        l0[:, 2 + k] = jnp.where(is_low, low, high)
        if k >= 2:
            l0[:, k - 2] = jnp.where(is_low, 0.0, swap_halves(low))

    def pack(two_tiles, half):
        first, second = two_tiles
        return jnp.where(is_low, *((swap_halves(first), second) if half else (first, swap_halves(second))))

    def main_copy(part, k):
        dest, which = dest_of(k), (pl.ds(0, 1), pl.ds(1, 2))[part]
        return pltpu.make_async_remote_copy(
            src_ref=s7.at[dest, which], dst_ref=recv.at[slot // 2, slot % 2, which],
            send_sem=main_send.at[part, k], recv_sem=main_recv.at[part, k],
            device_id={"band": dest}, device_id_type=MESH,
        )

    def front_copy(k):
        dest = dest_of(k)
        return pltpu.make_async_remote_copy(
            src_ref=fsend.at[dest], dst_ref=frecv.at[slot // 2, slot % 2],
            send_sem=front_send.at[k], recv_sem=front_recv.at[k],
            device_id={"band": dest}, device_id_type=MESH,
        )

    edges_first = t == NT // 2 - 1

    def start_all(copies):
        for copy in copies:
            copy.start()

    def shift_copy(i):
        needed = pl.ds(0, (i & -i).bit_length())
        return pltpu.make_async_remote_copy(
            src_ref=shsend.at[needed], dst_ref=shbuf.at[me, needed], send_sem=shs_sem.at[i], recv_sem=shr_sem.at[i],
            device_id={"band": lax.rem(me + 2 * i, NB)}, device_id_type=MESH,
        )

    halo_copy = pltpu.make_async_remote_copy(
        src_ref=hsend, dst_ref=hrecv, send_sem=halo_sem.at[0], recv_sem=halo_sem.at[1],
        device_id={"tm": later}, device_id_type=MESH,
    )
    edge_copies = [
        pltpu.make_async_remote_copy(
            src_ref=recv.at[:, column if e == 0 else 1 - column, 0], dst_ref=grecv.at[e],
            send_sem=halo_sem.at[2 + 2 * e], recv_sem=halo_sem.at[3 + 2 * e],
            device_id={"tm": later}, device_id_type=MESH,
        )
        for e in range(2)
    ]
    has_next, has_last = t < NT - 1, t > 0

    def local_sections(first):
        x = l0[:, first : first + 4]
        for s in range(1, LOCAL + 1):
            keep = x.shape[1] - (s in (3, 7))
            if s <= 5:
                x = major_section(x, idx1[s - 1], 2 ** (s - 1), keep)
            else:
                x = minor_section(x, idx1[s - 1], 2 ** (7 - s), keep)
        return x[:, 0], x[:, 1]

    tiles = local_sections(2)
    s7[:, 0] = pack(tiles, 1)
    s7[:, 1] = pack(tiles, 0)
    pl.semaphore_wait(barrier, NB + NT - 2)
    pl.when(has_next)(halo_copy.start)
    for i in range(1, NB // 2):
        shift_copy(i).start()
    start_all(main_copy(0, k) for k in [*own, *other])
    tiles = local_sections(0)
    s7[:, 2] = pack(tiles, 1)
    fsend[...] = pack(tiles, 0)
    pl.when(jnp.logical_not(edges_first))(lambda: start_all(main_copy(1, k) for k in other))
    start_all(main_copy(1, k) for k in own)
    pl.when(edges_first)(lambda: start_all(main_copy(1, k) for k in other))
    recv[slot // 2, slot % 2] = s7[me]

    offset, sample = iota((256, 128), 0) - 128, iota((256, 128), 1)
    row = jnp.broadcast_to(par[12:13, :], (8, 128))
    for j in range(NBOX):
        width = take_lanes(row, jnp.full((8, 128), j, I32))
        root = jnp.sqrt(width.astype(F32))
        roots[0, j] = root
        roots[1, j] = 1.0 / root
        width = jnp.broadcast_to(width[None], (32, 8, 128)).reshape(256, 128)
        inside = (offset <= sample) & (offset > sample - width)
        band[:, j * 128 : (j + 1) * 128] = jnp.where(inside, 1.0, 0.0).astype(BF16)

    @pl.when(t == 0)
    def _():
        hrecv[...] = jnp.zeros(hrecv.shape, F32)
        grecv[...] = jnp.zeros(grecv.shape, F32)

    pl.when(has_last)(halo_copy.wait_recv)
    def spread_edge(packed):
        return jnp.stack([packed, swap_halves(packed)], axis=1).reshape(-1, 8, 128)

    x = hrecv[...]
    empty = jnp.zeros((16, 1, 8, 128), F32)
    for s in range(1, LOCAL + 1):
        pairs = idx1[s - 1].reshape(16, 2, 8, 128)
        index = jnp.where(iota((16, 8, 128), 1) < 4, pairs[:, 0], pairs[:, 1])
        if s in (1, 5):
            x = jnp.concatenate([x, empty], axis=1)
        keep = x.shape[1] - (s in (3, 7))
        if 2 <= s <= 5:
            x = major_section(x, index, 2 ** (s - 2), keep)
        else:
            x = minor_section(x, index, 4 if s == 1 else 2 ** (7 - s), keep)
    fsend[...] = fsend[...] + pack((spread_edge(x[:, 0]), spread_edge(x[:, 1])), 0)
    start_all(front_copy(k) for k in [*other, *own])
    frecv[slot // 2, slot % 2] = fsend[me]

    for e in range(2):
        for k in other if e else own:
            main_copy(0, k).wait_recv()
        pl.when(has_next)(edge_copies[e].start)

    for i in range(1, NB // 2):
        shift_copy(i).wait_recv()
    quarter = sub8 % 4
    for j in range(1, CROSS + 1):
        base = 0
        for bit in range(j, CROSS):
            base = base + me // 2**bit % 2 * 2 ** (6 - bit + j)
        for low in range(2 ** (CROSS - j)):
            if j < CROSS:
                source = me % 2**j
                for bit in range(j, CROSS):
                    source = source + 2**bit * ((low >> (4 - bit)) & 1)
                row = shbuf[source, j - 1]
            else:
                row = par[LOCAL + j - 1 : LOCAL + j, :]
            row = jnp.broadcast_to(row, (8, 128))
            for high in range(2**j):
                delay = take_lanes(row, base + 2**j * quarter + high)
                idx2[j - 1, low + 2 ** (CROSS - j) * high] = (lane8 - delay) & 127

    for k in [*other, *own]:
        main_copy(1, k).wait_recv()

    def unpack(low, high):
        return jnp.where(is_low, low, swap_halves(high)), jnp.where(is_low, swap_halves(low), high)

    back = unpack(recv[:, :, 1].reshape(32, 8, 128), recv[:, :, 0].reshape(32, 8, 128))
    x = swap_halves(jnp.stack(back, axis=1))
    x = jnp.where(jnp.broadcast_to(is_low[:, None], x.shape), 0.0, x)
    aheads = []
    for j in range(1, CROSS + 1):
        aheads.append(x[:, -1:])
        x = major_section(x, idx2[j - 1], 2 ** (CROSS - j), x.shape[1] - (j == 3))
    front = x

    high = recv[:, :, 2].reshape(32, 8, 128)
    x = jnp.stack([jnp.where(is_low, 0.0, swap_halves(high)), jnp.where(is_low, 0.0, high), *back], axis=1)
    for j in range(1, CROSS + 1):
        x = major_section(jnp.concatenate([aheads[j - 1], x], axis=1), idx2[j - 1], 2 ** (CROSS - j), TILES)
    norm = 16384.0 ** (-0.5)
    x = jnp.concatenate([front, x], axis=1) * norm
    for k in range(5):
        t2[k] = x[:, k].reshape(256, 128)

    def output_rows(k, half):
        return jnp.concatenate([t2[k, pl.ds(b * 64 + half * 4 + q, 8, stride=8), :] for q in range(4) for b in range(4)])

    second = [output_rows(1 + k, 1) for k in range(TILES)]
    pivot = jnp.sum(second[0] + second[1] + second[2] + second[3], axis=1, keepdims=True) * (1.0 / 512)
    pivot = jnp.broadcast_to(pivot, (128, 128))
    sums, squares = jnp.zeros((128, 128), F32), jnp.zeros((128, 128), F32)

    def split(c, centred):
        high = centred.astype(BF16)
        low = (centred - high.astype(F32)).astype(BF16)
        for part, value in ((hi, high), (lo, low)):
            if c >= 0:
                part[128 * c : 128 * c + 128, 128:256] = value
            if c < 2 * TILES - 1:
                part[128 * c + 128 : 128 * c + 256, 0:128] = value

    for k in range(TILES):
        ded_ref[:, 512 + 128 * k : 640 + 128 * k] = second[k]
        centred = second[k] - pivot
        sums, squares = sums + centred, squares + centred * centred
        split(TILES + k, centred)

    def boxcars(first, tiles):
        at = pl.ds(128 * first, 128 * tiles)
        both = jnp.dot(hi[at], band[...], preferred_element_type=F32)
        both = both + jnp.dot(lo[at], band[...], preferred_element_type=F32)
        for j in range(NBOX):
            part = both[:, j * 128 : (j + 1) * 128].reshape(-1, 8, 128)
            part = (part * jnp.broadcast_to(roots[1, j][None], part.shape)).reshape(tiles, 128, 128)
            for c in range(tiles):
                bc[first + c, j] = part[c]

    for k in range(NB - 1):
        front_copy(k).wait_recv()
    for copy in edge_copies:
        pl.when(has_last)(copy.wait_recv)
    y = jnp.stack([grecv[column if f == 0 else 1 - column] for f in range(2)], axis=1).reshape(32, 8, 128)
    y = jnp.stack([y, frecv[...].reshape(32, 8, 128)], axis=1)
    for j in range(1, CROSS + 1):
        y = folded_section(y, idx2[j - 1], 2 ** (CROSS - j), j == 1)
    added = [swap_halves(y[:, 0]), y[:, 1], swap_halves(y[:, 1]), y[:, 2], swap_halves(y[:, 2])]
    for k in range(5):
        t2[k] = (x[:, k] + jnp.where(is_low, added[k], 0.0) * norm).reshape(256, 128)
    first = [output_rows(k, 0) for k in range(5)]
    for k in range(1, 5):
        centred = first[k] - pivot
        sums, squares = sums + centred, squares + centred * centred
    sums = jnp.broadcast_to(jnp.sum(sums, axis=1, keepdims=True), (128, 128))
    squares = jnp.broadcast_to(jnp.sum(squares, axis=1, keepdims=True), (128, 128))
    squares = squares - sums * sums * (1.0 / 1024)
    sums = pivot + sums * (1.0 / 1024)
    mine = jnp.transpose(jnp.where(iota((128, 128), 1) == 0, sums, squares))[0:2]
    stsend[...] = mine
    stbuf[t] = mine

    def stat_copy(i):
        return pltpu.make_async_remote_copy(
            src_ref=stsend, dst_ref=stbuf.at[t], send_sem=st_send.at[i], recv_sem=st_recv.at[i],
            device_id={"tm": lax.rem(t + i, NT)}, device_id_type=MESH,
        )

    for i in range(1, NT):
        stat_copy(i).start()

    for k in range(5):
        split(k - 1, first[k] - pivot)
        if k:
            ded_ref[:, 128 * k - 128 : 128 * k] = first[k]
    boxcars(0, 2 * TILES)
    for k in range(NB - 1):
        main_copy(0, k).wait_send()
        main_copy(1, k).wait_send()
        front_copy(k).wait_send()
    for i in range(1, NB // 2):
        shift_copy(i).wait_send()
    pl.when(has_next)(halo_copy.wait_send)
    for e in range(2):
        pl.when(has_next)(edge_copies[e].wait_send)
    for i in range(1, NT):
        stat_copy(i).wait_recv()
    means = [stbuf[i][0:1] for i in range(NT)]
    mean = sum(means) * (1.0 / NT)
    centred = [stbuf[i][1:2] + 1024.0 * ((m - mean) * (m - mean)) for i, m in enumerate(means)]
    scale = 1.0 / jnp.sqrt(sum(centred) * (1.0 / SAMPLES) + 1e-6)
    row_mean = jnp.transpose(jnp.broadcast_to(mean, (128, 128)))
    row_scale = jnp.transpose(jnp.broadcast_to(scale, (128, 128)))
    off = pivot - row_mean
    for h in range(8):
        at = pl.ds(16 * h, 16)
        best = [None] * (2 * TILES)
        for j in range(NBOX):
            up = jnp.broadcast_to(roots[0, j][None], (2, 8, 128)).reshape(16, 128)
            bias = up * off[16 * h : 16 * h + 16]
            for c in range(2 * TILES):
                score = bc[c, j, at] + bias
                best[c] = score if j == 0 else jnp.maximum(best[c], score)
        for c in range(2 * TILES):
            snr_ref[at, 128 * c : 128 * c + 128] = best[c] * row_scale[16 * h : 16 * h + 16]
    for i in range(1, NT):
        stat_copy(i).wait_send()


def store(a, b, a_hbm, b_hbm, sem):
    copies = [pltpu.make_async_copy(a, a_hbm, sem.at[0]), pltpu.make_async_copy(b, b_hbm, sem.at[1])]
    for copy in copies:
        copy.start()
    for copy in copies:
        copy.wait()


def body(intensity, shifts, boxcar_widths):
    dma = pltpu.SemaphoreType.DMA
    vmem, whole = pltpu.VMEM, pl.BlockSpec(memory_space=pl.ANY)
    in_vmem = pl.BlockSpec(memory_space=pltpu.VMEM)
    out = jax.ShapeDtypeStruct((128, 1024), F32)
    params = jnp.pad(shifts, ((0, 4), (0, 0)))
    params = lax.dynamic_update_slice(params, boxcar_widths[None], (12, 0))
    ded, snr = pl.pallas_call(
        kernel,
        out_shape=(out, out),
        in_specs=[whole, in_vmem],
        out_specs=[in_vmem] * 2,
        scratch_shapes=[
            vmem((512, 1024), BF16),
            vmem((4, 1, 128), I32),
            vmem((NB, 4, 1, 128), I32),
            vmem((LOCAL, 32, 8, 128), I32),
            vmem((CROSS, 32, 8, 128), I32),
            vmem((32, 6, 8, 128), F32),
            vmem((32, 3, 8, 128), F32),
            vmem((16, 2, 8, 128), F32),
            vmem((16, 2, 8, 128), F32),
            vmem((2, 16, 8, 128), F32),
            vmem((32, 8, 128), F32),
            vmem((16, 2, 8, 128), F32),
            vmem((16, 2, 3, 8, 128), F32),
            vmem((5, 256, 128), F32),
            vmem((1024, 256), BF16),
            vmem((1024, 256), BF16),
            vmem((2 * TILES, NBOX, 128, 128), F32),
            vmem((256, 1024), BF16),
            vmem((2, NBOX, 8, 128), F32),
            vmem((2, 128), F32),
            vmem((NT, 2, 128), F32),
            dma((4,)),
            dma((NB // 2,)),
            dma((NB // 2,)),
            dma((6,)),
            dma((2, NB - 1)),
            dma((2, NB - 1)),
            dma((NB - 1,)),
            dma((NB - 1,)),
            dma((NT,)),
            dma((NT,)),
        ],
        compiler_params=pltpu.CompilerParams(
            collective_id=0, has_side_effects=True, vmem_limit_bytes=52 * 2**20
        ),
    )(intensity, params)
    return pl.pallas_call(
        store,
        out_shape=(out, out),
        in_specs=[in_vmem] * 2,
        out_specs=[whole] * 2,
        scratch_shapes=[dma((2,))],
        compiler_params=pltpu.CompilerParams(vmem_limit_bytes=52 * 2**20),
    )(ded, snr)


def solution(mesh):
    assert mesh.shape["band"] == NB and mesh.shape["tm"] == NT
    in_specs = (P("band", "tm"), P(None, "band"), P())
    out_specs = (P("band", "tm"), P("band", "tm"))
    return jax.shard_map(body, mesh=mesh, in_specs=in_specs, out_specs=out_specs, check_vma=False)
```

```python
import jax
import jax.numpy as jnp
from jax import lax
from jax.experimental import pallas as pl
from jax.experimental.pallas import tpu as pltpu
from jax.sharding import PartitionSpec as P

MESH = pl.DeviceIdType.MESH
F32, BF16, I32 = jnp.float32, jnp.bfloat16, jnp.int32
NB, NT = 32, 8
NBOX = 8
NCOL = 16
LOCAL, CROSS = 7, 5
TILES = 4
SAMPLES = 8192

_ROWS = lax.GatherDimensionNumbers(
    offset_dims=(),
    collapsed_slice_dims=(1,),
    start_index_map=(1,),
    operand_batching_dims=(0,),
    start_indices_batching_dims=(0,),
)


def iota(shape, dim):
    return lax.broadcasted_iota(I32, shape, dim)


def take_lanes(x, index):
    return lax.gather(
        x, index[..., None], _ROWS, (1, 1), mode=lax.GatherScatterMode.PROMISE_IN_BOUNDS
    )


def rev5(v):
    out = 0
    for k in range(5):
        out = out + (v // 2**k) % 2 * 2 ** (4 - k)
    return out


OFFSETS = sorted(
    [(dx, dz, dc) for dx in range(2) for dz in range(8) for dc in range(2)][1:],
    key=lambda o: (o[0], -min(o[1], 8 - o[1])),
)


def delay_add(firsts, seconds, index, keep):
    rows, tiles = firsts.shape[:2]
    shape = (rows, keep, 8, 128)
    before = seconds[:, tiles - keep - 1 : tiles - 1] if keep < tiles else seconds
    if keep == tiles > 1:
        before = jnp.concatenate([seconds[:, :1], seconds[:, :-1]], axis=1)
    lane = iota(index.shape, 2)
    wraps = jnp.broadcast_to((((lane + lane - index) & 127) < lane)[:, None], shape)
    merged = jnp.where(wraps, before, seconds[:, tiles - keep :])
    spread = jnp.broadcast_to(index[:, None], shape).reshape(-1, 128)
    return firsts[:, tiles - keep :] + take_lanes(merged.reshape(-1, 128), spread).reshape(shape)


def major_section(x, index, apart, keep):
    rows, tiles = x.shape[:2]
    shape = (rows // (2 * apart), 2, apart, tiles, 8, 128)
    pairs = x.reshape(shape)
    both = [jnp.broadcast_to(pairs[:, e : e + 1], shape).reshape(x.shape) for e in (0, 1)]
    return delay_add(*both, index, keep)


def folded_section(x, index, apart, grow):
    rows, tiles = x.shape[:2]
    shape = (rows // (2 * apart), 2, apart, tiles, 8, 128)
    pairs = x.reshape(shape)
    firsts, seconds = (jnp.broadcast_to(pairs[:, e : e + 1], shape).reshape(x.shape) for e in (0, 1))
    spread = jnp.broadcast_to(index[:, None], x.shape).reshape(-1, 128)
    turned = take_lanes(seconds.reshape(-1, 128), spread).reshape(x.shape)
    swapped = swap_halves(turned)
    is_low, wraps = iota(index.shape, 1) < 4, index > iota(index.shape, 2)
    empty, outs = jnp.zeros(index.shape, F32), []
    for v in range(tiles + grow):
        before = jnp.where(is_low, swapped[:, v - 1] if v else empty, swapped[:, v] if v < tiles else empty)
        if v < tiles:
            outs.append(firsts[:, v] + jnp.where(wraps, before, turned[:, v]))
        else:
            outs.append(jnp.where(wraps, before, 0.0))
    return jnp.stack(outs, axis=1)


def minor_section(x, index, apart, keep):
    flat = x.reshape(-1, 8, 128)
    is_set = iota(flat.shape, 1) // apart % 2 == 1
    firsts = jnp.where(is_set, pltpu.roll(flat, apart, 1), flat)
    seconds = jnp.where(is_set, flat, pltpu.roll(flat, 8 - apart, 1))
    return delay_add(firsts.reshape(x.shape), seconds.reshape(x.shape), index, keep)


def swap_halves(x):
    return pltpu.roll(x.reshape(-1, 8, 128), 4, 1).reshape(x.shape)


def kernel(
    x_hbm, par, ded_ref, snr_ref,
    xc, shsend, shbuf, idx1, idx2, l0, s7, hsend, hrecv, grecv, fsend, frecv,
    recv, t2, hi, lo, bc, band, roots, stsend, stbuf,
    local_sem, shs_sem, shr_sem, halo_sem, main_send, main_recv, front_send, front_recv, st_send, st_recv,
):
    me, t = lax.axis_index("band"), lax.axis_index("tm")
    copies_x = [
        pltpu.make_async_copy(x_hbm.at[pl.ds(128 * i, 128)], xc.at[pl.ds(128 * i, 128)], local_sem.at[i])
        for i in range(4)
    ]
    for copy in copies_x:
        copy.start()

    barrier = pltpu.get_barrier_semaphore()
    column, place = me // NCOL, me % NCOL
    z, core = place // 2, place % 2

    def dest_of(k):
        dx, dz, dc = OFFSETS[k]
        return (column + dx) % 2 * NCOL + (z + dz) % 8 * 2 + (core + dc) % 2

    own, other = range(NCOL - 1), range(NCOL - 1, NB - 1)
    for k in other:
        pl.semaphore_signal(barrier, inc=1, device_id={"band": dest_of(k)}, device_id_type=MESH)
    for i in range(1, NT):
        pl.semaphore_signal(barrier, inc=1, device_id={"tm": lax.rem(t + i, NT)}, device_id_type=MESH)
    for k in own:
        pl.semaphore_signal(barrier, inc=1, device_id={"band": dest_of(k)}, device_id_type=MESH)
    later = lax.rem(t + 1, NT)
    slot = rev5(me)
    sub8, lane8 = iota((8, 128), 0), iota((8, 128), 1)

    ones = jnp.ones((128, 128), BF16)
    for s in range(1, LOCAL + 1):
        row = jnp.broadcast_to(par[s - 1 : s, :].astype(F32), (8, 128))
        if s <= 5:
            base = sub8 // 2 % 2 * 32 + sub8 % 2 * 64
        else:
            base = sub8 // 2 % 2 * (1, 2)[s - 6] + sub8 % 2 * (64, 1)[s - 6]
        picks = []
        for m in range(32):
            turned = int(f"{m:05b}"[::-1], 2)
            if s <= 5:
                turned = (turned >> (5 - s)) + (m >> s << s)
            else:
                turned = turned << (s - 5)
            picks.append(jnp.where(lane8 - base == turned, row, 0.0))
        picks = jnp.stack(picks).reshape(256, 128).astype(BF16)
        delay = jnp.dot(picks, ones, preferred_element_type=F32).astype(I32)
        idx1[s - 1] = ((iota((256, 128), 1) - delay) & 127).reshape(32, 8, 128)
    for j in range(CROSS - 1):
        shsend[j] = par[LOCAL + j : LOCAL + j + 1, :]
        shbuf[me, j] = par[LOCAL + j : LOCAL + j + 1, :]

    is_low = iota((32, 8, 128), 1) < 4
    i = iota((128, 512), 0)
    group = i // 4 + 32 * (i // 2 % 2) + 64 * (i % 2)
    presum = jnp.where(iota((128, 512), 1) // 4 == group, 1.0, 0.0).astype(BF16)
    level = 0.0
    for i in range(2):
        copies_x[2 * i].wait()
        copies_x[2 * i + 1].wait()
        at = pl.ds(256 * i, 256)
        level = level + jnp.dot(presum[:, 256 * i : 256 * i + 256], xc[at], preferred_element_type=F32)
    for k in range(TILES):
        low, high = (level[:, c * 128 : c * 128 + 128].reshape(16, 8, 128) for c in (k, k + 4))
        if k >= 2:
            hsend[:, k - 2] = high
        low, high = (jnp.stack([p, swap_halves(p)], axis=1).reshape(32, 8, 128) for p in (low, swap_halves(high)))
        l0[:, 2 + k] = jnp.where(is_low, low, high)
        if k >= 2:
            l0[:, k - 2] = jnp.where(is_low, 0.0, swap_halves(low))

    def pack(two_tiles, half):
        first, second = two_tiles
        return jnp.where(is_low, *((swap_halves(first), second) if half else (first, swap_halves(second))))

    def main_copy(part, k):
        dest, which = dest_of(k), (pl.ds(0, 1), pl.ds(1, 2))[part]
        return pltpu.make_async_remote_copy(
            src_ref=s7.at[dest, which], dst_ref=recv.at[slot // 2, slot % 2, which],
            send_sem=main_send.at[part, k], recv_sem=main_recv.at[part, k],
            device_id={"band": dest}, device_id_type=MESH,
        )

    def front_copy(k):
        dest = dest_of(k)
        return pltpu.make_async_remote_copy(
            src_ref=fsend.at[dest], dst_ref=frecv.at[slot // 2, slot % 2],
            send_sem=front_send.at[k], recv_sem=front_recv.at[k],
            device_id={"band": dest}, device_id_type=MESH,
        )

    edges_first = t == NT // 2 - 1

    def start_all(copies):
        for copy in copies:
            copy.start()

    def shift_copy(i):
        needed = pl.ds(0, (i & -i).bit_length())
        return pltpu.make_async_remote_copy(
            src_ref=shsend.at[needed], dst_ref=shbuf.at[me, needed], send_sem=shs_sem.at[i], recv_sem=shr_sem.at[i],
            device_id={"band": lax.rem(me + 2 * i, NB)}, device_id_type=MESH,
        )

    halo_copy = pltpu.make_async_remote_copy(
        src_ref=hsend, dst_ref=hrecv, send_sem=halo_sem.at[0], recv_sem=halo_sem.at[1],
        device_id={"tm": later}, device_id_type=MESH,
    )
    edge_copies = [
        pltpu.make_async_remote_copy(
            src_ref=recv.at[:, column if e == 0 else 1 - column, 0], dst_ref=grecv.at[e],
            send_sem=halo_sem.at[2 + 2 * e], recv_sem=halo_sem.at[3 + 2 * e],
            device_id={"tm": later}, device_id_type=MESH,
        )
        for e in range(2)
    ]
    has_next, has_last = t < NT - 1, t > 0

    def local_sections(first):
        x = l0[:, first : first + 4]
        for s in range(1, LOCAL + 1):
            keep = x.shape[1] - (s in (3, 7))
            if s <= 5:
                x = major_section(x, idx1[s - 1], 2 ** (s - 1), keep)
            else:
                x = minor_section(x, idx1[s - 1], 2 ** (7 - s), keep)
        return x[:, 0], x[:, 1]

    tiles = local_sections(2)
    s7[:, 0] = pack(tiles, 1)
    s7[:, 1] = pack(tiles, 0)
    pl.semaphore_wait(barrier, NB + NT - 2)
    pl.when(has_next)(halo_copy.start)
    for i in range(1, NB // 2):
        shift_copy(i).start()
    start_all(main_copy(0, k) for k in [*own, *other])
    tiles = local_sections(0)
    s7[:, 2] = pack(tiles, 1)
    fsend[...] = pack(tiles, 0)
    pl.when(edges_first)(lambda: start_all(main_copy(1, k) for k in own[:6]))
    start_all(main_copy(1, k) for k in other)
    pl.when(jnp.logical_not(edges_first))(lambda: start_all(main_copy(1, k) for k in own[:6]))
    start_all(main_copy(1, k) for k in own[6:])
    recv[slot // 2, slot % 2] = s7[me]

    offset, sample = iota((256, 128), 0) - 128, iota((256, 128), 1)
    row = jnp.broadcast_to(par[12:13, :], (8, 128))
    for j in range(NBOX):
        width = take_lanes(row, jnp.full((8, 128), j, I32))
        root = jnp.sqrt(width.astype(F32))
        roots[0, j] = root
        roots[1, j] = 1.0 / root
        width = jnp.broadcast_to(width[None], (32, 8, 128)).reshape(256, 128)
        inside = (offset <= sample) & (offset > sample - width)
        band[:, j * 128 : (j + 1) * 128] = jnp.where(inside, 1.0, 0.0).astype(BF16)

    @pl.when(t == 0)
    def _():
        hrecv[...] = jnp.zeros(hrecv.shape, F32)
        grecv[...] = jnp.zeros(grecv.shape, F32)

    pl.when(has_last)(halo_copy.wait_recv)
    def spread_edge(packed):
        return jnp.stack([packed, swap_halves(packed)], axis=1).reshape(-1, 8, 128)

    x = hrecv[...]
    empty = jnp.zeros((16, 1, 8, 128), F32)
    for s in range(1, LOCAL + 1):
        pairs = idx1[s - 1].reshape(16, 2, 8, 128)
        index = jnp.where(iota((16, 8, 128), 1) < 4, pairs[:, 0], pairs[:, 1])
        if s in (1, 5):
            x = jnp.concatenate([x, empty], axis=1)
        keep = x.shape[1] - (s in (3, 7))
        if 2 <= s <= 5:
            x = major_section(x, index, 2 ** (s - 2), keep)
        else:
            x = minor_section(x, index, 4 if s == 1 else 2 ** (7 - s), keep)
    fsend[...] = fsend[...] + pack((spread_edge(x[:, 0]), spread_edge(x[:, 1])), 0)
    hops = [2 * dx + min(dz, 8 - dz) for dx, dz, _ in OFFSETS]
    start_all(front_copy(k) for k in sorted(range(NB - 1), key=lambda k: -hops[k]))
    frecv[slot // 2, slot % 2] = fsend[me]

    for e in range(2):
        for k in other if e else own:
            main_copy(0, k).wait_recv()
        pl.when(has_next)(edge_copies[e].start)

    for i in range(1, NB // 2):
        shift_copy(i).wait_recv()
    quarter = sub8 % 4
    for j in range(1, CROSS + 1):
        base = 0
        for bit in range(j, CROSS):
            base = base + me // 2**bit % 2 * 2 ** (6 - bit + j)
        for low in range(2 ** (CROSS - j)):
            if j < CROSS:
                source = me % 2**j
                for bit in range(j, CROSS):
                    source = source + 2**bit * ((low >> (4 - bit)) & 1)
                row = shbuf[source, j - 1]
            else:
                row = par[LOCAL + j - 1 : LOCAL + j, :]
            row = jnp.broadcast_to(row, (8, 128))
            for high in range(2**j):
                delay = take_lanes(row, base + 2**j * quarter + high)
                idx2[j - 1, low + 2 ** (CROSS - j) * high] = (lane8 - delay) & 127

    for k in [*other, *own]:
        main_copy(1, k).wait_recv()

    def unpack(low, high):
        return jnp.where(is_low, low, swap_halves(high)), jnp.where(is_low, swap_halves(low), high)

    back = unpack(recv[:, :, 1].reshape(32, 8, 128), recv[:, :, 0].reshape(32, 8, 128))
    x = swap_halves(jnp.stack(back, axis=1))
    x = jnp.where(jnp.broadcast_to(is_low[:, None], x.shape), 0.0, x)
    aheads = []
    for j in range(1, CROSS + 1):
        aheads.append(x[:, -1:])
        x = major_section(x, idx2[j - 1], 2 ** (CROSS - j), x.shape[1] - (j == 3))
    front = x

    high = recv[:, :, 2].reshape(32, 8, 128)
    x = jnp.stack([jnp.where(is_low, 0.0, swap_halves(high)), jnp.where(is_low, 0.0, high), *back], axis=1)
    for j in range(1, CROSS + 1):
        x = major_section(jnp.concatenate([aheads[j - 1], x], axis=1), idx2[j - 1], 2 ** (CROSS - j), TILES)
    norm = 16384.0 ** (-0.5)
    x = jnp.concatenate([front, x], axis=1) * norm
    for k in range(5):
        t2[k] = x[:, k].reshape(256, 128)

    def output_rows(k, half):
        return jnp.concatenate([t2[k, pl.ds(b * 64 + half * 4 + q, 8, stride=8), :] for q in range(4) for b in range(4)])

    second = [output_rows(1 + k, 1) for k in range(TILES)]
    pivot = jnp.sum(second[0] + second[1] + second[2] + second[3], axis=1, keepdims=True) * (1.0 / 512)
    pivot = jnp.broadcast_to(pivot, (128, 128))
    sums, squares = jnp.zeros((128, 128), F32), jnp.zeros((128, 128), F32)

    def split(c, centred):
        high = centred.astype(BF16)
        low = (centred - high.astype(F32)).astype(BF16)
        for part, value in ((hi, high), (lo, low)):
            if c >= 0:
                part[128 * c : 128 * c + 128, 128:256] = value
            if c < 2 * TILES - 1:
                part[128 * c + 128 : 128 * c + 256, 0:128] = value

    for k in range(TILES):
        ded_ref[:, 512 + 128 * k : 640 + 128 * k] = second[k]
        centred = second[k] - pivot
        sums, squares = sums + centred, squares + centred * centred
        split(TILES + k, centred)

    def boxcars(first, tiles):
        at = pl.ds(128 * first, 128 * tiles)
        both = jnp.dot(hi[at], band[...], preferred_element_type=F32)
        both = both + jnp.dot(lo[at], band[...], preferred_element_type=F32)
        for j in range(NBOX):
            part = both[:, j * 128 : (j + 1) * 128].reshape(-1, 8, 128)
            part = (part * jnp.broadcast_to(roots[1, j][None], part.shape)).reshape(tiles, 128, 128)
            for c in range(tiles):
                bc[first + c, j] = part[c]

    for k in range(NB - 1):
        front_copy(k).wait_recv()
    for copy in edge_copies:
        pl.when(has_last)(copy.wait_recv)
    y = jnp.stack([grecv[column if f == 0 else 1 - column] for f in range(2)], axis=1).reshape(32, 8, 128)
    y = jnp.stack([y, frecv[...].reshape(32, 8, 128)], axis=1)
    for j in range(1, CROSS + 1):
        y = folded_section(y, idx2[j - 1], 2 ** (CROSS - j), j == 1)
    added = [swap_halves(y[:, 0]), y[:, 1], swap_halves(y[:, 1]), y[:, 2], swap_halves(y[:, 2])]
    for k in range(5):
        t2[k] = (x[:, k] + jnp.where(is_low, added[k], 0.0) * norm).reshape(256, 128)
    first = [output_rows(k, 0) for k in range(5)]
    for k in range(1, 5):
        centred = first[k] - pivot
        sums, squares = sums + centred, squares + centred * centred
    sums = jnp.broadcast_to(jnp.sum(sums, axis=1, keepdims=True), (128, 128))
    squares = jnp.broadcast_to(jnp.sum(squares, axis=1, keepdims=True), (128, 128))
    squares = squares - sums * sums * (1.0 / 1024)
    sums = pivot + sums * (1.0 / 1024)
    mine = jnp.transpose(jnp.where(iota((128, 128), 1) == 0, sums, squares))[0:2]
    stsend[...] = mine
    stbuf[t] = mine

    def stat_copy(i):
        return pltpu.make_async_remote_copy(
            src_ref=stsend, dst_ref=stbuf.at[t], send_sem=st_send.at[i], recv_sem=st_recv.at[i],
            device_id={"tm": lax.rem(t + i, NT)}, device_id_type=MESH,
        )

    for i in range(1, NT):
        stat_copy(i).start()

    for k in range(5):
        split(k - 1, first[k] - pivot)
        if k:
            ded_ref[:, 128 * k - 128 : 128 * k] = first[k]
    boxcars(0, 2 * TILES)
    for k in range(NB - 1):
        main_copy(0, k).wait_send()
        main_copy(1, k).wait_send()
        front_copy(k).wait_send()
    for i in range(1, NB // 2):
        shift_copy(i).wait_send()
    pl.when(has_next)(halo_copy.wait_send)
    for e in range(2):
        pl.when(has_next)(edge_copies[e].wait_send)
    for i in range(1, NT):
        stat_copy(i).wait_recv()
    means = [stbuf[i][0:1] for i in range(NT)]
    mean = sum(means) * (1.0 / NT)
    centred = [stbuf[i][1:2] + 1024.0 * ((m - mean) * (m - mean)) for i, m in enumerate(means)]
    scale = 1.0 / jnp.sqrt(sum(centred) * (1.0 / SAMPLES) + 1e-6)
    row_mean = jnp.transpose(jnp.broadcast_to(mean, (128, 128)))
    row_scale = jnp.transpose(jnp.broadcast_to(scale, (128, 128)))
    off = pivot - row_mean
    for h in range(8):
        at = pl.ds(16 * h, 16)
        best = [None] * (2 * TILES)
        for j in range(NBOX):
            up = jnp.broadcast_to(roots[0, j][None], (2, 8, 128)).reshape(16, 128)
            bias = up * off[16 * h : 16 * h + 16]
            for c in range(2 * TILES):
                score = bc[c, j, at] + bias
                best[c] = score if j == 0 else jnp.maximum(best[c], score)
        for c in range(2 * TILES):
            snr_ref[at, 128 * c : 128 * c + 128] = best[c] * row_scale[16 * h : 16 * h + 16]
    for i in range(1, NT):
        stat_copy(i).wait_send()


def store(a, b, a_hbm, b_hbm, sem):
    copies = [pltpu.make_async_copy(a, a_hbm, sem.at[0]), pltpu.make_async_copy(b, b_hbm, sem.at[1])]
    for copy in copies:
        copy.start()
    for copy in copies:
        copy.wait()


def body(intensity, shifts, boxcar_widths):
    dma = pltpu.SemaphoreType.DMA
    vmem, whole = pltpu.VMEM, pl.BlockSpec(memory_space=pl.ANY)
    in_vmem = pl.BlockSpec(memory_space=pltpu.VMEM)
    out = jax.ShapeDtypeStruct((128, 1024), F32)
    params = jnp.pad(shifts, ((0, 4), (0, 0)))
    params = lax.dynamic_update_slice(params, boxcar_widths[None], (12, 0))
    ded, snr = pl.pallas_call(
        kernel,
        out_shape=(out, out),
        in_specs=[whole, in_vmem],
        out_specs=[in_vmem] * 2,
        scratch_shapes=[
            vmem((512, 1024), BF16),
            vmem((4, 1, 128), I32),
            vmem((NB, 4, 1, 128), I32),
            vmem((LOCAL, 32, 8, 128), I32),
            vmem((CROSS, 32, 8, 128), I32),
            vmem((32, 6, 8, 128), F32),
            vmem((32, 3, 8, 128), F32),
            vmem((16, 2, 8, 128), F32),
            vmem((16, 2, 8, 128), F32),
            vmem((2, 16, 8, 128), F32),
            vmem((32, 8, 128), F32),
            vmem((16, 2, 8, 128), F32),
            vmem((16, 2, 3, 8, 128), F32),
            vmem((5, 256, 128), F32),
            vmem((1024, 256), BF16),
            vmem((1024, 256), BF16),
            vmem((2 * TILES, NBOX, 128, 128), F32),
            vmem((256, 1024), BF16),
            vmem((2, NBOX, 8, 128), F32),
            vmem((2, 128), F32),
            vmem((NT, 2, 128), F32),
            dma((4,)),
            dma((NB // 2,)),
            dma((NB // 2,)),
            dma((6,)),
            dma((2, NB - 1)),
            dma((2, NB - 1)),
            dma((NB - 1,)),
            dma((NB - 1,)),
            dma((NT,)),
            dma((NT,)),
        ],
        compiler_params=pltpu.CompilerParams(
            collective_id=0, has_side_effects=True, vmem_limit_bytes=52 * 2**20
        ),
    )(intensity, params)
    return pl.pallas_call(
        store,
        out_shape=(out, out),
        in_specs=[in_vmem] * 2,
        out_specs=[whole] * 2,
        scratch_shapes=[dma((2,))],
        compiler_params=pltpu.CompilerParams(vmem_limit_bytes=52 * 2**20),
    )(ded, snr)


def solution(mesh):
    assert mesh.shape["band"] == NB and mesh.shape["tm"] == NT
    in_specs = (P("band", "tm"), P(None, "band"), P())
    out_specs = (P("band", "tm"), P("band", "tm"))
    return jax.shard_map(body, mesh=mesh, in_specs=in_specs, out_specs=out_specs, check_vma=False)
```

```python
import jax
import jax.numpy as jnp
from jax import lax
from jax.experimental import pallas as pl
from jax.experimental.pallas import tpu as pltpu
from jax.sharding import PartitionSpec as P

MESH = pl.DeviceIdType.MESH
F32, BF16, I32 = jnp.float32, jnp.bfloat16, jnp.int32
NB, NT = 32, 8
NBOX = 8
NCOL = 16
LOCAL, CROSS = 7, 5
TILES = 4
SAMPLES = 8192

_ROWS = lax.GatherDimensionNumbers(
    offset_dims=(),
    collapsed_slice_dims=(1,),
    start_index_map=(1,),
    operand_batching_dims=(0,),
    start_indices_batching_dims=(0,),
)


def iota(shape, dim):
    return lax.broadcasted_iota(I32, shape, dim)


def take_lanes(x, index):
    return lax.gather(
        x, index[..., None], _ROWS, (1, 1), mode=lax.GatherScatterMode.PROMISE_IN_BOUNDS
    )


def rev5(v):
    out = 0
    for k in range(5):
        out = out + (v // 2**k) % 2 * 2 ** (4 - k)
    return out


OFFSETS = sorted(
    [(dx, dz, dc) for dx in range(2) for dz in range(8) for dc in range(2)][1:],
    key=lambda o: (o[0], -min(o[1], 8 - o[1])),
)


def delay_add(firsts, seconds, index, keep):
    rows, tiles = firsts.shape[:2]
    shape = (rows, keep, 8, 128)
    before = seconds[:, tiles - keep - 1 : tiles - 1] if keep < tiles else seconds
    if keep == tiles > 1:
        before = jnp.concatenate([seconds[:, :1], seconds[:, :-1]], axis=1)
    lane = iota(index.shape, 2)
    wraps = jnp.broadcast_to((((lane + lane - index) & 127) < lane)[:, None], shape)
    merged = jnp.where(wraps, before, seconds[:, tiles - keep :])
    spread = jnp.broadcast_to(index[:, None], shape).reshape(-1, 128)
    return firsts[:, tiles - keep :] + take_lanes(merged.reshape(-1, 128), spread).reshape(shape)


def major_section(x, index, apart, keep):
    rows, tiles = x.shape[:2]
    shape = (rows // (2 * apart), 2, apart, tiles, 8, 128)
    pairs = x.reshape(shape)
    both = [jnp.broadcast_to(pairs[:, e : e + 1], shape).reshape(x.shape) for e in (0, 1)]
    return delay_add(*both, index, keep)


def folded_section(x, index, apart, grow):
    rows, tiles = x.shape[:2]
    shape = (rows // (2 * apart), 2, apart, tiles, 8, 128)
    pairs = x.reshape(shape)
    firsts, seconds = (jnp.broadcast_to(pairs[:, e : e + 1], shape).reshape(x.shape) for e in (0, 1))
    spread = jnp.broadcast_to(index[:, None], x.shape).reshape(-1, 128)
    turned = take_lanes(seconds.reshape(-1, 128), spread).reshape(x.shape)
    swapped = swap_halves(turned)
    is_low, wraps = iota(index.shape, 1) < 4, index > iota(index.shape, 2)
    empty, outs = jnp.zeros(index.shape, F32), []
    for v in range(tiles + grow):
        before = jnp.where(is_low, swapped[:, v - 1] if v else empty, swapped[:, v] if v < tiles else empty)
        if v < tiles:
            outs.append(firsts[:, v] + jnp.where(wraps, before, turned[:, v]))
        else:
            outs.append(jnp.where(wraps, before, 0.0))
    return jnp.stack(outs, axis=1)


def minor_section(x, index, apart, keep):
    flat = x.reshape(-1, 8, 128)
    is_set = iota(flat.shape, 1) // apart % 2 == 1
    firsts = jnp.where(is_set, pltpu.roll(flat, apart, 1), flat)
    seconds = jnp.where(is_set, flat, pltpu.roll(flat, 8 - apart, 1))
    return delay_add(firsts.reshape(x.shape), seconds.reshape(x.shape), index, keep)


def swap_halves(x):
    return pltpu.roll(x.reshape(-1, 8, 128), 4, 1).reshape(x.shape)


def kernel(
    x_hbm, par, ded_ref, snr_ref,
    xc, shsend, shbuf, idx1, idx2, l0, s7, hsend, hrecv, grecv, fsend, frecv,
    recv, t2, hi, lo, bc, band, roots, stsend, stbuf,
    local_sem, shs_sem, shr_sem, halo_sem, main_send, main_recv, front_send, front_recv, st_send, st_recv,
):
    me, t = lax.axis_index("band"), lax.axis_index("tm")
    copies_x = [
        pltpu.make_async_copy(x_hbm.at[pl.ds(128 * i, 128)], xc.at[pl.ds(128 * i, 128)], local_sem.at[i])
        for i in range(4)
    ]
    for copy in copies_x:
        copy.start()

    barrier = pltpu.get_barrier_semaphore()
    column, place = me // NCOL, me % NCOL
    z, core = place // 2, place % 2

    def dest_of(k):
        dx, dz, dc = OFFSETS[k]
        return (column + dx) % 2 * NCOL + (z + dz) % 8 * 2 + (core + dc) % 2

    own, other = range(NCOL - 1), range(NCOL - 1, NB - 1)
    for k in other:
        pl.semaphore_signal(barrier, inc=1, device_id={"band": dest_of(k)}, device_id_type=MESH)
    for i in range(1, NT):
        pl.semaphore_signal(barrier, inc=1, device_id={"tm": lax.rem(t + i, NT)}, device_id_type=MESH)
    for k in own:
        pl.semaphore_signal(barrier, inc=1, device_id={"band": dest_of(k)}, device_id_type=MESH)
    later = lax.rem(t + 1, NT)
    slot = rev5(me)
    sub8, lane8 = iota((8, 128), 0), iota((8, 128), 1)

    ones = jnp.ones((128, 128), BF16)
    for s in range(1, LOCAL + 1):
        row = jnp.broadcast_to(par[s - 1 : s, :].astype(F32), (8, 128))
        if s <= 5:
            base = sub8 // 2 % 2 * 32 + sub8 % 2 * 64
        else:
            base = sub8 // 2 % 2 * (1, 2)[s - 6] + sub8 % 2 * (64, 1)[s - 6]
        picks = []
        for m in range(32):
            turned = int(f"{m:05b}"[::-1], 2)
            if s <= 5:
                turned = (turned >> (5 - s)) + (m >> s << s)
            else:
                turned = turned << (s - 5)
            picks.append(jnp.where(lane8 - base == turned, row, 0.0))
        picks = jnp.stack(picks).reshape(256, 128).astype(BF16)
        delay = jnp.dot(picks, ones, preferred_element_type=F32).astype(I32)
        idx1[s - 1] = ((iota((256, 128), 1) - delay) & 127).reshape(32, 8, 128)
    for j in range(CROSS - 1):
        shsend[j] = par[LOCAL + j : LOCAL + j + 1, :]
        shbuf[me, j] = par[LOCAL + j : LOCAL + j + 1, :]

    is_low = iota((32, 8, 128), 1) < 4
    i = iota((128, 512), 0)
    group = i // 4 + 32 * (i // 2 % 2) + 64 * (i % 2)
    presum = jnp.where(iota((128, 512), 1) // 4 == group, 1.0, 0.0).astype(BF16)
    level = 0.0
    for i in range(2):
        copies_x[2 * i].wait()
        copies_x[2 * i + 1].wait()
        at = pl.ds(256 * i, 256)
        level = level + jnp.dot(presum[:, 256 * i : 256 * i + 256], xc[at], preferred_element_type=F32)
    for k in range(TILES):
        low, high = (level[:, c * 128 : c * 128 + 128].reshape(16, 8, 128) for c in (k, k + 4))
        if k >= 2:
            hsend[:, k - 2] = high
        low, high = (jnp.stack([p, swap_halves(p)], axis=1).reshape(32, 8, 128) for p in (low, swap_halves(high)))
        l0[:, 2 + k] = jnp.where(is_low, low, high)
        if k >= 2:
            l0[:, k - 2] = jnp.where(is_low, 0.0, swap_halves(low))

    def pack(two_tiles, half):
        first, second = two_tiles
        return jnp.where(is_low, *((swap_halves(first), second) if half else (first, swap_halves(second))))

    def main_copy(part, k):
        dest, which = dest_of(k), (pl.ds(0, 1), pl.ds(1, 2))[part]
        return pltpu.make_async_remote_copy(
            src_ref=s7.at[dest, which], dst_ref=recv.at[slot // 2, slot % 2, which],
            send_sem=main_send.at[part, k], recv_sem=main_recv.at[part, k],
            device_id={"band": dest}, device_id_type=MESH,
        )

    def front_copy(k):
        dest = dest_of(k)
        return pltpu.make_async_remote_copy(
            src_ref=fsend.at[dest], dst_ref=frecv.at[slot // 2, slot % 2],
            send_sem=front_send.at[k], recv_sem=front_recv.at[k],
            device_id={"band": dest}, device_id_type=MESH,
        )

    edges_first = t == NT // 2 - 1

    def start_all(copies):
        for copy in copies:
            copy.start()

    def shift_copy(i):
        needed = pl.ds(0, (i & -i).bit_length())
        return pltpu.make_async_remote_copy(
            src_ref=shsend.at[needed], dst_ref=shbuf.at[me, needed], send_sem=shs_sem.at[i], recv_sem=shr_sem.at[i],
            device_id={"band": lax.rem(me + 2 * i, NB)}, device_id_type=MESH,
        )

    halo_copy = pltpu.make_async_remote_copy(
        src_ref=hsend, dst_ref=hrecv, send_sem=halo_sem.at[0], recv_sem=halo_sem.at[1],
        device_id={"tm": later}, device_id_type=MESH,
    )
    edge_copies = [
        pltpu.make_async_remote_copy(
            src_ref=recv.at[:, column if e == 0 else 1 - column, 0], dst_ref=grecv.at[e],
            send_sem=halo_sem.at[2 + 2 * e], recv_sem=halo_sem.at[3 + 2 * e],
            device_id={"tm": later}, device_id_type=MESH,
        )
        for e in range(2)
    ]
    has_next, has_last = t < NT - 1, t > 0

    def local_sections(first):
        x = l0[:, first : first + 4]
        for s in range(1, LOCAL + 1):
            keep = x.shape[1] - (s in (3, 7))
            if s <= 5:
                x = major_section(x, idx1[s - 1], 2 ** (s - 1), keep)
            else:
                x = minor_section(x, idx1[s - 1], 2 ** (7 - s), keep)
        return x[:, 0], x[:, 1]

    tiles = local_sections(2)
    s7[:, 0] = pack(tiles, 1)
    s7[:, 1] = pack(tiles, 0)
    pl.semaphore_wait(barrier, NB + NT - 2)
    pl.when(has_next)(halo_copy.start)
    hops = [2 * dx + min(dz, 8 - dz) for dx, dz, _ in OFFSETS]
    by_hops = sorted(range(NB - 1), key=lambda k: -hops[k])
    pl.when(edges_first)(lambda: start_all(main_copy(0, k) for k in [*own, *other]))
    pl.when(jnp.logical_not(edges_first))(lambda: start_all(main_copy(0, k) for k in by_hops))
    start_all(shift_copy(i) for i in range(1, NB // 2))
    tiles = local_sections(0)
    s7[:, 2] = pack(tiles, 1)
    fsend[...] = pack(tiles, 0)
    pl.when(edges_first)(lambda: start_all(main_copy(1, k) for k in [*own[:6], *other, *own[6:]]))
    pl.when(jnp.logical_not(edges_first))(lambda: start_all(main_copy(1, k) for k in by_hops))
    recv[slot // 2, slot % 2] = s7[me]

    @pl.when(t == 0)
    def _():
        hrecv[...] = jnp.zeros(hrecv.shape, F32)
        grecv[...] = jnp.zeros(grecv.shape, F32)

    pl.when(has_last)(halo_copy.wait_recv)
    def spread_edge(packed):
        return jnp.stack([packed, swap_halves(packed)], axis=1).reshape(-1, 8, 128)

    x = hrecv[...]
    empty = jnp.zeros((16, 1, 8, 128), F32)
    for s in range(1, LOCAL + 1):
        pairs = idx1[s - 1].reshape(16, 2, 8, 128)
        index = jnp.where(iota((16, 8, 128), 1) < 4, pairs[:, 0], pairs[:, 1])
        if s in (1, 5):
            x = jnp.concatenate([x, empty], axis=1)
        keep = x.shape[1] - (s in (3, 7))
        if 2 <= s <= 5:
            x = major_section(x, index, 2 ** (s - 2), keep)
        else:
            x = minor_section(x, index, 4 if s == 1 else 2 ** (7 - s), keep)
    fsend[...] = fsend[...] + pack((spread_edge(x[:, 0]), spread_edge(x[:, 1])), 0)
    start_all(front_copy(k) for k in by_hops)
    frecv[slot // 2, slot % 2] = fsend[me]

    for e in range(2):
        for k in other if e else own:
            main_copy(0, k).wait_recv()
        pl.when(has_next)(edge_copies[e].start)

    offset, sample = iota((256, 128), 0) - 128, iota((256, 128), 1)
    row = jnp.broadcast_to(par[12:13, :], (8, 128))
    for j in range(NBOX):
        width = take_lanes(row, jnp.full((8, 128), j, I32))
        root = jnp.sqrt(width.astype(F32))
        roots[0, j] = root
        roots[1, j] = 1.0 / root
        width = jnp.broadcast_to(width[None], (32, 8, 128)).reshape(256, 128)
        inside = (offset <= sample) & (offset > sample - width)
        band[:, j * 128 : (j + 1) * 128] = jnp.where(inside, 1.0, 0.0).astype(BF16)

    for i in range(1, NB // 2):
        shift_copy(i).wait_recv()
    quarter = sub8 % 4
    for j in range(1, CROSS + 1):
        base = 0
        for bit in range(j, CROSS):
            base = base + me // 2**bit % 2 * 2 ** (6 - bit + j)
        for low in range(2 ** (CROSS - j)):
            if j < CROSS:
                source = me % 2**j
                for bit in range(j, CROSS):
                    source = source + 2**bit * ((low >> (4 - bit)) & 1)
                row = shbuf[source, j - 1]
            else:
                row = par[LOCAL + j - 1 : LOCAL + j, :]
            row = jnp.broadcast_to(row, (8, 128))
            for high in range(2**j):
                delay = take_lanes(row, base + 2**j * quarter + high)
                idx2[j - 1, low + 2 ** (CROSS - j) * high] = (lane8 - delay) & 127

    for k in [*other, *own]:
        main_copy(1, k).wait_recv()

    def unpack(low, high):
        return jnp.where(is_low, low, swap_halves(high)), jnp.where(is_low, swap_halves(low), high)

    back = unpack(recv[:, :, 1].reshape(32, 8, 128), recv[:, :, 0].reshape(32, 8, 128))
    x = swap_halves(jnp.stack(back, axis=1))
    x = jnp.where(jnp.broadcast_to(is_low[:, None], x.shape), 0.0, x)
    aheads = []
    for j in range(1, CROSS + 1):
        aheads.append(x[:, -1:])
        x = major_section(x, idx2[j - 1], 2 ** (CROSS - j), x.shape[1] - (j == 3))
    front = x

    high = recv[:, :, 2].reshape(32, 8, 128)
    x = jnp.stack([jnp.where(is_low, 0.0, swap_halves(high)), jnp.where(is_low, 0.0, high), *back], axis=1)
    for j in range(1, CROSS + 1):
        x = major_section(jnp.concatenate([aheads[j - 1], x], axis=1), idx2[j - 1], 2 ** (CROSS - j), TILES)
    norm = 16384.0 ** (-0.5)
    x = jnp.concatenate([front, x], axis=1) * norm
    for k in range(5):
        t2[k, 0:256] = x[:, k].reshape(256, 128)

    def output_rows(k, half):
        return jnp.concatenate([t2[k, pl.ds(b * 64 + half * 4 + q, 8, stride=8), :] for q in range(4) for b in range(4)])

    second = [output_rows(1 + k, 1) for k in range(TILES)]
    pivot = jnp.sum(second[0] + second[1] + second[2] + second[3], axis=1, keepdims=True) * (1.0 / 512)
    pivot = jnp.broadcast_to(pivot, (128, 128))
    sums, squares = jnp.zeros((128, 128), F32), jnp.zeros((128, 128), F32)

    def split(c, centred):
        high = centred.astype(BF16)
        low = (centred - high.astype(F32)).astype(BF16)
        for part, value in ((hi, high), (lo, low)):
            if c >= 0:
                part[128 * c : 128 * c + 128, 128:256] = value
            if c < 2 * TILES - 1:
                part[128 * c + 128 : 128 * c + 256, 0:128] = value

    for k in range(TILES):
        ded_ref[:, 512 + 128 * k : 640 + 128 * k] = second[k]
        centred = second[k] - pivot
        sums, squares = sums + centred, squares + centred * centred
        split(TILES + k, centred)

    def boxcars(first, tiles):
        at = pl.ds(128 * first, 128 * tiles)
        both = jnp.dot(hi[at], band[...], preferred_element_type=F32)
        both = both + jnp.dot(lo[at], band[...], preferred_element_type=F32)
        for j in range(NBOX):
            part = both[:, j * 128 : (j + 1) * 128].reshape(-1, 8, 128)
            part = (part * jnp.broadcast_to(roots[1, j][None], part.shape)).reshape(tiles, 128, 128)
            for c in range(tiles):
                bc[first + c, j] = part[c]

    for k in range(NB - 1):
        front_copy(k).wait_recv()
    for copy in edge_copies:
        pl.when(has_last)(copy.wait_recv)
    y = jnp.stack([grecv[column if f == 0 else 1 - column] for f in range(2)], axis=1).reshape(32, 8, 128)
    y = jnp.stack([y, frecv[...].reshape(32, 8, 128)], axis=1)
    for j in range(1, CROSS + 1):
        y = folded_section(y, idx2[j - 1], 2 ** (CROSS - j), j == 1)
    added = [swap_halves(y[:, 0]), y[:, 1], swap_halves(y[:, 1]), y[:, 2], swap_halves(y[:, 2])]
    for k in range(5):
        t2[k, 0:256] = (x[:, k] + jnp.where(is_low, added[k], 0.0) * norm).reshape(256, 128)
    first = [output_rows(k, 0) for k in range(5)]
    for k in range(1, 5):
        centred = first[k] - pivot
        sums, squares = sums + centred, squares + centred * centred
    sums = jnp.broadcast_to(jnp.sum(sums, axis=1, keepdims=True), (128, 128))
    squares = jnp.broadcast_to(jnp.sum(squares, axis=1, keepdims=True), (128, 128))
    squares = squares - sums * sums * (1.0 / 1024)
    sums = pivot + sums * (1.0 / 1024)
    mine = jnp.transpose(jnp.where(iota((128, 128), 1) == 0, sums, squares))[0:2]
    stsend[...] = mine
    stbuf[t] = mine

    def stat_copy(i):
        return pltpu.make_async_remote_copy(
            src_ref=stsend, dst_ref=stbuf.at[t], send_sem=st_send.at[i], recv_sem=st_recv.at[i],
            device_id={"tm": lax.rem(t + i, NT)}, device_id_type=MESH,
        )

    start_all(stat_copy(i) for i in (2, 6, 3, 5, 1, 7, 4))

    for k in range(5):
        split(k - 1, first[k] - pivot)
        if k:
            ded_ref[:, 128 * k - 128 : 128 * k] = first[k]
    boxcars(0, 2 * TILES)
    for k in range(NB - 1):
        main_copy(0, k).wait_send()
        main_copy(1, k).wait_send()
        front_copy(k).wait_send()
    for i in range(1, NB // 2):
        shift_copy(i).wait_send()
    pl.when(has_next)(halo_copy.wait_send)
    for e in range(2):
        pl.when(has_next)(edge_copies[e].wait_send)
    for i in range(1, NT):
        stat_copy(i).wait_recv()
    means = [stbuf[i][0:1] for i in range(NT)]
    mean = sum(means) * (1.0 / NT)
    centred = [stbuf[i][1:2] + 1024.0 * ((m - mean) * (m - mean)) for i, m in enumerate(means)]
    scale = 1.0 / jnp.sqrt(sum(centred) * (1.0 / SAMPLES) + 1e-6)
    row_mean = jnp.transpose(jnp.broadcast_to(mean, (128, 128)))
    row_scale = jnp.transpose(jnp.broadcast_to(scale, (128, 128)))
    off = pivot - row_mean
    for h in range(8):
        at = pl.ds(16 * h, 16)
        best = [None] * (2 * TILES)
        for j in range(NBOX):
            up = jnp.broadcast_to(roots[0, j][None], (2, 8, 128)).reshape(16, 128)
            bias = up * off[16 * h : 16 * h + 16]
            for c in range(2 * TILES):
                score = bc[c, j, at] + bias
                best[c] = score if j == 0 else jnp.maximum(best[c], score)
        for c in range(2 * TILES):
            snr_ref[at, 128 * c : 128 * c + 128] = best[c] * row_scale[16 * h : 16 * h + 16]
    for i in range(1, NT):
        stat_copy(i).wait_send()


def store(a, b, a_hbm, b_hbm, sem):
    copies = [pltpu.make_async_copy(a, a_hbm, sem.at[0]), pltpu.make_async_copy(b, b_hbm, sem.at[1])]
    for copy in copies:
        copy.start()
    for copy in copies:
        copy.wait()


def body(intensity, shifts, boxcar_widths):
    dma = pltpu.SemaphoreType.DMA
    vmem, whole = pltpu.VMEM, pl.BlockSpec(memory_space=pl.ANY)
    in_vmem = pl.BlockSpec(memory_space=pltpu.VMEM)
    out = jax.ShapeDtypeStruct((128, 1024), F32)
    params = jnp.pad(shifts, ((0, 4), (0, 0)))
    params = lax.dynamic_update_slice(params, boxcar_widths[None], (12, 0))
    ded, snr = pl.pallas_call(
        kernel,
        out_shape=(out, out),
        in_specs=[whole, in_vmem],
        out_specs=[in_vmem] * 2,
        scratch_shapes=[
            vmem((512, 1024), BF16),
            vmem((4, 1, 128), I32),
            vmem((NB, 4, 1, 128), I32),
            vmem((LOCAL, 32, 8, 128), I32),
            vmem((CROSS, 32, 8, 128), I32),
            vmem((32, 6, 8, 128), F32),
            vmem((32, 3, 8, 128), F32),
            vmem((16, 2, 8, 128), F32),
            vmem((16, 2, 8, 128), F32),
            vmem((2, 16, 8, 128), F32),
            vmem((32, 8, 128), F32),
            vmem((16, 2, 8, 128), F32),
            vmem((16, 2, 3, 8, 128), F32),
            vmem((5, 264, 128), F32),
            vmem((1024, 256), BF16),
            vmem((1024, 256), BF16),
            vmem((2 * TILES, NBOX, 128, 128), F32),
            vmem((256, 1024), BF16),
            vmem((2, NBOX, 8, 128), F32),
            vmem((2, 128), F32),
            vmem((NT, 2, 128), F32),
            dma((4,)),
            dma((NB // 2,)),
            dma((NB // 2,)),
            dma((6,)),
            dma((2, NB - 1)),
            dma((2, NB - 1)),
            dma((NB - 1,)),
            dma((NB - 1,)),
            dma((NT,)),
            dma((NT,)),
        ],
        compiler_params=pltpu.CompilerParams(
            collective_id=0, has_side_effects=True, vmem_limit_bytes=52 * 2**20
        ),
    )(intensity, params)
    return pl.pallas_call(
        store,
        out_shape=(out, out),
        in_specs=[in_vmem] * 2,
        out_specs=[whole] * 2,
        scratch_shapes=[dma((2,))],
        compiler_params=pltpu.CompilerParams(vmem_limit_bytes=52 * 2**20),
    )(ded, snr)


def solution(mesh):
    assert mesh.shape["band"] == NB and mesh.shape["tm"] == NT
    in_specs = (P("band", "tm"), P(None, "band"), P())
    out_specs = (P("band", "tm"), P("band", "tm"))
    return jax.shard_map(body, mesh=mesh, in_specs=in_specs, out_specs=out_specs, check_vma=False)
```

```python
import jax
import jax.numpy as jnp
from jax import lax
from jax.experimental import pallas as pl
from jax.experimental.pallas import tpu as pltpu
from jax.sharding import PartitionSpec as P

MESH = pl.DeviceIdType.MESH
F32, BF16, I32 = jnp.float32, jnp.bfloat16, jnp.int32
NB, NT = 32, 8
NBOX = 8
NCOL = 16
LOCAL, CROSS = 7, 5
TILES = 4
SAMPLES = 8192

_ROWS = lax.GatherDimensionNumbers(
    offset_dims=(),
    collapsed_slice_dims=(1,),
    start_index_map=(1,),
    operand_batching_dims=(0,),
    start_indices_batching_dims=(0,),
)


def iota(shape, dim):
    return lax.broadcasted_iota(I32, shape, dim)


def take_lanes(x, index):
    return lax.gather(
        x, index[..., None], _ROWS, (1, 1), mode=lax.GatherScatterMode.PROMISE_IN_BOUNDS
    )


def rev5(v):
    out = 0
    for k in range(5):
        out = out + (v // 2**k) % 2 * 2 ** (4 - k)
    return out


OFFSETS = sorted(
    [(dx, dz, dc) for dx in range(2) for dz in range(8) for dc in range(2)][1:],
    key=lambda o: (o[0], -min(o[1], 8 - o[1])),
)


def delay_add(firsts, seconds, index, keep):
    rows, tiles = firsts.shape[:2]
    shape = (rows, keep, 8, 128)
    before = seconds[:, tiles - keep - 1 : tiles - 1] if keep < tiles else seconds
    if keep == tiles > 1:
        before = jnp.concatenate([seconds[:, :1], seconds[:, :-1]], axis=1)
    lane = iota(index.shape, 2)
    wraps = jnp.broadcast_to((((lane + lane - index) & 127) < lane)[:, None], shape)
    merged = jnp.where(wraps, before, seconds[:, tiles - keep :])
    spread = jnp.broadcast_to(index[:, None], shape).reshape(-1, 128)
    return firsts[:, tiles - keep :] + take_lanes(merged.reshape(-1, 128), spread).reshape(shape)


def major_section(x, index, apart, keep):
    rows, tiles = x.shape[:2]
    shape = (rows // (2 * apart), 2, apart, tiles, 8, 128)
    pairs = x.reshape(shape)
    both = [jnp.broadcast_to(pairs[:, e : e + 1], shape).reshape(x.shape) for e in (0, 1)]
    return delay_add(*both, index, keep)


def folded_section(x, index, apart, grow):
    rows, tiles = x.shape[:2]
    shape = (rows // (2 * apart), 2, apart, tiles, 8, 128)
    pairs = x.reshape(shape)
    firsts, seconds = (jnp.broadcast_to(pairs[:, e : e + 1], shape).reshape(x.shape) for e in (0, 1))
    spread = jnp.broadcast_to(index[:, None], x.shape).reshape(-1, 128)
    turned = take_lanes(seconds.reshape(-1, 128), spread).reshape(x.shape)
    swapped = swap_halves(turned)
    is_low, wraps = iota(index.shape, 1) < 4, index > iota(index.shape, 2)
    empty, outs = jnp.zeros(index.shape, F32), []
    for v in range(tiles + grow):
        before = jnp.where(is_low, swapped[:, v - 1] if v else empty, swapped[:, v] if v < tiles else empty)
        if v < tiles:
            outs.append(firsts[:, v] + jnp.where(wraps, before, turned[:, v]))
        else:
            outs.append(jnp.where(wraps, before, 0.0))
    return jnp.stack(outs, axis=1)


def minor_section(x, index, apart, keep):
    flat = x.reshape(-1, 8, 128)
    is_set = iota(flat.shape, 1) // apart % 2 == 1
    firsts = jnp.where(is_set, pltpu.roll(flat, apart, 1), flat)
    seconds = jnp.where(is_set, flat, pltpu.roll(flat, 8 - apart, 1))
    return delay_add(firsts.reshape(x.shape), seconds.reshape(x.shape), index, keep)


def swap_halves(x):
    return pltpu.roll(x.reshape(-1, 8, 128), 4, 1).reshape(x.shape)


def kernel(
    x_hbm, par, ded_ref, snr_ref,
    xc, shsend, shbuf, idx1, idx2, l0, s7, hsend, hrecv, grecv, fsend, frecv,
    recv, t2, hi, lo, bc, band, roots, stsend, stbuf,
    local_sem, shs_sem, shr_sem, halo_sem, main_send, main_recv, front_send, front_recv, st_send, st_recv,
):
    me, t = lax.axis_index("band"), lax.axis_index("tm")
    copies_x = [
        pltpu.make_async_copy(x_hbm.at[pl.ds(128 * i, 128)], xc.at[pl.ds(128 * i, 128)], local_sem.at[i])
        for i in range(4)
    ]
    for copy in copies_x:
        copy.start()

    barrier = pltpu.get_barrier_semaphore()
    column, place = me // NCOL, me % NCOL
    z, core = place // 2, place % 2

    def dest_of(k):
        dx, dz, dc = OFFSETS[k]
        return (column + dx) % 2 * NCOL + (z + dz) % 8 * 2 + (core + dc) % 2

    own, other = range(NCOL - 1), range(NCOL - 1, NB - 1)
    for k in other:
        pl.semaphore_signal(barrier, inc=1, device_id={"band": dest_of(k)}, device_id_type=MESH)
    for i in range(1, NT):
        pl.semaphore_signal(barrier, inc=1, device_id={"tm": lax.rem(t + i, NT)}, device_id_type=MESH)
    for k in own:
        pl.semaphore_signal(barrier, inc=1, device_id={"band": dest_of(k)}, device_id_type=MESH)
    later = lax.rem(t + 1, NT)
    slot = rev5(me)
    sub8, lane8 = iota((8, 128), 0), iota((8, 128), 1)

    ones = jnp.ones((128, 128), BF16)
    for s in range(1, LOCAL + 1):
        row = jnp.broadcast_to(par[s - 1 : s, :].astype(F32), (8, 128))
        if s <= 5:
            base = sub8 // 2 % 2 * 32 + sub8 % 2 * 64
        else:
            base = sub8 // 2 % 2 * (1, 2)[s - 6] + sub8 % 2 * (64, 1)[s - 6]
        picks = []
        for m in range(32):
            turned = int(f"{m:05b}"[::-1], 2)
            if s <= 5:
                turned = (turned >> (5 - s)) + (m >> s << s)
            else:
                turned = turned << (s - 5)
            picks.append(jnp.where(lane8 - base == turned, row, 0.0))
        picks = jnp.stack(picks).reshape(256, 128).astype(BF16)
        delay = jnp.dot(picks, ones, preferred_element_type=F32).astype(I32)
        idx1[s - 1] = ((iota((256, 128), 1) - delay) & 127).reshape(32, 8, 128)
    for j in range(CROSS - 1):
        shsend[j] = par[LOCAL + j : LOCAL + j + 1, :]
        shbuf[me, j] = par[LOCAL + j : LOCAL + j + 1, :]

    is_low = iota((32, 8, 128), 1) < 4
    i = iota((128, 512), 0)
    group = i // 4 + 32 * (i // 2 % 2) + 64 * (i % 2)
    presum = jnp.where(iota((128, 512), 1) // 4 == group, 1.0, 0.0).astype(BF16)
    level = 0.0
    for i in range(2):
        copies_x[2 * i].wait()
        copies_x[2 * i + 1].wait()
        at = pl.ds(256 * i, 256)
        level = level + jnp.dot(presum[:, 256 * i : 256 * i + 256], xc[at], preferred_element_type=F32)
    for k in range(TILES):
        low, high = (level[:, c * 128 : c * 128 + 128].reshape(16, 8, 128) for c in (k, k + 4))
        if k >= 2:
            hsend[:, k - 2] = high
        low, high = (jnp.stack([p, swap_halves(p)], axis=1).reshape(32, 8, 128) for p in (low, swap_halves(high)))
        l0[:, 2 + k] = jnp.where(is_low, low, high)
        if k >= 2:
            l0[:, k - 2] = jnp.where(is_low, 0.0, swap_halves(low))

    def pack(two_tiles, half):
        first, second = two_tiles
        return jnp.where(is_low, *((swap_halves(first), second) if half else (first, swap_halves(second))))

    def main_copy(part, k):
        dest, which = dest_of(k), (pl.ds(0, 1), pl.ds(1, 2))[part]
        return pltpu.make_async_remote_copy(
            src_ref=s7.at[dest, which], dst_ref=recv.at[slot // 2, slot % 2, which],
            send_sem=main_send.at[part, k], recv_sem=main_recv.at[part, k],
            device_id={"band": dest}, device_id_type=MESH,
        )

    def front_copy(k):
        dest = dest_of(k)
        return pltpu.make_async_remote_copy(
            src_ref=fsend.at[dest], dst_ref=frecv.at[slot // 2, slot % 2],
            send_sem=front_send.at[k], recv_sem=front_recv.at[k],
            device_id={"band": dest}, device_id_type=MESH,
        )

    edges_first = t == NT // 2 - 1

    def start_all(copies):
        for copy in copies:
            copy.start()

    def shift_copy(i):
        needed = pl.ds(0, (i & -i).bit_length())
        return pltpu.make_async_remote_copy(
            src_ref=shsend.at[needed], dst_ref=shbuf.at[me, needed], send_sem=shs_sem.at[i], recv_sem=shr_sem.at[i],
            device_id={"band": lax.rem(me + 2 * i, NB)}, device_id_type=MESH,
        )

    halo_copy = pltpu.make_async_remote_copy(
        src_ref=hsend, dst_ref=hrecv, send_sem=halo_sem.at[0], recv_sem=halo_sem.at[1],
        device_id={"tm": later}, device_id_type=MESH,
    )
    edge_copies = [
        pltpu.make_async_remote_copy(
            src_ref=recv.at[:, column if e == 0 else 1 - column, 0], dst_ref=grecv.at[e],
            send_sem=halo_sem.at[2 + 2 * e], recv_sem=halo_sem.at[3 + 2 * e],
            device_id={"tm": later}, device_id_type=MESH,
        )
        for e in range(2)
    ]
    has_next, has_last = t < NT - 1, t > 0

    def local_sections(first):
        x = l0[:, first : first + 4]
        for s in range(1, LOCAL + 1):
            keep = x.shape[1] - (s in (3, 7))
            if s <= 5:
                x = major_section(x, idx1[s - 1], 2 ** (s - 1), keep)
            else:
                x = minor_section(x, idx1[s - 1], 2 ** (7 - s), keep)
        return x[:, 0], x[:, 1]

    tiles = local_sections(2)
    s7[:, 0] = pack(tiles, 1)
    s7[:, 1] = pack(tiles, 0)
    pl.semaphore_wait(barrier, NB + NT - 2)
    pl.when(has_next)(halo_copy.start)
    for i in range(1, NB // 2):
        shift_copy(i).start()
    start_all(main_copy(0, k) for k in [*own, *other])
    tiles = local_sections(0)
    s7[:, 2] = pack(tiles, 1)
    fsend[...] = pack(tiles, 0)
    pl.when(edges_first)(lambda: start_all(main_copy(1, k) for k in own[:6]))
    start_all(main_copy(1, k) for k in other)
    pl.when(jnp.logical_not(edges_first))(lambda: start_all(main_copy(1, k) for k in own[:6]))
    start_all(main_copy(1, k) for k in own[6:])
    recv[slot // 2, slot % 2] = s7[me]

    offset, sample = iota((256, 128), 0) - 128, iota((256, 128), 1)
    row = jnp.broadcast_to(par[12:13, :], (8, 128))
    for j in range(NBOX):
        width = take_lanes(row, jnp.full((8, 128), j, I32))
        root = jnp.sqrt(width.astype(F32))
        roots[0, j] = root
        roots[1, j] = 1.0 / root
        width = jnp.broadcast_to(width[None], (32, 8, 128)).reshape(256, 128)
        inside = (offset <= sample) & (offset > sample - width)
        band[:, j * 128 : (j + 1) * 128] = jnp.where(inside, 1.0, 0.0).astype(BF16)

    @pl.when(t == 0)
    def _():
        hrecv[...] = jnp.zeros(hrecv.shape, F32)
        grecv[...] = jnp.zeros(grecv.shape, F32)

    pl.when(has_last)(halo_copy.wait_recv)
    def spread_edge(packed):
        return jnp.stack([packed, swap_halves(packed)], axis=1).reshape(-1, 8, 128)

    x = hrecv[...]
    empty = jnp.zeros((16, 1, 8, 128), F32)
    for s in range(1, LOCAL + 1):
        pairs = idx1[s - 1].reshape(16, 2, 8, 128)
        index = jnp.where(iota((16, 8, 128), 1) < 4, pairs[:, 0], pairs[:, 1])
        if s in (1, 5):
            x = jnp.concatenate([x, empty], axis=1)
        keep = x.shape[1] - (s in (3, 7))
        if 2 <= s <= 5:
            x = major_section(x, index, 2 ** (s - 2), keep)
        else:
            x = minor_section(x, index, 4 if s == 1 else 2 ** (7 - s), keep)
    fsend[...] = fsend[...] + pack((spread_edge(x[:, 0]), spread_edge(x[:, 1])), 0)
    hops = [2 * dx + min(dz, 8 - dz) for dx, dz, _ in OFFSETS]
    start_all(front_copy(k) for k in sorted(range(NB - 1), key=lambda k: -hops[k]))
    frecv[slot // 2, slot % 2] = fsend[me]

    for e in range(2):
        for k in other if e else own:
            main_copy(0, k).wait_recv()
        pl.when(has_next)(edge_copies[e].start)

    for i in range(1, NB // 2):
        shift_copy(i).wait_recv()
    quarter = sub8 % 4
    for j in range(1, CROSS + 1):
        base = 0
        for bit in range(j, CROSS):
            base = base + me // 2**bit % 2 * 2 ** (6 - bit + j)
        for low in range(2 ** (CROSS - j)):
            if j < CROSS:
                source = me % 2**j
                for bit in range(j, CROSS):
                    source = source + 2**bit * ((low >> (4 - bit)) & 1)
                row = shbuf[source, j - 1]
            else:
                row = par[LOCAL + j - 1 : LOCAL + j, :]
            row = jnp.broadcast_to(row, (8, 128))
            for high in range(2**j):
                delay = take_lanes(row, base + 2**j * quarter + high)
                idx2[j - 1, low + 2 ** (CROSS - j) * high] = (lane8 - delay) & 127

    for k in [*other, *own]:
        main_copy(1, k).wait_recv()

    def unpack(low, high):
        return jnp.where(is_low, low, swap_halves(high)), jnp.where(is_low, swap_halves(low), high)

    back = unpack(recv[:, :, 1].reshape(32, 8, 128), recv[:, :, 0].reshape(32, 8, 128))
    x = swap_halves(jnp.stack(back, axis=1))
    x = jnp.where(jnp.broadcast_to(is_low[:, None], x.shape), 0.0, x)
    aheads = []
    for j in range(1, CROSS + 1):
        aheads.append(x[:, -1:])
        x = major_section(x, idx2[j - 1], 2 ** (CROSS - j), x.shape[1] - (j == 3))
    front = x

    high = recv[:, :, 2].reshape(32, 8, 128)
    x = jnp.stack([jnp.where(is_low, 0.0, swap_halves(high)), jnp.where(is_low, 0.0, high), *back], axis=1)
    for j in range(1, CROSS + 1):
        x = major_section(jnp.concatenate([aheads[j - 1], x], axis=1), idx2[j - 1], 2 ** (CROSS - j), TILES)
    norm = 16384.0 ** (-0.5)
    x = jnp.concatenate([front, x], axis=1) * norm
    for k in range(5):
        t2[k, 0:256] = x[:, k].reshape(256, 128)

    def output_rows(k, half):
        return jnp.concatenate([t2[k, pl.ds(b * 64 + half * 4 + q, 8, stride=8), :] for q in range(4) for b in range(4)])

    second = [output_rows(1 + k, 1) for k in range(TILES)]
    pivot = jnp.sum(second[0] + second[1] + second[2] + second[3], axis=1, keepdims=True) * (1.0 / 512)
    pivot = jnp.broadcast_to(pivot, (128, 128))
    sums, squares = jnp.zeros((128, 128), F32), jnp.zeros((128, 128), F32)

    def split(c, centred):
        high = centred.astype(BF16)
        low = (centred - high.astype(F32)).astype(BF16)
        for part, value in ((hi, high), (lo, low)):
            if c >= 0:
                part[128 * c : 128 * c + 128, 128:256] = value
            if c < 2 * TILES - 1:
                part[128 * c + 128 : 128 * c + 256, 0:128] = value

    for k in range(TILES):
        ded_ref[:, 512 + 128 * k : 640 + 128 * k] = second[k]
        centred = second[k] - pivot
        sums, squares = sums + centred, squares + centred * centred
        split(TILES + k, centred)

    def boxcars(first, tiles):
        at = pl.ds(128 * first, 128 * tiles)
        both = jnp.dot(hi[at], band[...], preferred_element_type=F32)
        both = both + jnp.dot(lo[at], band[...], preferred_element_type=F32)
        for j in range(NBOX):
            part = both[:, j * 128 : (j + 1) * 128].reshape(-1, 8, 128)
            part = (part * jnp.broadcast_to(roots[1, j][None], part.shape)).reshape(tiles, 128, 128)
            for c in range(tiles):
                bc[first + c, j] = part[c]

    for k in range(NB - 1):
        front_copy(k).wait_recv()
    for copy in edge_copies:
        pl.when(has_last)(copy.wait_recv)
    y = jnp.stack([grecv[column if f == 0 else 1 - column] for f in range(2)], axis=1).reshape(32, 8, 128)
    y = jnp.stack([y, frecv[...].reshape(32, 8, 128)], axis=1)
    for j in range(1, CROSS + 1):
        y = folded_section(y, idx2[j - 1], 2 ** (CROSS - j), j == 1)
    added = [swap_halves(y[:, 0]), y[:, 1], swap_halves(y[:, 1]), y[:, 2], swap_halves(y[:, 2])]
    for k in range(5):
        t2[k, 0:256] = (x[:, k] + jnp.where(is_low, added[k], 0.0) * norm).reshape(256, 128)
    first = [output_rows(k, 0) for k in range(5)]
    for k in range(1, 5):
        centred = first[k] - pivot
        sums, squares = sums + centred, squares + centred * centred
    sums = jnp.broadcast_to(jnp.sum(sums, axis=1, keepdims=True), (128, 128))
    squares = jnp.broadcast_to(jnp.sum(squares, axis=1, keepdims=True), (128, 128))
    squares = squares - sums * sums * (1.0 / 1024)
    sums = pivot + sums * (1.0 / 1024)
    mine = jnp.transpose(jnp.where(iota((128, 128), 1) == 0, sums, squares))[0:2]
    stsend[...] = mine
    stbuf[t] = mine

    def stat_copy(i):
        return pltpu.make_async_remote_copy(
            src_ref=stsend, dst_ref=stbuf.at[t], send_sem=st_send.at[i], recv_sem=st_recv.at[i],
            device_id={"tm": lax.rem(t + i, NT)}, device_id_type=MESH,
        )

    for i in range(1, NT):
        stat_copy(i).start()

    for k in range(5):
        split(k - 1, first[k] - pivot)
        if k:
            ded_ref[:, 128 * k - 128 : 128 * k] = first[k]
    boxcars(0, 2 * TILES)
    for k in range(NB - 1):
        main_copy(0, k).wait_send()
        main_copy(1, k).wait_send()
        front_copy(k).wait_send()
    for i in range(1, NB // 2):
        shift_copy(i).wait_send()
    pl.when(has_next)(halo_copy.wait_send)
    for e in range(2):
        pl.when(has_next)(edge_copies[e].wait_send)
    for i in range(1, NT):
        stat_copy(i).wait_recv()
    means = [stbuf[i][0:1] for i in range(NT)]
    mean = sum(means) * (1.0 / NT)
    centred = [stbuf[i][1:2] + 1024.0 * ((m - mean) * (m - mean)) for i, m in enumerate(means)]
    scale = 1.0 / jnp.sqrt(sum(centred) * (1.0 / SAMPLES) + 1e-6)
    row_mean = jnp.transpose(jnp.broadcast_to(mean, (128, 128)))
    row_scale = jnp.transpose(jnp.broadcast_to(scale, (128, 128)))
    off = pivot - row_mean
    for h in range(8):
        at = pl.ds(16 * h, 16)
        best = [None] * (2 * TILES)
        for j in range(NBOX):
            up = jnp.broadcast_to(roots[0, j][None], (2, 8, 128)).reshape(16, 128)
            bias = up * off[16 * h : 16 * h + 16]
            for c in range(2 * TILES):
                score = bc[c, j, at] + bias
                best[c] = score if j == 0 else jnp.maximum(best[c], score)
        for c in range(2 * TILES):
            snr_ref[at, 128 * c : 128 * c + 128] = best[c] * row_scale[16 * h : 16 * h + 16]
    for i in range(1, NT):
        stat_copy(i).wait_send()


def store(a, b, a_hbm, b_hbm, sem):
    copies = [pltpu.make_async_copy(a, a_hbm, sem.at[0]), pltpu.make_async_copy(b, b_hbm, sem.at[1])]
    for copy in copies:
        copy.start()
    for copy in copies:
        copy.wait()


def body(intensity, shifts, boxcar_widths):
    dma = pltpu.SemaphoreType.DMA
    vmem, whole = pltpu.VMEM, pl.BlockSpec(memory_space=pl.ANY)
    in_vmem = pl.BlockSpec(memory_space=pltpu.VMEM)
    out = jax.ShapeDtypeStruct((128, 1024), F32)
    params = jnp.pad(shifts, ((0, 4), (0, 0)))
    params = lax.dynamic_update_slice(params, boxcar_widths[None], (12, 0))
    ded, snr = pl.pallas_call(
        kernel,
        out_shape=(out, out),
        in_specs=[whole, in_vmem],
        out_specs=[in_vmem] * 2,
        scratch_shapes=[
            vmem((512, 1024), BF16),
            vmem((4, 1, 128), I32),
            vmem((NB, 4, 1, 128), I32),
            vmem((LOCAL, 32, 8, 128), I32),
            vmem((CROSS, 32, 8, 128), I32),
            vmem((32, 6, 8, 128), F32),
            vmem((32, 3, 8, 128), F32),
            vmem((16, 2, 8, 128), F32),
            vmem((16, 2, 8, 128), F32),
            vmem((2, 16, 8, 128), F32),
            vmem((32, 8, 128), F32),
            vmem((16, 2, 8, 128), F32),
            vmem((16, 2, 3, 8, 128), F32),
            vmem((5, 264, 128), F32),
            vmem((1024, 256), BF16),
            vmem((1024, 256), BF16),
            vmem((2 * TILES, NBOX, 128, 128), F32),
            vmem((256, 1024), BF16),
            vmem((2, NBOX, 8, 128), F32),
            vmem((2, 128), F32),
            vmem((NT, 2, 128), F32),
            dma((4,)),
            dma((NB // 2,)),
            dma((NB // 2,)),
            dma((6,)),
            dma((2, NB - 1)),
            dma((2, NB - 1)),
            dma((NB - 1,)),
            dma((NB - 1,)),
            dma((NT,)),
            dma((NT,)),
        ],
        compiler_params=pltpu.CompilerParams(
            collective_id=0, has_side_effects=True, vmem_limit_bytes=52 * 2**20
        ),
    )(intensity, params)
    return pl.pallas_call(
        store,
        out_shape=(out, out),
        in_specs=[in_vmem] * 2,
        out_specs=[whole] * 2,
        scratch_shapes=[dma((2,))],
        compiler_params=pltpu.CompilerParams(vmem_limit_bytes=52 * 2**20),
    )(ded, snr)


def solution(mesh):
    assert mesh.shape["band"] == NB and mesh.shape["tm"] == NT
    in_specs = (P("band", "tm"), P(None, "band"), P())
    out_specs = (P("band", "tm"), P("band", "tm"))
    return jax.shard_map(body, mesh=mesh, in_specs=in_specs, out_specs=out_specs, check_vma=False)
```
